32 devices in a mesh: lead: 4 (over y, x), dp: 2 (over core), lat: 4 (over z).
Axes of the slice: x: 2, y: 2, z: 4, core: 2. Of those that a mesh axis runs over, the one named last changes fastest.
Arguments:
- field: bfloat16 [4, 16, 32, 64, 128], P('lead', 'dp', 'lat'), may hold values from -6 to 6
- cotangent: bfloat16 [4, 16, 32, 64, 128], P('lead', 'dp', 'lat'), may hold values from -6 to 6
- land_sea: int32 [4, 16, 32, 64], P('lead', 'dp', 'lat'), may hold values from 0 to 1, as said below
- conv1_weight: bfloat16 [3, 3, 128, 128], replicated, may hold values from -0.1875 to 0.1875
- conv1_bias: float32 [128], replicated, may hold values from -3 to 3
- first_norm_scale: float32 [128], replicated, may hold values from 0.5 to 1.5
- norm1_shift: float32 [128], replicated, may hold values from -3 to 3
- conv2_weight: bfloat16 [3, 3, 128, 128], replicated, may hold values from -0.1875 to 0.1875
- conv2_bias: float32 [128], replicated, may hold values from -3 to 3
- second_norm_scale: float32 [128], replicated, may hold values from 0.5 to 1.5
- norm2_shift: float32 [128], replicated, may hold values from -3 to 3
Outputs:
- output: bfloat16 [4, 16, 32, 64, 128], P('lead', 'dp', 'lat')
- field_grad: bfloat16 [4, 16, 32, 64, 128], P('lead', 'dp', 'lat')
- conv1_weight_grad: float32 [3, 3, 128, 128], replicated
- conv1_bias_grad: float32 [128], replicated
- norm1_gain_grad: float32 [128], replicated
- norm1_shift_grad: float32 [128], replicated
- conv2_weight_grad: float32 [3, 3, 128, 128], replicated
- conv2_bias_grad: float32 [128], replicated
- norm2_gain_grad: float32 [128], replicated
- norm2_shift_grad: float32 [128], replicated
The draws below stay inside these ranges and needn't reach their ends.
Inputs may be any that keep to these rules, and one draw needn't show every extreme that they name: `land_sea`: 1 marks a pixel that counts in the norms, 0 one that is left out.
All inputs are finite; a program needn't handle non-finite values.
Results may differ from the reference program's by a relative error of at most 0.024.
Values may be sent and summed in bfloat16 or wider, within the bound.
No kernel may reach another device: no remote copies, remote signals or barrier semaphores. Data moves between devices by JAX's collectives and lax.ppermute only.
A program may use at most 64 MiB of HBM per device.

```python
import jax
import jax.numpy as jnp
from jax import lax

C = 128
LON = 64
LEADS = 4
SAMPLES = 16
LAT = 32


def draw_land_sea(key, part):
    key = jax.random.fold_in(key, 11)
    random_bits = jax.random.randint(key, (LEADS, SAMPLES, LAT, LON), 0, 1000)
    row_index = jnp.arange(LAT, dtype=jnp.int32)
    limits = 300 + 600 * row_index // max(LAT - 1, 1)
    return (random_bits < limits[None, None, :, None]).astype(jnp.int32)


def block_levels(own_key, shape, shards, smallest, top_value):
    gain = 1.0
    for position, blocks in shards:
        steps = jax.random.uniform(jax.random.fold_in(jax.random.fold_in(own_key, 6), position), (blocks,), jnp.float32, smallest / len(shards), top_value / len(shards))
        gain = gain * jnp.repeat(jnp.exp(steps), shape[position] // blocks).reshape((-1,) + (1,) * (len(shape) - 1 - position))
    return gain


def gaussian(key, shape, spread, reach, split=(), kind=jnp.bfloat16):
    loudness = block_levels(key, shape, split, -0.22, 0.18) if split else 1.0
    entries = jax.random.normal(key, shape, jnp.float32) * spread * loudness
    return jnp.minimum(jnp.maximum(entries, -reach), reach).astype(kind)


def setup_inputs(seed: int = 0) -> dict:
    splits = jax.random.split(jax.random.key(seed), 12)
    return {
        "field": gaussian(splits[0], (LEADS, SAMPLES, LAT, LON, C), 1.0, 6.0, ((0, 4), (1, 2), (2, 4))),
        "cotangent": gaussian(splits[1], (LEADS, SAMPLES, LAT, LON, C), 1.0, 6.0, ((0, 4), (1, 2), (2, 4))),
        "land_sea": draw_land_sea(jax.random.fold_in(splits[11], 71), 0),
        "conv1_weight": gaussian(splits[3], (3, 3, C, C), (9 * C) ** -0.5, 0.1875),
        "conv1_bias": gaussian(splits[4], (C,), 0.5, 3.0, (), jnp.float32),
        "first_norm_scale": jnp.clip(1.0 + 0.1 * jax.random.normal(splits[5], (C,), jnp.float32), 0.5, 1.5),
        "norm1_shift": gaussian(splits[6], (C,), 0.5, 3.0, (), jnp.float32),
        "conv2_weight": gaussian(splits[7], (3, 3, C, C), (9 * C) ** -0.5, 0.1875),
        "conv2_bias": gaussian(splits[8], (C,), 0.5, 3.0, (), jnp.float32),
        "second_norm_scale": jnp.clip(1.0 + 0.1 * jax.random.normal(splits[9], (C,), jnp.float32), 0.5, 1.5),
        "norm2_shift": gaussian(splits[10], (C,), 0.5, 3.0, (), jnp.float32),
    }


EPSILON = 1e-05

@jax.custom_vjp
def low(v):
    return lax.optimization_barrier(v.astype(jnp.bfloat16)).astype(jnp.float32)

@jax.custom_vjp
def low_back(v):
    return v

def low_keep(v):
    return (low(v), None)

def low_pass(kept, grad):
    return (grad,)

def back_keep(v):
    return (v, None)

def back_low(kept, grad):
    return (low(grad),)
low.defvjp(low_keep, low_pass)
low_back.defvjp(back_keep, back_low)

def convolve(values, kernel):
    padded = jnp.pad(values, ((0, 0), (1, 1), (0, 0), (0, 0)))
    padded = jnp.concatenate([padded[:, :, -1:], padded, padded[:, :, :1]], axis=2)
    return lax.conv_general_dilated(padded, kernel, (1, 1), 'VALID', dimension_numbers=('NHWC', 'HWIO', 'NHWC'), precision=lax.Precision.HIGHEST)

def masked_norm(active, ocean_land_mask, valid_pixel_count, norm_gain, norm_shift):
    mean_value = lax.optimization_barrier(jnp.sum(ocean_land_mask * active, axis=(0, 1, 2))) / valid_pixel_count
    centred = active - mean_value
    variance = lax.optimization_barrier(jnp.sum(ocean_land_mask * centred * centred, axis=(0, 1, 2))) / valid_pixel_count
    return ocean_land_mask * (centred * lax.rsqrt(variance + EPSILON) * norm_gain + norm_shift)

def block(inputs, kernel_one, bias_one, gain_one, shift_one, kernel_two, bias_two, gain_two, shift_two, ocean_land_mask):
    valid_pixel_count = jnp.sum(ocean_land_mask)
    hidden_one = low_back(convolve(inputs, kernel_one) + bias_one)
    first_normalized = low(masked_norm(jax.nn.silu(hidden_one), ocean_land_mask, valid_pixel_count, gain_one, shift_one))
    hidden_two = low_back(convolve(first_normalized, kernel_two) + bias_two)
    second_normalized = masked_norm(jax.nn.silu(hidden_two), ocean_land_mask, valid_pixel_count, gain_two, shift_two)
    return inputs + second_normalized

def reference(field, cotangent, land_sea, conv1_weight, conv1_bias, first_norm_scale, norm1_shift, conv2_weight, conv2_bias, second_norm_scale, norm2_shift):
    parameters = tuple((parameter.astype(jnp.float32) for parameter in (conv1_weight, conv1_bias, first_norm_scale, norm1_shift, conv2_weight, conv2_bias, second_norm_scale, norm2_shift)))
    outputs = []
    input_grads = []
    totals = [jnp.zeros(parameter.shape, jnp.float32) for parameter in parameters]
    for lead_step in range(LEADS):
        ocean_land_mask = land_sea[lead_step].astype(jnp.float32)[..., None]

        def forward(inputs, *weights):
            return block(inputs, *weights, ocean_land_mask)
        result, pullback = jax.vjp(forward, field[lead_step].astype(jnp.float32), *parameters)
        gradients = pullback(cotangent[lead_step].astype(jnp.float32))
        outputs.append(result.astype(jnp.bfloat16))
        input_grads.append(gradients[0].astype(jnp.bfloat16))
        totals = [summed + gradient for summed, gradient in zip(totals, gradients[1:])]
    return (jnp.stack(outputs), jnp.stack(input_grads), totals[0], totals[1], totals[2], totals[3], totals[4], totals[5], totals[6], totals[7])
```

```python
import functools

import jax
import jax.numpy as jnp
from jax import lax
from jax.experimental import pallas as pl
from jax.experimental.pallas import tpu as pltpu
from jax.sharding import PartitionSpec as P

EPSILON = 1e-05
BF16 = jnp.bfloat16
F32 = jnp.float32
VMEM = pl.BlockSpec(memory_space=pltpu.VMEM)
SMALL = 16


def fill_toeplitz(taps_ref, out_ref):
    c = taps_ref.shape[-1]
    zero = jnp.zeros((c, c), BF16)
    for b in range(3):
        for i in range(4):
            for j in range(2):
                block = taps_ref[i - j, b] if 0 <= i - j < 3 else zero
                out_ref[b, i * c : (i + 1) * c, j * c : (j + 1) * c] = block


def fill_toeplitz_transposed(taps_ref, out_ref):
    c = taps_ref.shape[-1]
    zero = jnp.zeros((c, c), BF16)
    for b in range(3):
        for i in range(4):
            for j in range(2):
                block = taps_ref[2 - (i - j), 2 - b] if 0 <= i - j < 3 else zero
                out_ref[b, j * c : (j + 1) * c, i * c : (i + 1) * c] = block


def column_sum(products, across):
    shaped = [p.reshape(-1, across, p.shape[-1]) for p in products]
    return (
        pltpu.roll(shaped[0], 1, 1) + shaped[1] + pltpu.roll(shaped[2], across - 1, 1)
    )


def convolve_pairs(row, starts, weights_ref, across, transposed):
    left = jnp.concatenate(
        [jnp.concatenate([row(r - 1 + i) for r in starts], 0) for i in range(4)], 1
    )
    dims = (((1,), (1 if transposed else 0,)), ((), ()))
    return column_sum(
        [
            lax.dot_general(left, weights_ref[b], dims, preferred_element_type=F32)
            for b in range(3)
        ],
        across,
    )


def convolve_single(rows, weights_ref, first, across):
    c = rows[0].shape[-1]
    left = jnp.concatenate(rows, 1)
    low, col = (0, 0) if first else (c, c)
    return column_sum(
        [
            jnp.dot(
                left,
                weights_ref[b, low : low + 3 * c, col : col + c],
                preferred_element_type=F32,
            )
            for b in range(3)
        ],
        across,
    )


def silu_and_slope(hidden):
    gate = 0.5 + 0.5 * jnp.tanh(0.5 * hidden)
    active = hidden * gate
    return active, gate + active * (1.0 - gate)


def silu(value):
    return value * (0.5 + 0.5 * jnp.tanh(0.5 * value))


def fold(value):
    return value.reshape(-1, 8, value.shape[-1]).sum(0)


def norm_terms(stats, count):
    offset = stats[0:1] / count
    variance = jnp.maximum(stats[1:2] / count - offset * offset, 0.0)
    return offset, lax.rsqrt(variance + EPSILON)


def pick(even, when_even, when_odd):
    return jnp.where(even, when_even, when_odd)


def conv1_kernel(x_ref, gx_ref, gp_ref, m_ref, w_ref, b_ref, a_ref, s_ref, st_ref, t_ref):
    samples, height, across, c = x_ref.shape
    even = lax.axis_index("lat") % 2 == 0
    fill_toeplitz(w_ref, t_ref)
    bias = b_ref[...]
    centre = silu(bias)
    sums = [jnp.zeros((8, c), F32) for _ in range(3)]
    for s in range(samples):

        def row(r):
            if r < 0:
                return pick(even, gp_ref[s], gx_ref[s])
            if r >= height:
                return pick(even, gx_ref[s], gp_ref[s])
            return x_ref[s, r]

        out = convolve_pairs(row, range(0, height, 2), t_ref, across, False)
        for j in range(2):
            active, slope = silu_and_slope(out[:, :, j * c : (j + 1) * c] + bias)
            active = active - centre
            for q in range(height // 2):
                r = 2 * q + j
                a_ref[s, r] = active[q]
                s_ref[s, r] = slope[q].astype(BF16)
                mask = m_ref[s, r].astype(F32)
                masked = active[q] * mask
                sums[0] += fold(masked)
                sums[1] += fold(masked * active[q])
                sums[2] += fold(mask)
    total = jnp.concatenate(
        [v.sum(0, keepdims=True) for v in sums] + [jnp.zeros((5, c), F32)], 0
    )
    st_ref[...] = jnp.broadcast_to(total[None], st_ref.shape)


def conv1_edge_kernel(x_ref, gx_ref, gp_ref, hx_ref, hp_ref, w_ref, b_ref, a_ref, s_ref, t_ref):
    samples, height, across, c = x_ref.shape
    even = lax.axis_index("lat") % 2 == 0
    fill_toeplitz(w_ref, t_ref)
    bias = b_ref[...]
    centre = silu(bias)

    def far(ref, s, j):
        at = (s * 3 + j) * across
        return ref[at : at + across]

    def row(r):
        parts = []
        for s in range(samples):
            if r < -1:
                parts.append(pick(even, far(hp_ref, s, r + 4), far(hx_ref, s, r + 4)))
            elif r == -1:
                parts.append(pick(even, gp_ref[s], gx_ref[s]))
            elif r < height:
                parts.append(x_ref[s, r])
            elif r == height:
                parts.append(pick(even, gx_ref[s], gp_ref[s]))
            else:
                j = r - height - 1
                parts.append(pick(even, far(hx_ref, s, j), far(hp_ref, s, j)))
        return jnp.concatenate(parts, 0)

    def put(slot, value):
        active, slope = silu_and_slope(value + bias)
        active = active - centre
        for s in range(samples):
            a_ref[s, slot] = active[s]
            s_ref[s, slot] = slope[s].astype(BF16)

    top = convolve_pairs(row, (-2,), t_ref, across, False)
    put(1, top[:, :, :c])
    put(2, top[:, :, c:])
    bottom = convolve_pairs(row, (height,), t_ref, across, False)
    put(3, bottom[:, :, :c])
    put(4, bottom[:, :, c:])
    put(0, convolve_single([row(r) for r in (-4, -3, -2)], t_ref, False, across))
    put(
        5,
        convolve_single([row(height + r) for r in (1, 2, 3)], t_ref, True, across),
    )


def conv2_kernel(
    st_ref, a_ref, ah_ref, m_ref, mh_ref, u_ref, w_ref, b_ref, g_ref, t_ref,
    n_ref, a2_ref, s2_ref, c1_ref, st2_ref, k_ref,
):
    samples, height, across, c = a_ref.shape
    fill_toeplitz(w_ref, k_ref)
    stats = st_ref[...].sum(0)
    count = stats[2:3]
    offset, inverse = norm_terms(stats, count)
    scale = inverse * g_ref[...]
    shift = t_ref[...] - offset * scale
    c1_ref[...] = jnp.concatenate([offset, inverse, count, jnp.zeros((5, c), F32)], 0)
    bias = b_ref[...]
    centre = silu(bias)
    sums = [jnp.zeros((8, c), F32) for _ in range(4)]
    for s in range(samples):
        for i in range(height + 6):
            r = i - 3
            if r < 0:
                value, mask = ah_ref[s, i], mh_ref[s, i]
            elif r >= height:
                value, mask = ah_ref[s, r - height + 3], mh_ref[s, r - height + 3]
            else:
                value, mask = a_ref[s, r], m_ref[s, r]
            n_ref[s, i] = (value * scale + shift).astype(BF16) * mask

        out = convolve_pairs(
            lambda r: n_ref[s, r + 3], range(-2, height + 2, 2), k_ref, across, False
        )
        for j in range(2):
            active, slope = silu_and_slope(out[:, :, j * c : (j + 1) * c] + bias)
            active = active - centre
            for q in range(height // 2 + 2):
                i = 2 * q + j
                r = i - 2
                a2_ref[s, i] = active[q]
                s2_ref[s, i] = slope[q].astype(BF16)
                if 0 <= r < height:
                    mask = m_ref[s, r].astype(F32)
                    masked = active[q] * mask
                    upstream = u_ref[s, r].astype(F32)
                    sums[0] += fold(masked)
                    sums[1] += fold(masked * active[q])
                    sums[2] += fold(masked * upstream)
                    sums[3] += fold(mask * upstream)
    total = jnp.concatenate(
        [v.sum(0, keepdims=True) for v in sums] + [jnp.zeros((4, c), F32)], 0
    )
    st2_ref[...] = jnp.broadcast_to(total[None], st2_ref.shape)


def back2_kernel(
    st_ref, c1_ref, a2_ref, s2_ref, u_ref, hx_ref, hp_ref, m_ref, mh_ref, a1_ref, w_ref, g_ref, t_ref,
    d_ref, dn_ref, c2_ref, st3_ref, k_ref,
):
    samples, height, across, c = u_ref.shape
    even = lax.axis_index("lat") % 2 == 0
    fill_toeplitz_transposed(w_ref, k_ref)
    stats = st_ref[...].sum(0)
    count = c1_ref[2:3]
    offset, inverse = norm_terms(stats, count)
    shift_sum = stats[3:4]
    gain_sum = inverse * (stats[2:3] - offset * shift_sum)
    scale = inverse * g_ref[...]
    by_active = -scale * gain_sum * inverse / count
    constant = -scale * (shift_sum - offset * inverse * gain_sum) / count
    c2_ref[...] = jnp.concatenate(
        [scale, t_ref[...] - offset * scale, gain_sum, shift_sum, jnp.zeros((4, c), F32)], 0
    )

    def far(ref, s, j):
        at = (samples * 3 + s * 2 + j) * across
        return ref[at : at + across]

    sums = [jnp.zeros((8, c), F32) for _ in range(2)]
    for s in range(samples):
        for i in range(height + 4):
            r = i - 2
            if r < 0:
                upstream, mask = pick(even, far(hp_ref, s, i), far(hx_ref, s, i)), mh_ref[s, i + 1]
            elif r >= height:
                j = r - height
                upstream, mask = pick(even, far(hx_ref, s, j), far(hp_ref, s, j)), mh_ref[s, j + 3]
            else:
                upstream, mask = u_ref[s, r], m_ref[s, r]
            grad = upstream.astype(F32) * scale + (a2_ref[s, i] * by_active + constant)
            d_ref[s, i] = (grad * s2_ref[s, i].astype(F32)).astype(BF16) * mask
        out = convolve_pairs(
            lambda r: d_ref[s, r + 2], range(-1, height + 1, 2), k_ref, across, True
        )
        for j in range(2):
            part = out[:, :, j * c : (j + 1) * c]
            for q in range(height // 2 + 1):
                i = 2 * q + j
                r = i - 1
                dn_ref[s, i] = part[q]
                if 0 <= r < height:
                    masked = part[q] * m_ref[s, r].astype(F32)
                    sums[0] += fold(masked)
                    sums[1] += fold(masked * a1_ref[s, r])
    total = jnp.concatenate(
        [v.sum(0, keepdims=True) for v in sums] + [jnp.zeros((6, c), F32)], 0
    )
    st3_ref[...] = jnp.broadcast_to(total[None], st3_ref.shape)


def weight_products(rows, centre, turned, total_ref, first):
    windows = jnp.concatenate(rows, 1)
    product = lax.dot_general(
        windows,
        jnp.concatenate([turned[0], centre, turned[1]], 1),
        (((0,), (0,)), ((), ())),
        preferred_element_type=F32,
    )
    if first:
        total_ref[...] = product
    else:
        total_ref[...] += product


def turn(value, across):
    c = value.shape[-1]
    return [
        pltpu.roll(value, k, 1).astype(BF16).reshape(-1, c) for k in (across - 1, 1)
    ]


def weight2_kernel(n_ref, d_ref, x_ref, a2_ref, m_ref, c2_ref, o_ref, w_ref, b_ref, acc_ref):
    samples, height, across, c = x_ref.shape
    scale, shift = c2_ref[0:1], c2_ref[1:2]
    bias = jnp.zeros((8, c), F32)
    for s in range(samples):
        grad = d_ref[s, 2 : 2 + height]
        wide = grad.astype(F32)
        bias += fold(wide)
        rows = [n_ref[s, a + 2 : a + 2 + height].reshape(-1, c) for a in range(3)]
        weight_products(rows, grad.reshape(-1, c), turn(wide, across), acc_ref, s == 0)
        for r in range(height):
            normed = (a2_ref[s, r + 2] * scale + shift) * m_ref[s, r].astype(F32)
            o_ref[s, r] = (x_ref[s, r].astype(F32) + normed).astype(BF16)
    b_ref[...] = jnp.broadcast_to(bias.sum(0, keepdims=True), b_ref.shape)
    for a in range(3):
        for b in range(3):
            at = (a * 3 + b) * c
            w_ref[at : at + c] = acc_ref[a * c : (a + 1) * c, b * c : (b + 1) * c].astype(BF16)


def small_rows(rows, c):
    high = jnp.concatenate(rows + [jnp.zeros((8 - len(rows), c), F32)], 0)
    first = high.astype(BF16)
    return jnp.concatenate([first, (high - first.astype(F32)).astype(BF16)], 0)


def weight1_kernel(
    group, leads,
    st_ref, c1_ref, c2_ref, dn_ref, a_ref, ah_ref, s_ref, sh_ref, m_ref, mh_ref,
    x_ref, gx_ref, gp_ref, g_ref, w2_ref, b2_ref,
    d_ref, send_ref, keep_ref, acc_ref,
):
    samples, height, across, c = x_ref.shape
    even = lax.axis_index("lat") % 2 == 0
    lead = lax.axis_index("lead")
    core = lax.axis_index("dp") % 2
    stats = st_ref[...].sum(0)
    offset, inverse, count = c1_ref[0:1], c1_ref[1:2], c1_ref[2:3]
    shift_sum = stats[0:1]
    gain_sum = inverse * (stats[1:2] - offset * shift_sum)
    scale = inverse * g_ref[...]
    by_active = -scale * gain_sum * inverse / count
    constant = -scale * (shift_sum - offset * inverse * gain_sum) / count
    bias = jnp.zeros((8, c), F32)
    for s in range(samples):
        for i in range(height + 2):
            r = i - 1
            if r < 0:
                active, slope, mask = ah_ref[s, 2], sh_ref[s, 2], mh_ref[s, 2]
            elif r >= height:
                active, slope, mask = ah_ref[s, 3], sh_ref[s, 3], mh_ref[s, 3]
            else:
                active, slope, mask = a_ref[s, r], s_ref[s, r], m_ref[s, r]
            grad = dn_ref[s, i] * scale + (active * by_active + constant)
            d_ref[s, i] = (grad * slope.astype(F32)).astype(BF16) * mask
        grad = d_ref[s, 1 : 1 + height]
        wide = grad.astype(F32)
        bias += fold(wide)
        above = pick(even, gp_ref[s], gx_ref[s])
        below = pick(even, gx_ref[s], gp_ref[s])
        body = x_ref[s].reshape(-1, c)
        rows = [
            jnp.concatenate([above, body[: (height - 1) * across]], 0),
            body,
            jnp.concatenate([body[across:], below], 0),
        ]
        weight_products(rows, grad.reshape(-1, c), turn(wide, across), acc_ref, s == 0)

    share = 1.0 / group
    small = [
        small_rows([bias.sum(0, keepdims=True), gain_sum * share, shift_sum * share], c),
        small_rows([b2_ref[0:1], c2_ref[2:3] * share, c2_ref[3:4] * share], c),
    ]

    def put(target, which):
        size = 9 * c // leads
        for j in range(leads):
            slot = j ^ lead
            if which == 1:
                target[slot, :size] = w2_ref[j * size : (j + 1) * size]
            else:
                at = j * size
                while at < (j + 1) * size:
                    tap, low = at // c, at % c
                    step = min(c - low, (j + 1) * size - at)
                    a, b = tap // 3, tap % 3
                    target[slot, at - j * size : at - j * size + step] = acc_ref[
                        a * c + low : a * c + low + step, b * c : (b + 1) * c
                    ].astype(BF16)
                    at += step
            target[slot, size:] = small[which]

    @pl.when(core == 0)
    def _():
        put(keep_ref, 0)
        put(send_ref, 1)

    @pl.when(core != 0)
    def _():
        put(keep_ref, 1)
        put(send_ref, 0)


def input_grad_kernel(d_ref, u_ref, w_ref, o_ref, k_ref):
    samples, height, across, c = u_ref.shape
    fill_toeplitz_transposed(w_ref, k_ref)
    for s in range(samples):
        out = convolve_pairs(
            lambda r: d_ref[s, r + 1], range(0, height, 2), k_ref, across, True
        )
        for q in range(height // 2):
            for j in range(2):
                r = 2 * q + j
                o_ref[s, r] = (
                    u_ref[s, r].astype(F32) + out[q, :, j * c : (j + 1) * c]
                ).astype(BF16)


def call(kernel, outs, scratch, operands, name, flops=0):
    size = sum(o.size * o.dtype.itemsize for o in operands)
    return pl.pallas_call(
        kernel,
        out_shape=outs,
        in_specs=[VMEM] * len(operands),
        out_specs=jax.tree.map(lambda _: VMEM, outs),
        scratch_shapes=scratch,
        compiler_params=pltpu.CompilerParams(vmem_limit_bytes=24 * 2**20),
        cost_estimate=pl.CostEstimate(flops=flops, bytes_accessed=size, transcendentals=0),
        name=name,
    )(*operands)


def swap(value, axis, k):
    return lax.ppermute(value, axis, [(i, i ^ k) for i in range(lax.axis_size(axis))])


def neighbours(value_x, value_p, axis):
    n = lax.axis_size(axis)
    first = [(i, i ^ 1) for i in range(n) if i ^ 1 < n]
    second = [(i, i + 1) for i in range(1, n - 1, 2)]
    second += [(j, i) for i, j in second]
    return lax.ppermute(value_x, axis, first), lax.ppermute(value_p, axis, second)


def spread(stats):
    return lax.all_to_all(stats, ("dp", "lat"), 0, 0)


def add_chunks(parts):
    total = functools.reduce(lambda a, b: a + b, [p.astype(F32) for p in parts])
    size = total.shape[-2] - SMALL
    small = total[..., size : size + 8, :] + total[..., size + 8 :, :]
    high = lax.reduce_precision(small, 8, 7)
    return jnp.concatenate(
        [total[..., :size, :].astype(BF16), high.astype(BF16), (small - high).astype(BF16)], -2
    )


def sum_everywhere(send, keep):
    leads, lats = lax.axis_size("lead"), lax.axis_size("lat")
    chunks = add_chunks([keep, swap(send, "dp", 1)])
    mine = add_chunks([chunks[0]] + [swap(chunks[k], "lead", k) for k in range(1, leads)])
    mine = add_chunks([mine] + [swap(mine, "lat", k) for k in range(1, lats)])
    k = 2
    while k < lax.axis_size("dp"):
        mine = add_chunks([mine, swap(mine, "dp", k)])
        k *= 2
    size = mine.shape[0] - SMALL
    weights = jnp.stack(
        [mine[:size]] + [swap(mine[:size], "lead", k) for k in range(1, leads)]
    ).reshape(-1, mine.shape[-1])
    own = jnp.concatenate([weights, mine[size:]], 0)
    other = swap(own, "dp", 1)
    core = lax.axis_index("dp") % 2
    lead = lax.axis_index("lead")

    def finish(value):
        blocks = value[: leads * size].reshape(leads, size, -1)
        whole = jnp.concatenate(
            [lax.dynamic_index_in_dim(blocks, j ^ lead, 0, False) for j in range(leads)], 0
        )
        c = whole.shape[-1]
        small = value[leads * size :].astype(F32)
        return whole.astype(F32).reshape(3, 3, c, c), small[:8] + small[8:]

    first = finish(jnp.where(core == 0, own, other))
    second = finish(jnp.where(core == 0, other, own))
    return first, second


def shards(
    field,
    cotangent,
    land_sea,
    conv1_weight,
    conv1_bias,
    first_norm_scale,
    norm1_shift,
    conv2_weight,
    conv2_bias,
    second_norm_scale,
    norm2_shift,
):
    x, u, mask = field[0], cotangent[0], land_sea[0]
    samples, height, across, c = x.shape
    pixels = samples * across
    group = lax.axis_size("dp") * lax.axis_size("lat")
    leads = lax.axis_size("lead")
    even = lax.axis_index("lat") % 2 == 0
    vec = lambda v: v.reshape(1, c)
    b1, g1, t1 = vec(conv1_bias), vec(first_norm_scale), vec(norm1_shift)
    b2, g2, t2 = vec(conv2_bias), vec(second_norm_scale), vec(norm2_shift)

    def edge(array, rows, skip, down):
        start = jnp.where(down, height - skip - rows, skip)
        return lax.dynamic_slice_in_dim(array, start, rows, 1)

    bits = mask.astype(BF16)

    def far(down):
        return jnp.concatenate(
            [
                edge(x, 3, 1, down).reshape(-1, c),
                edge(u, 2, 0, down).reshape(-1, c),
                edge(bits, 3, 0, down).reshape(-1, c),
            ],
            0,
        )

    gx, gp = neighbours(
        edge(x, 1, 0, even).reshape(samples, across, c),
        edge(x, 1, 0, ~even).reshape(samples, across, c),
        "lat",
    )
    hx, hp = neighbours(far(even), far(~even), "lat")

    wide_mask = jnp.broadcast_to(bits[..., None], x.shape)

    def halo_bits(far_rows):
        return far_rows[5 * pixels :].reshape(samples, 3, across)

    halo_mask = jnp.concatenate(
        [
            jnp.where(even, halo_bits(hp), halo_bits(hx)),
            jnp.where(even, halo_bits(hx), halo_bits(hp)),
        ],
        1,
    )
    halo_mask = jnp.broadcast_to(halo_mask[..., None], (samples, 6, across, c))

    shape = lambda rows, dtype: jax.ShapeDtypeStruct((samples, rows, across, c), dtype)
    stats_shape = jax.ShapeDtypeStruct((group, 8, c), F32)
    vector = jax.ShapeDtypeStruct((8, c), F32)
    weights = pltpu.VMEM((3, 4 * c, 2 * c), BF16)
    turned = pltpu.VMEM((3, 2 * c, 4 * c), BF16)
    conv_flops = 2 * 9 * c * c * samples * height * across

    a1, s1, st1 = call(
        conv1_kernel,
        (shape(height, F32), shape(height, BF16), stats_shape),
        [weights],
        (x, gx, gp, wide_mask, conv1_weight, b1),
        "conv1",
        conv_flops,
    )
    a1h, s1h = call(
        conv1_edge_kernel,
        (shape(6, F32), shape(6, BF16)),
        [weights],
        (x, gx, gp, hx, hp, conv1_weight, b1),
        "conv1_edges",
        conv_flops,
    )
    st1 = spread(st1)
    n1, a2, s2, c1, st2 = call(
        conv2_kernel,
        (shape(height + 6, BF16), shape(height + 4, F32), shape(height + 4, BF16), vector, stats_shape),
        [weights],
        (st1, a1, a1h, wide_mask, halo_mask, u, conv2_weight, b2, g1, t1),
        "conv2",
        conv_flops,
    )
    st2 = spread(st2)
    d2, dn1, c2, st3 = call(
        back2_kernel,
        (shape(height + 4, BF16), shape(height + 2, F32), vector, stats_shape),
        [turned],
        (st2, c1, a2, s2, u, hx, hp, wide_mask, halo_mask, a1, conv2_weight, g2, t2),
        "conv2_back",
        conv_flops,
    )
    output, w2, bias2 = call(
        weight2_kernel,
        (shape(height, BF16), jax.ShapeDtypeStruct((9 * c, c), BF16), vector),
        [pltpu.VMEM((3 * c, 3 * c), F32)],
        (n1, d2, x, a2, wide_mask, c2),
        "conv2_weight_grad",
        conv_flops,
    )
    st3 = spread(st3)
    chunks = jax.ShapeDtypeStruct((leads, 9 * c // leads + SMALL, c), BF16)
    d1, send, keep = call(
        functools.partial(weight1_kernel, group, leads),
        (shape(height + 2, BF16), chunks, chunks),
        [pltpu.VMEM((3 * c, 3 * c), F32)],
        (st3, c1, c2, dn1, a1, a1h, s1, s1h, wide_mask, halo_mask, x, gx, gp, g1, w2, bias2),
        "conv1_weight_grad",
        conv_flops,
    )
    grad_input = call(
        input_grad_kernel,
        shape(height, BF16),
        [turned],
        (d1, u, conv1_weight),
        "conv1_back",
        conv_flops,
    )
    (k1, small1), (k2, small2) = sum_everywhere(send, keep)
    return (
        output[None],
        grad_input[None],
        k1,
        small1[0],
        small1[1],
        small1[2],
        k2,
        small2[0],
        small2[1],
        small2[2],
    )


def solution(mesh):
    tiles = P("lead", "dp", "lat", None, None)
    in_specs = (tiles, tiles, P("lead", "dp", "lat", None)) + (P(),) * 8
    out_specs = (tiles, tiles) + (P(),) * 8
    return jax.shard_map(shards, mesh=mesh, in_specs=in_specs, out_specs=out_specs, check_vma=False)
```

```python
import functools

import jax
import jax.numpy as jnp
from jax import lax
from jax.experimental import pallas as pl
from jax.experimental.pallas import tpu as pltpu
from jax.sharding import PartitionSpec as P

EPSILON = 1e-05
BF16 = jnp.bfloat16
F32 = jnp.float32
VMEM = pl.BlockSpec(memory_space=pltpu.VMEM)
SMALL = 16


def fill_toeplitz(taps_ref, out_ref):
    c = taps_ref.shape[-1]
    zero = jnp.zeros((c, c), BF16)
    for b in range(3):
        for i in range(4):
            for j in range(2):
                block = taps_ref[i - j, b] if 0 <= i - j < 3 else zero
                out_ref[b, i * c : (i + 1) * c, j * c : (j + 1) * c] = block


def fill_toeplitz_transposed(taps_ref, out_ref):
    c = taps_ref.shape[-1]
    zero = jnp.zeros((c, c), BF16)
    for b in range(3):
        for i in range(4):
            for j in range(2):
                block = taps_ref[2 - (i - j), 2 - b] if 0 <= i - j < 3 else zero
                out_ref[b, j * c : (j + 1) * c, i * c : (i + 1) * c] = block


def column_sum(products, across):
    shaped = [p.reshape(-1, across, p.shape[-1]) for p in products]
    return (
        pltpu.roll(shaped[0], 1, 1) + shaped[1] + pltpu.roll(shaped[2], across - 1, 1)
    )


def convolve_pairs(row, starts, weights_ref, across, transposed):
    left = jnp.concatenate(
        [jnp.concatenate([row(r - 1 + i) for r in starts], 0) for i in range(4)], 1
    )
    dims = (((1,), (1 if transposed else 0,)), ((), ()))
    return column_sum(
        [
            lax.dot_general(left, weights_ref[b], dims, preferred_element_type=F32)
            for b in range(3)
        ],
        across,
    )


def convolve_single(rows, weights_ref, first, across):
    c = rows[0].shape[-1]
    left = jnp.concatenate(rows, 1)
    low, col = (0, 0) if first else (c, c)
    return column_sum(
        [
            jnp.dot(
                left,
                weights_ref[b, low : low + 3 * c, col : col + c],
                preferred_element_type=F32,
            )
            for b in range(3)
        ],
        across,
    )


def silu_and_slope(hidden):
    gate = 0.5 + 0.5 * jnp.tanh(0.5 * hidden)
    active = hidden * gate
    return active, gate + active * (1.0 - gate)


def silu(value):
    return value * (0.5 + 0.5 * jnp.tanh(0.5 * value))


def fold(value):
    return value.reshape(-1, 8, value.shape[-1]).sum(0)


def join(stats, count, at, sums):
    centres = stats[:, at + 2 : at + 3]
    mean = (stats[:, at : at + 1] + sums * centres).sum(0) / count
    away = centres - mean
    squares = stats[:, at + 1 : at + 2] + away * (2.0 * stats[:, at : at + 1] + sums * away)
    variance = jnp.maximum(squares.sum(0) / count, 0.0)
    return mean, lax.rsqrt(variance + EPSILON)


def pick(even, when_even, when_odd):
    return jnp.where(even, when_even, when_odd)


def column_mask(bits_ref, k, c):
    tile = bits_ref[k // 128]
    return jnp.broadcast_to(tile[:, k % 128 : k % 128 + 1].astype(F32), (tile.shape[0], c))


def near_rows_kernel(x_ref, gx_ref, gp_ref, sems):
    height = x_ref.shape[1]
    even = lax.axis_index("lat") % 2 == 0
    last = jnp.where(even, height - 1, 0)
    copies = [
        pltpu.make_async_copy(x_ref.at[:, pl.ds(at, 1)], out, sems.at[i])
        for i, (at, out) in enumerate(((last, gx_ref), (height - 1 - last, gp_ref)))
    ]
    for copy in copies:
        copy.start()
    for copy in copies:
        copy.wait()


def far_rows_kernel(x_ref, u_ref, m_ref, hx_ref, hp_ref, bits_ref):
    samples, height, across, c = x_ref.shape
    even = lax.axis_index("lat") % 2 == 0
    slabs = bits_ref.shape[0]
    for k in range(slabs):
        bits = m_ref[k * 128 : (k + 1) * 128].astype(F32)
        bits = jnp.concatenate([bits, jnp.zeros((bits.shape[0], 128 - across), F32)], 1)
        if bits.shape[0] < 128:
            bits = jnp.concatenate([bits, jnp.zeros((128 - bits.shape[0], 128), F32)], 0)
        tile = bits.T[:across]
        bits_ref[k] = tile
        hx_ref[3 * samples + k] = tile.astype(BF16)
        hp_ref[3 * samples + k] = tile.astype(BF16)
    for out, down in ((hx_ref, even), (hp_ref, jnp.logical_not(even))):
        first = jnp.where(down, height - 3, 1)
        edge = jnp.where(down, height - 1, 0)
        for s in range(samples):
            out[2 * s] = x_ref[s, first]
            out[2 * s + 1] = x_ref[s, first + 1]
            out[2 * samples + s] = u_ref[s, edge]


def stats_block(rows, c):
    return jnp.concatenate(rows + [jnp.zeros((8 - len(rows), c), F32)], 0)


def conv1_kernel(x_ref, gx_ref, gp_ref, bits_ref, w_ref, b_ref, a_ref, s_ref, m_ref, st_ref, t_ref):
    samples, height, across, c = x_ref.shape
    even = lax.axis_index("lat") % 2 == 0
    fill_toeplitz(w_ref, t_ref)
    bias = b_ref[...]
    sums = [jnp.zeros((8, c), F32) for _ in range(3)]
    centre = None
    for s in range(samples):

        def row(r):
            if r < 0:
                return pick(even, gp_ref[s, 0], gx_ref[s, 0])
            if r >= height:
                return pick(even, gx_ref[s, 0], gp_ref[s, 0])
            return x_ref[s, r]

        out = convolve_pairs(row, range(0, height, 2), t_ref, across, False)
        pairs = [silu_and_slope(out[:, :, j * c : (j + 1) * c] + bias) for j in range(2)]
        if s == 0:
            centre = middle([active for active, _ in pairs])
        for j in range(2):
            active, slope = pairs[j]
            active = active - centre
            for q in range(height // 2):
                r = 2 * q + j
                mask = column_mask(bits_ref, s * height + r, c)
                a_ref[s, r] = active[q].astype(BF16)
                s_ref[s, r] = (slope[q] * mask).astype(BF16)
                m_ref[s, r] = mask.astype(BF16)
                masked = active[q] * mask
                sums[0] += fold(masked)
                sums[1] += fold(masked * active[q])
                sums[2] += fold(mask)
    rows = [v.sum(0, keepdims=True) for v in sums]
    st_ref[...] = stats_block([rows[0], rows[1], centre, rows[2]], c)


def middle(parts):
    total = functools.reduce(lambda a, b: a + b, [fold(p) for p in parts])
    return total.sum(0, keepdims=True) / sum(p.size // p.shape[-1] for p in parts)


def conv1_edge_kernel(x_ref, gx_ref, gp_ref, hx_ref, hp_ref, st_ref, w_ref, b_ref, a_ref, t_ref):
    samples, height, across, c = x_ref.shape
    even = lax.axis_index("lat") % 2 == 0
    fill_toeplitz(w_ref, t_ref)
    bias = b_ref[...]
    centre = st_ref[2:3]

    def row(r):
        parts = []
        for s in range(samples):
            if r < -1:
                parts.append(pick(even, hp_ref[2 * s + r + 3], hx_ref[2 * s + r + 3]))
            elif r == -1:
                parts.append(pick(even, gp_ref[s, 0], gx_ref[s, 0]))
            elif r < height:
                parts.append(x_ref[s, r])
            elif r == height:
                parts.append(pick(even, gx_ref[s, 0], gp_ref[s, 0]))
            else:
                j = r - height - 1
                parts.append(pick(even, hx_ref[2 * s + j], hp_ref[2 * s + j]))
        return jnp.concatenate(parts, 0)

    for slot, start in ((0, -2), (2, height)):
        out = convolve_pairs(row, (start,), t_ref, across, False)
        for j in range(2):
            active = silu(out[:, :, j * c : (j + 1) * c] + bias) - centre
            for s in range(samples):
                a_ref[s, slot + j] = active[s].astype(BF16)


def conv2_kernel(
    st_ref, own_ref, a_ref, ah_ref, m_ref, hx_ref, hp_ref, u_ref, w_ref, b_ref, g_ref, t_ref,
    n_ref, a2_ref, s2_ref, c1_ref, st2_ref, k_ref, ext_ref,
):
    samples, height, across, c = a_ref.shape
    even = lax.axis_index("lat") % 2 == 0
    fill_toeplitz(w_ref, k_ref)
    counts = st_ref[:, 3:4]
    count = counts.sum(0)
    mean, inverse = join(st_ref, count, 0, counts)
    offset = mean - own_ref[2:3]
    scale = inverse * g_ref[...]
    shift = t_ref[...] - offset * scale
    c1_ref[...] = stats_block([offset, inverse, count, mean], c)
    bias = b_ref[...]
    slabs = slice(3 * samples, hx_ref.shape[0])

    def halo_mask(s, r):
        if r < 0:
            k = s * height + height + r
            refs = (hp_ref.at[slabs], hx_ref.at[slabs])
        else:
            k = s * height + r - height
            refs = (hx_ref.at[slabs], hp_ref.at[slabs])
        return column_mask(pick(even, refs[0][...], refs[1][...]), k, c)

    sums = [jnp.zeros((8, c), F32) for _ in range(4)]
    centre = None
    for s in range(samples):
        ext = ext_ref.at[s % 2]
        for i in range(height + 4):
            r = i - 2
            if 0 <= r < height:
                value = a_ref[s, r].astype(F32) * scale + shift
                ext[i] = value.astype(BF16) * m_ref[s, r]
            else:
                value = ah_ref[s, i if r < 0 else r - height + 2].astype(F32) * scale + shift
                ext[i] = (value * halo_mask(s, r)).astype(BF16)
            if 1 <= i < height + 3:
                n_ref[s, i - 1] = ext[i]

        out = convolve_pairs(
            lambda r: ext[r + 2], range(-1, height + 1, 2), k_ref, across, False
        )
        pairs = [silu_and_slope(out[:, :, j * c : (j + 1) * c] + bias) for j in range(2)]
        if s == 0:
            centre = middle([active for active, _ in pairs])
        for j in range(2):
            active, slope = pairs[j]
            active = active - centre
            for q in range(height // 2 + 1):
                i = 2 * q + j
                r = i - 1
                mask = m_ref[s, r].astype(F32) if 0 <= r < height else halo_mask(s, r)
                a2_ref[s, i] = active[q].astype(BF16)
                s2_ref[s, i] = (slope[q] * mask).astype(BF16)
                if 0 <= r < height:
                    masked = active[q] * mask
                    upstream = u_ref[s, r].astype(F32)
                    sums[0] += fold(masked)
                    sums[1] += fold(masked * active[q])
                    sums[2] += fold(masked * upstream)
                    sums[3] += fold(mask * upstream)
    rows = [v.sum(0, keepdims=True) for v in sums]
    st2_ref[...] = stats_block(
        [rows[0], rows[1], centre, rows[2], rows[3], own_ref[3:4]], c
    )


def back_terms(scale, inverse, offset, gain_sum, shift_sum, count):
    by_active = -scale * gain_sum * inverse / count
    constant = -scale * (shift_sum - offset * inverse * gain_sum) / count
    return by_active, constant


def back2_kernel(
    st_ref, own_ref, st1_ref, c1_ref, a2_ref, s2_ref, u_ref, hx_ref, hp_ref, m_ref, a1_ref, w_ref, g_ref, t_ref,
    d_ref, dn_ref, c2_ref, st3_ref, k_ref, ext_ref,
):
    samples, height, across, c = u_ref.shape
    even = lax.axis_index("lat") % 2 == 0
    fill_toeplitz_transposed(w_ref, k_ref)
    count = c1_ref[2:3]
    mean, inverse = join(st_ref, count, 0, st_ref[:, 5:6])
    offset = mean - own_ref[2:3]
    shift_sum = st_ref[:, 4:5].sum(0)
    away = st_ref[:, 2:3] - mean
    gain_sum = inverse * (st_ref[:, 3:4] + away * st_ref[:, 4:5]).sum(0)
    scale = inverse * g_ref[...]
    by_active, constant = back_terms(scale, inverse, offset, gain_sum, shift_sum, count)
    c2_ref[...] = stats_block([scale, t_ref[...] - offset * scale, gain_sum, shift_sum], c)
    sums = [jnp.zeros((8, c), F32) for _ in range(2)]
    for s in range(samples):
        ext = ext_ref.at[s % 2]
        for i in range(height + 2):
            r = i - 1
            if r < 0:
                upstream = pick(even, hp_ref[2 * samples + s], hx_ref[2 * samples + s])
            elif r >= height:
                upstream = pick(even, hx_ref[2 * samples + s], hp_ref[2 * samples + s])
            else:
                upstream = u_ref[s, r]
            grad = upstream.astype(F32) * scale + (a2_ref[s, i].astype(F32) * by_active + constant)
            ext[i] = (grad * s2_ref[s, i].astype(F32)).astype(BF16)
            if 0 <= r < height:
                d_ref[s, r] = ext[i]
        out = convolve_pairs(
            lambda r: ext[r + 1], range(0, height, 2), k_ref, across, True
        )
        for j in range(2):
            part = out[:, :, j * c : (j + 1) * c]
            for q in range(height // 2):
                r = 2 * q + j
                dn_ref[s, r] = part[q]
                masked = part[q] * m_ref[s, r].astype(F32)
                sums[0] += fold(masked)
                sums[1] += fold(masked * a1_ref[s, r].astype(F32))
    rows = [v.sum(0, keepdims=True) for v in sums]
    st3_ref[...] = stats_block([rows[0], rows[1], st1_ref[2:3]], c)


def weight_products(rows, centre, turned, total_ref, first):
    windows = jnp.concatenate(rows, 1)
    product = lax.dot_general(
        windows,
        jnp.concatenate([turned[0], centre, turned[1]], 1),
        (((0,), (0,)), ((), ())),
        preferred_element_type=F32,
    )
    if first:
        total_ref[...] = product
    else:
        total_ref[...] += product


def turn(value, across):
    c = value.shape[-1]
    return [
        pltpu.roll(value, k, 1).astype(BF16).reshape(-1, c) for k in (across - 1, 1)
    ]


def weight2_kernel(n_ref, d_ref, x_ref, a2_ref, m_ref, c2_ref, o_ref, w_ref, b_ref, acc_ref):
    samples, height, across, c = x_ref.shape
    scale, shift = c2_ref[0:1], c2_ref[1:2]
    bias = jnp.zeros((8, c), F32)
    for s in range(samples):
        grad = d_ref[s]
        wide = grad.astype(F32)
        bias += fold(wide)
        rows = [n_ref[s, a : a + height].reshape(-1, c) for a in range(3)]
        weight_products(rows, grad.reshape(-1, c), turn(wide, across), acc_ref, s == 0)
        for r in range(height):
            normed = (a2_ref[s, r + 1].astype(F32) * scale + shift) * m_ref[s, r].astype(F32)
            o_ref[s, r] = (x_ref[s, r].astype(F32) + normed).astype(BF16)
    b_ref[...] = jnp.broadcast_to(bias.sum(0, keepdims=True), b_ref.shape)
    for a in range(3):
        for b in range(3):
            at = (a * 3 + b) * c
            w_ref[at : at + c] = acc_ref[a * c : (a + 1) * c, b * c : (b + 1) * c].astype(BF16)


def small_rows(rows, c):
    high = jnp.concatenate(rows + [jnp.zeros((8 - len(rows), c), F32)], 0)
    first = high.astype(BF16)
    return jnp.concatenate([first, (high - first.astype(F32)).astype(BF16)], 0)


def weight1_kernel(
    group, leads,
    st_ref, c1_ref, c2_ref, dn_ref, a_ref, s_ref, x_ref, gx_ref, gp_ref, g_ref, w2_ref, b2_ref,
    d_ref, dx_ref, dp_ref, send_ref, keep_ref, acc_ref,
):
    samples, height, across, c = x_ref.shape
    even = lax.axis_index("lat") % 2 == 0
    lead = lax.axis_index("lead")
    core = lax.axis_index("dp") % 2
    offset, inverse, count, mean = (c1_ref[i : i + 1] for i in range(4))
    shift_sum = st_ref[:, 0:1].sum(0)
    away = st_ref[:, 2:3] - mean
    gain_sum = inverse * (st_ref[:, 1:2] + away * st_ref[:, 0:1]).sum(0)
    scale = inverse * g_ref[...]
    by_active, constant = back_terms(scale, inverse, offset, gain_sum, shift_sum, count)
    bias = jnp.zeros((8, c), F32)
    for s in range(samples):
        grad = dn_ref[s] * scale + (a_ref[s].astype(F32) * by_active + constant)
        grad = (grad * s_ref[s].astype(F32)).astype(BF16)
        d_ref[s] = grad
        dx_ref[s] = pick(even, grad[height - 1], grad[0])
        dp_ref[s] = pick(even, grad[0], grad[height - 1])
        wide = grad.astype(F32)
        bias += fold(wide)
        above = pick(even, gp_ref[s, 0], gx_ref[s, 0])
        below = pick(even, gx_ref[s, 0], gp_ref[s, 0])
        body = x_ref[s].reshape(-1, c)
        rows = [
            jnp.concatenate([above, body[: (height - 1) * across]], 0),
            body,
            jnp.concatenate([body[across:], below], 0),
        ]
        weight_products(rows, grad.reshape(-1, c), turn(wide, across), acc_ref, s == 0)

    share = 1.0 / group
    small = [
        small_rows([bias.sum(0, keepdims=True), gain_sum * share, shift_sum * share], c),
        small_rows([b2_ref[0:1], c2_ref[2:3] * share, c2_ref[3:4] * share], c),
    ]

    def put(target, which):
        size = 9 * c // leads
        for j in range(leads):
            slot = j ^ lead
            if which == 1:
                target[slot, :size] = w2_ref[j * size : (j + 1) * size]
            else:
                at = j * size
                while at < (j + 1) * size:
                    tap, low = at // c, at % c
                    step = min(c - low, (j + 1) * size - at)
                    a, b = tap // 3, tap % 3
                    target[slot, at - j * size : at - j * size + step] = acc_ref[
                        a * c + low : a * c + low + step, b * c : (b + 1) * c
                    ].astype(BF16)
                    at += step
            target[slot, size:] = small[which]

    @pl.when(core == 0)
    def _():
        put(keep_ref, 0)
        put(send_ref, 1)

    @pl.when(core != 0)
    def _():
        put(keep_ref, 1)
        put(send_ref, 0)


def input_grad_kernel(d_ref, ex_ref, ep_ref, u_ref, w_ref, o_ref, k_ref):
    samples, height, across, c = u_ref.shape
    even = lax.axis_index("lat") % 2 == 0
    fill_toeplitz_transposed(w_ref, k_ref)
    for s in range(samples):

        def row(r):
            if r < 0:
                return pick(even, ep_ref[s], ex_ref[s])
            if r >= height:
                return pick(even, ex_ref[s], ep_ref[s])
            return d_ref[s, r]

        out = convolve_pairs(row, range(0, height, 2), k_ref, across, True)
        for q in range(height // 2):
            for j in range(2):
                r = 2 * q + j
                o_ref[s, r] = (
                    u_ref[s, r].astype(F32) + out[q, :, j * c : (j + 1) * c]
                ).astype(BF16)


def finish_kernel(leads, mine_ref, *refs):
    got_refs, other_ref = refs[: leads - 1], refs[leads - 1]
    first, second = refs[leads : leads + 4], refs[leads + 4 :]
    core = lax.axis_index("dp") % 2
    lead = lax.axis_index("lead")
    size = mine_ref.shape[0] - SMALL

    def put(outs, chunk, small):
        for k in range(leads):
            at = pl.multiple_of((k ^ lead) * size, 16)
            outs[0][pl.ds(at, size)] = chunk(k).astype(F32)
        total = small[:8].astype(F32) + small[8:].astype(F32)
        for i in range(3):
            outs[i + 1][...] = total[i : i + 1]

    def own(outs):
        put(outs, lambda k: got_refs[k - 1][...] if k else mine_ref[:size], mine_ref[size:])

    def other(outs):
        put(
            outs,
            lambda k: other_ref[k * size : (k + 1) * size],
            other_ref[leads * size :],
        )

    @pl.when(core == 0)
    def _():
        own(first)
        other(second)

    @pl.when(core != 0)
    def _():
        other(first)
        own(second)


def call(kernel, outs, scratch, operands, name, flops=0, space=VMEM):
    size = sum(o.size * o.dtype.itemsize for o in operands)
    return pl.pallas_call(
        kernel,
        out_shape=outs,
        in_specs=[space] * len(operands),
        out_specs=jax.tree.map(lambda _: space, outs),
        scratch_shapes=scratch,
        compiler_params=pltpu.CompilerParams(vmem_limit_bytes=24 * 2**20),
        cost_estimate=pl.CostEstimate(flops=flops, bytes_accessed=size, transcendentals=0),
        name=name,
    )(*operands)


def swap(value, axis, k):
    return lax.ppermute(value, axis, [(i, i ^ k) for i in range(lax.axis_size(axis))])


def neighbours(value_x, value_p, axis):
    n = lax.axis_size(axis)
    first = [(i, i ^ 1) for i in range(n) if i ^ 1 < n]
    second = [(i, i + 1) for i in range(1, n - 1, 2)]
    second += [(j, i) for i, j in second]
    return lax.ppermute(value_x, axis, first), lax.ppermute(value_p, axis, second)


def spread(stats):
    blocks, k = stats[None], 1
    while k < lax.axis_size("dp"):
        blocks = jnp.concatenate([blocks, swap(blocks, "dp", k)], 0)
        k *= 2
    others = [swap(blocks, "lat", k) for k in range(1, lax.axis_size("lat"))]
    return jnp.concatenate([blocks] + others, 0)


def add_chunks(parts):
    total = functools.reduce(lambda a, b: a + b, [p.astype(F32) for p in parts])
    size = total.shape[-2] - SMALL
    small = total[..., size : size + 8, :] + total[..., size + 8 :, :]
    high = lax.reduce_precision(small, 8, 7)
    return jnp.concatenate(
        [total[..., :size, :].astype(BF16), high.astype(BF16), (small - high).astype(BF16)], -2
    )


def sum_everywhere(send, keep):
    leads, lats = lax.axis_size("lead"), lax.axis_size("lat")
    chunks = add_chunks([keep, swap(send, "dp", 1)])
    mine = add_chunks([chunks[0]] + [swap(chunks[k], "lead", k) for k in range(1, leads)])
    mine = add_chunks([mine] + [swap(mine, "lat", k) for k in range(1, lats)])
    k = 2
    while k < lax.axis_size("dp"):
        mine = add_chunks([mine, swap(mine, "dp", k)])
        k *= 2
    size = mine.shape[0] - SMALL
    c = mine.shape[1]
    got = [swap(mine[:size], "lead", k) for k in range(1, leads)]
    other = swap(jnp.concatenate([mine[:size]] + got + [mine[size:]], 0), "dp", 1)
    one = [jax.ShapeDtypeStruct((leads * size, c), F32)] + [jax.ShapeDtypeStruct((1, c), F32)] * 3
    outs = call(
        functools.partial(finish_kernel, leads), one + one, [], (mine, *got, other), "finish"
    )
    return outs[:4], outs[4:]


def shards(
    field,
    cotangent,
    land_sea,
    conv1_weight,
    conv1_bias,
    first_norm_scale,
    norm1_shift,
    conv2_weight,
    conv2_bias,
    second_norm_scale,
    norm2_shift,
):
    x, u, mask = field[0], cotangent[0], land_sea[0]
    samples, height, across, c = x.shape
    group = lax.axis_size("dp") * lax.axis_size("lat")
    leads = lax.axis_size("lead")
    slabs = -(-samples * height // 128)
    vec = lambda v: v.reshape(1, c)
    b1, g1, t1 = vec(conv1_bias), vec(first_norm_scale), vec(norm1_shift)
    b2, g2, t2 = vec(conv2_bias), vec(second_norm_scale), vec(norm2_shift)

    shape = lambda rows, dtype=BF16: jax.ShapeDtypeStruct((samples, rows, across, c), dtype)
    edge = jax.ShapeDtypeStruct((samples, across, c), BF16)
    vector = jax.ShapeDtypeStruct((8, c), F32)
    weights = pltpu.VMEM((3, 4 * c, 2 * c), BF16)
    turned = pltpu.VMEM((3, 2 * c, 4 * c), BF16)
    ext = lambda rows: pltpu.VMEM((2, rows, across, c), BF16)
    acc = pltpu.VMEM((3 * c, 3 * c), F32)
    conv_flops = 2 * 9 * c * c * samples * height * across

    near = call(
        near_rows_kernel,
        (shape(1), shape(1)),
        [pltpu.SemaphoreType.DMA((2,))],
        (x,),
        "near_rows",
        space=pl.BlockSpec(memory_space=pl.ANY),
    )
    gx, gp = neighbours(*near, "lat")
    packed = jax.ShapeDtypeStruct((3 * samples + slabs, across, c), BF16)
    far_x, far_p, bits = call(
        far_rows_kernel,
        (packed, packed, jax.ShapeDtypeStruct((slabs, across, 128), F32)),
        [],
        (x, u, mask.reshape(samples * height, across)),
        "far_rows",
        conv_flops,
    )
    hx, hp = neighbours(far_x, far_p, "lat")

    a1, s1, wide_mask, own1 = call(
        conv1_kernel,
        (shape(height), shape(height), shape(height), vector),
        [weights],
        (x, gx, gp, bits, conv1_weight, b1),
        "conv1",
        conv_flops,
    )
    a1h = call(
        conv1_edge_kernel,
        shape(4),
        [weights],
        (x, gx, gp, hx, hp, own1, conv1_weight, b1),
        "conv1_edges",
        conv_flops,
    )
    st1 = spread(own1)
    n1, a2, s2, c1, own2 = call(
        conv2_kernel,
        (shape(height + 2), shape(height + 2), shape(height + 2), vector, vector),
        [weights, ext(height + 4)],
        (st1, own1, a1, a1h, wide_mask, hx, hp, u, conv2_weight, b2, g1, t1),
        "conv2",
        conv_flops,
    )
    st2 = spread(own2)
    d2, dn1, c2, own3 = call(
        back2_kernel,
        (shape(height), shape(height, F32), vector, vector),
        [turned, ext(height + 2)],
        (st2, own2, own1, c1, a2, s2, u, hx, hp, wide_mask, a1, conv2_weight, g2, t2),
        "conv2_back",
        conv_flops,
    )
    output, w2, bias2 = call(
        weight2_kernel,
        (shape(height), jax.ShapeDtypeStruct((9 * c, c), BF16), vector),
        [acc],
        (n1, d2, x, a2, wide_mask, c2),
        "conv2_weight_grad",
        conv_flops,
    )
    st3 = spread(own3)
    chunks = jax.ShapeDtypeStruct((leads, 9 * c // leads + SMALL, c), BF16)
    d1, dx, dp, send, keep = call(
        functools.partial(weight1_kernel, group, leads),
        (shape(height), edge, edge, chunks, chunks),
        [acc],
        (st3, c1, c2, dn1, a1, s1, x, gx, gp, g1, w2, bias2),
        "conv1_weight_grad",
        conv_flops,
    )
    dx, dp = neighbours(dx, dp, "lat")
    grad_input = call(
        input_grad_kernel,
        shape(height),
        [turned],
        (d1, dx, dp, u, conv1_weight),
        "conv1_back",
        conv_flops,
    )
    first, second = sum_everywhere(send, keep)
    sums = []
    for part in (first, second):
        sums += [part[0].reshape(3, 3, c, c)] + [v.reshape(c) for v in part[1:]]
    return (output[None], grad_input[None], *sums)


def solution(mesh):
    tiles = P("lead", "dp", "lat", None, None)
    in_specs = (tiles, tiles, P("lead", "dp", "lat", None)) + (P(),) * 8
    out_specs = (tiles, tiles) + (P(),) * 8
    return jax.shard_map(shards, mesh=mesh, in_specs=in_specs, out_specs=out_specs, check_vma=False)
```

```python
import functools

import jax
import jax.numpy as jnp
from jax import lax
from jax.experimental import pallas as pl
from jax.experimental.pallas import tpu as pltpu
from jax.sharding import PartitionSpec as P

EPSILON = 1e-05
BF16 = jnp.bfloat16
F32 = jnp.float32
VMEM = pl.BlockSpec(memory_space=pltpu.VMEM)
SMALL = 16


def fill_toeplitz(taps_ref, out_ref):
    c = taps_ref.shape[-1]
    zero = jnp.zeros((c, c), BF16)
    for b in range(3):
        for i in range(4):
            for j in range(2):
                block = taps_ref[i - j, b] if 0 <= i - j < 3 else zero
                out_ref[b, i * c : (i + 1) * c, j * c : (j + 1) * c] = block


def fill_toeplitz_transposed(taps_ref, out_ref):
    c = taps_ref.shape[-1]
    zero = jnp.zeros((c, c), BF16)
    for b in range(3):
        for i in range(4):
            for j in range(2):
                block = taps_ref[2 - (i - j), 2 - b] if 0 <= i - j < 3 else zero
                out_ref[b, j * c : (j + 1) * c, i * c : (i + 1) * c] = block


def convolve_rows(row, starts, weights_ref, across, transposed):
    left = jnp.concatenate(
        [jnp.concatenate([row(r - 1 + i) for r in starts], 0) for i in range(4)], 1
    )
    c = left.shape[1] // 4
    dims = (((1,), (1 if transposed else 0,)), ((), ()))
    taps = [
        lax.dot_general(left, weights_ref[b], dims, preferred_element_type=F32)
        for b in range(3)
    ]

    def piece(pair, j):
        part = [t[pair * across : (pair + 1) * across, j * c : (j + 1) * c] for t in taps]
        return pltpu.roll(part[0], 1, 0) + part[1] + pltpu.roll(part[2], across - 1, 0)

    return piece


def silu_and_slope(hidden):
    gate = 0.5 + 0.5 * jnp.tanh(0.5 * hidden)
    active = hidden * gate
    return active, gate + active * (1.0 - gate)


def silu(value):
    return value * (0.5 + 0.5 * jnp.tanh(0.5 * value))


def fold(value):
    return value.reshape(-1, 8, value.shape[-1]).sum(0)


def join(stats, count, at, sums):
    centres = stats[:, at + 2 : at + 3]
    mean = (stats[:, at : at + 1] + sums * centres).sum(0) / count
    away = centres - mean
    squares = stats[:, at + 1 : at + 2] + away * (2.0 * stats[:, at : at + 1] + sums * away)
    variance = jnp.maximum(squares.sum(0) / count, 0.0)
    return mean, lax.rsqrt(variance + EPSILON)


def pick(even, when_even, when_odd):
    return jnp.where(even, when_even, when_odd)


def column_mask(bits, k, c):
    tile = bits[k // 128]
    return jnp.broadcast_to(tile[:, k % 128 : k % 128 + 1].astype(F32), (tile.shape[0], c))


def near_rows_kernel(x_ref, gx_ref, gp_ref, sems):
    height = x_ref.shape[1]
    even = lax.axis_index("lat") % 2 == 0
    last = jnp.where(even, height - 1, 0)
    copies = [
        pltpu.make_async_copy(x_ref.at[:, pl.ds(at, 1)], out, sems.at[i])
        for i, (at, out) in enumerate(((last, gx_ref), (height - 1 - last, gp_ref)))
    ]
    for copy in copies:
        copy.start()
    for copy in copies:
        copy.wait()


def far_rows_kernel(x_ref, u_ref, bits_ref, gx_ref, gp_ref, hx_ref, hp_ref):
    samples, height, across, c = x_ref.shape
    even = lax.axis_index("lat") % 2 == 0
    for out, down in ((hx_ref, even), (hp_ref, jnp.logical_not(even))):
        first = jnp.where(down, height - 3, 1)
        edge = jnp.where(down, height - 1, 0)
        for s in range(samples):
            out[2 * s] = x_ref[s, first]
            out[2 * s + 1] = x_ref[s, first + 1]
            out[2 * samples + s] = u_ref[s, edge]
        for k in range(bits_ref.shape[0]):
            out[3 * samples + k] = bits_ref[k].astype(BF16)


def stats_block(rows, c):
    return jnp.concatenate(rows + [jnp.zeros((8 - len(rows), c), F32)], 0)


def gather(refs):
    return jnp.concatenate([r[...] for r in refs], 0)


def own_row(inner_ref, outer_ref, s, r, height):
    if 2 <= r < height - 2:
        return inner_ref[s, r - 2]
    return outer_ref[s, r if r < 2 else r - height + 4]


def middle(value):
    return value.mean(0, keepdims=True)


def add_moments(sums, active, mask):
    masked = active * mask
    sums[0] += fold(masked)
    sums[1] += fold(masked * active)
    return masked


def conv1_inner_kernel(x_ref, mask_ref, w_ref, b_ref, a_ref, s_ref, m_ref, bits_ref, t_ref, st_ref):
    samples, height, across, c = x_ref.shape
    for k in range(bits_ref.shape[0]):
        bits = mask_ref[k * 128 : (k + 1) * 128].astype(F32)
        bits = jnp.concatenate([bits, jnp.zeros((bits.shape[0], 128 - across), F32)], 1)
        if bits.shape[0] < 128:
            bits = jnp.concatenate([bits, jnp.zeros((128 - bits.shape[0], 128), F32)], 0)
        bits_ref[k] = bits.T[:across]
    fill_toeplitz(w_ref, t_ref)
    bias = b_ref[...]
    sums = [jnp.zeros((8, c), F32) for _ in range(3)]
    centre = None
    for s in range(samples):
        piece = convolve_rows(lambda r: x_ref[s, r], range(2, height - 2, 2), t_ref, across, False)
        for r in range(height):
            mask = column_mask(bits_ref, s * height + r, c)
            m_ref[s, r] = mask
            sums[2] += fold(mask)
            if not 2 <= r < height - 2:
                continue
            active, slope = silu_and_slope(piece((r - 2) // 2, r % 2) + bias)
            if centre is None:
                centre = middle(active)
            active = active - centre
            a_ref[s, r - 2] = active
            s_ref[s, r - 2] = slope * mask
            add_moments(sums, active, mask)
    rows = [v.sum(0, keepdims=True) for v in sums]
    st_ref[...] = stats_block([rows[0], rows[1], centre, rows[2]], c)


def conv1_outer_kernel(x_ref, gx_ref, gp_ref, m_ref, t_ref, b_ref, part_ref, a_ref, s_ref, st_ref):
    samples, height, across, c = x_ref.shape
    even = lax.axis_index("lat") % 2 == 0
    bias = b_ref[...]
    centre = part_ref[2:3]

    def row(r):
        if r < 0:
            parts = [pick(even, gp_ref[s, 0], gx_ref[s, 0]) for s in range(samples)]
        elif r >= height:
            parts = [pick(even, gx_ref[s, 0], gp_ref[s, 0]) for s in range(samples)]
        else:
            parts = [x_ref[s, r] for s in range(samples)]
        return jnp.concatenate(parts, 0)

    sums = [jnp.zeros((8, c), F32) for _ in range(2)]
    for slot, start in ((0, 0), (2, height - 2)):
        piece = convolve_rows(row, (start,), t_ref, across, False)
        for s in range(samples):
            for j in range(2):
                active, slope = silu_and_slope(piece(s, j) + bias)
                active = active - centre
                mask = m_ref[s, start + j]
                a_ref[s, slot + j] = active
                s_ref[s, slot + j] = slope * mask
                add_moments(sums, active, mask)
    rows = [part_ref[i : i + 1] + v.sum(0, keepdims=True) for i, v in enumerate(sums)]
    st_ref[...] = stats_block([rows[0], rows[1], centre, part_ref[3:4]], c)


def conv1_edge_kernel(
    x_ref, gx_ref, gp_ref, hx_ref, hp_ref, u_ref, m_ref, st_ref, t_ref, b_ref, w2_ref,
    a_ref, mh_ref, mu_ref, su_ref, t2_ref, tt2_ref,
):
    samples, height, across, c = x_ref.shape
    even = lax.axis_index("lat") % 2 == 0
    fill_toeplitz(w2_ref, t2_ref)
    fill_toeplitz_transposed(w2_ref, tt2_ref)
    bias = b_ref[...]
    centre = st_ref[2:3]

    def row(r):
        parts = []
        for s in range(samples):
            if r < -1:
                parts.append(pick(even, hp_ref[2 * s + r + 3], hx_ref[2 * s + r + 3]))
            elif r == -1:
                parts.append(pick(even, gp_ref[s, 0], gx_ref[s, 0]))
            elif r < height:
                parts.append(x_ref[s, r])
            elif r == height:
                parts.append(pick(even, gx_ref[s, 0], gp_ref[s, 0]))
            else:
                j = r - height - 1
                parts.append(pick(even, hx_ref[2 * s + j], hp_ref[2 * s + j]))
        return jnp.concatenate(parts, 0)

    slabs = slice(3 * samples, hx_ref.shape[0])
    above = pick(even, hp_ref[slabs], hx_ref[slabs])
    below = pick(even, hx_ref[slabs], hp_ref[slabs])
    total = jnp.zeros((8, c), F32)
    for slot, start in ((0, -2), (2, height)):
        piece = convolve_rows(row, (start,), t_ref, across, False)
        for s in range(samples):
            for j in range(2):
                a_ref[s, slot + j] = silu(piece(s, j) + bias) - centre
                if start < 0:
                    mask = column_mask(above, s * height + height - 2 + j, c)
                else:
                    mask = column_mask(below, s * height + j, c)
                mh_ref[s, slot + j] = mask
    for s in range(samples):
        up = pick(even, hp_ref[2 * samples + s], hx_ref[2 * samples + s])
        mu_ref[s, 0] = up.astype(F32) * mh_ref[s, 1]
        for r in range(height):
            value = u_ref[s, r].astype(F32) * m_ref[s, r]
            mu_ref[s, r + 1] = value
            total += fold(value)
        down = pick(even, hx_ref[2 * samples + s], hp_ref[2 * samples + s])
        mu_ref[s, height + 1] = down.astype(F32) * mh_ref[s, 2]
    su_ref[...] = stats_block([total.sum(0, keepdims=True)], c)


def conv2_kernel(
    pieces,
    own_ref, a_ref, ao_ref, ah_ref, m_ref, mh_ref, mu_ref, su_ref, k_ref, b_ref, g_ref, t_ref, *refs,
):
    stats, (n_ref, a2_ref, s2_ref, c1_ref, st2_ref, ext_ref) = gather(refs[:pieces]), refs[pieces:]
    samples, height, across, c = m_ref.shape
    counts = stats[:, 3:4]
    count = counts.sum(0)
    mean, inverse = join(stats, count, 0, counts)
    offset = mean - own_ref[2:3]
    scale = inverse * g_ref[...]
    shift = t_ref[...] - offset * scale
    c1_ref[...] = stats_block([offset, inverse, count, mean], c)
    bias = b_ref[...]
    sums = [jnp.zeros((8, c), F32) for _ in range(3)]
    centre = None
    for s in range(samples):
        ext = ext_ref.at[s % 2]
        for i in range(height + 4):
            r = i - 2
            if 0 <= r < height:
                value, mask = own_row(a_ref, ao_ref, s, r, height), m_ref[s, r]
            else:
                j = i if r < 0 else r - height + 2
                value, mask = ah_ref[s, j], mh_ref[s, j]
            ext[i] = ((value * scale + shift) * mask).astype(BF16)
            if 1 <= i < height + 3:
                n_ref[s, i - 1] = ext[i]

        piece = convolve_rows(
            lambda r: ext[r + 2], range(-1, height + 1, 2), k_ref, across, False
        )
        for i in range(height + 2):
            r = i - 1
            active, slope = silu_and_slope(piece(i // 2, i % 2) + bias)
            if centre is None:
                centre = middle(active)
            active = active - centre
            if 0 <= r < height:
                mask = m_ref[s, r]
                add_moments(sums, active, mask)
                sums[2] += fold(active * mu_ref[s, i])
            else:
                mask = mh_ref[s, 1 if r < 0 else 2]
            a2_ref[s, i] = active
            s2_ref[s, i] = slope * mask
    rows = [v.sum(0, keepdims=True) for v in sums]
    st2_ref[...] = stats_block(
        [rows[0], rows[1], centre, rows[2], su_ref[0:1], own_ref[3:4]], c
    )


def back_terms(scale, inverse, offset, gain_sum, shift_sum, count):
    by_active = -scale * gain_sum * inverse / count
    constant = -scale * (shift_sum - offset * inverse * gain_sum) / count
    return by_active, constant


def back2_kernel(
    pieces,
    own_ref, st1_ref, c1_ref, a2_ref, s2_ref, mu_ref, m_ref, a_ref, ao_ref, k_ref, g_ref, t_ref, *refs,
):
    stats, (d_ref, dn_ref, c2_ref, st3_ref, ext_ref) = gather(refs[:pieces]), refs[pieces:]
    samples, height, across, c = m_ref.shape
    count = c1_ref[2:3]
    mean, inverse = join(stats, count, 0, stats[:, 5:6])
    offset = mean - own_ref[2:3]
    shift_sum = stats[:, 4:5].sum(0)
    away = stats[:, 2:3] - mean
    gain_sum = inverse * (stats[:, 3:4] + away * stats[:, 4:5]).sum(0)
    scale = inverse * g_ref[...]
    by_active, constant = back_terms(scale, inverse, offset, gain_sum, shift_sum, count)
    c2_ref[...] = stats_block([scale, t_ref[...] - offset * scale, gain_sum, shift_sum], c)
    sums = [jnp.zeros((8, c), F32) for _ in range(2)]
    for s in range(samples):
        ext = ext_ref.at[s % 2]
        for i in range(height + 2):
            grad = mu_ref[s, i] * scale + (a2_ref[s, i] * by_active + constant)
            ext[i] = (grad * s2_ref[s, i]).astype(BF16)
            if 0 < i <= height:
                d_ref[s, i - 1] = ext[i]
        piece = convolve_rows(
            lambda r: ext[r + 1], range(0, height, 2), k_ref, across, True
        )
        for r in range(height):
            part = piece(r // 2, r % 2)
            dn_ref[s, r] = part
            masked = part * m_ref[s, r]
            sums[0] += fold(masked)
            sums[1] += fold(masked * own_row(a_ref, ao_ref, s, r, height))
    rows = [v.sum(0, keepdims=True) for v in sums]
    st3_ref[...] = stats_block([rows[0], rows[1], st1_ref[2:3]], c)


def weight_products(rows, centre, turned, total_ref, first):
    windows = jnp.concatenate(rows, 1)
    product = lax.dot_general(
        windows,
        jnp.concatenate([turned[0], centre, turned[1]], 1),
        (((0,), (0,)), ((), ())),
        preferred_element_type=F32,
    )
    if first:
        total_ref[...] = product
    else:
        total_ref[...] += product


def turn(value, across):
    c = value.shape[-1]
    return [
        pltpu.roll(value, k, 1).astype(BF16).reshape(-1, c) for k in (across - 1, 1)
    ]


def weight2_kernel(n_ref, d_ref, after_ref, w_ref, b_ref, acc_ref):
    samples, height, across, c = d_ref.shape
    bias = jnp.zeros((8, c), F32)
    for s in range(samples):
        grad = d_ref[s]
        wide = grad.astype(F32)
        bias += fold(wide)
        rows = [n_ref[s, a : a + height].reshape(-1, c) for a in range(3)]
        weight_products(rows, grad.reshape(-1, c), turn(wide, across), acc_ref, s == 0)
    b_ref[...] = jnp.broadcast_to(bias.sum(0, keepdims=True), b_ref.shape)
    for a in range(3):
        for b in range(3):
            at = (a * 3 + b) * c
            w_ref[at : at + c] = acc_ref[a * c : (a + 1) * c, b * c : (b + 1) * c].astype(BF16)


def output_kernel(x_ref, a2_ref, m_ref, c2_ref, after_ref, o_ref, done_ref):
    samples, height, across, c = x_ref.shape
    scale, shift = c2_ref[0:1], c2_ref[1:2]
    for s in range(samples):
        for r in range(height):
            normed = (a2_ref[s, r + 1] * scale + shift) * m_ref[s, r]
            o_ref[s, r] = (x_ref[s, r].astype(F32) + normed).astype(BF16)
    done_ref[...] = jnp.zeros(done_ref.shape, F32)


def small_rows(rows, c):
    high = jnp.concatenate(rows + [jnp.zeros((8 - len(rows), c), F32)], 0)
    first = high.astype(BF16)
    return jnp.concatenate([first, (high - first.astype(F32)).astype(BF16)], 0)


def weight1_kernel(
    group, leads, pieces,
    c1_ref, c2_ref, dn_ref, a_ref, ao_ref, s_ref, so_ref, x_ref, gx_ref, gp_ref, g_ref, w2_ref, b2_ref, *refs,
):
    stats = gather(refs[:pieces])
    d_ref, dx_ref, dp_ref, send_ref, keep_ref, acc_ref = refs[pieces:]
    samples, height, across, c = x_ref.shape
    even = lax.axis_index("lat") % 2 == 0
    lead = lax.axis_index("lead")
    core = lax.axis_index("dp") % 2
    offset, inverse, count, mean = (c1_ref[i : i + 1] for i in range(4))
    shift_sum = stats[:, 0:1].sum(0)
    away = stats[:, 2:3] - mean
    gain_sum = inverse * (stats[:, 1:2] + away * stats[:, 0:1]).sum(0)
    scale = inverse * g_ref[...]
    by_active, constant = back_terms(scale, inverse, offset, gain_sum, shift_sum, count)
    bias = jnp.zeros((8, c), F32)
    for s in range(samples):
        for r in range(height):
            active = own_row(a_ref, ao_ref, s, r, height)
            grad = dn_ref[s, r] * scale + (active * by_active + constant)
            d_ref[s, r] = (grad * own_row(s_ref, so_ref, s, r, height)).astype(BF16)
        grad = d_ref[s]
        dx_ref[s] = pick(even, grad[height - 1], grad[0])
        dp_ref[s] = pick(even, grad[0], grad[height - 1])
        wide = grad.astype(F32)
        bias += fold(wide)
        above = pick(even, gp_ref[s, 0], gx_ref[s, 0])
        below = pick(even, gx_ref[s, 0], gp_ref[s, 0])
        body = x_ref[s].reshape(-1, c)
        rows = [
            jnp.concatenate([above, body[: (height - 1) * across]], 0),
            body,
            jnp.concatenate([body[across:], below], 0),
        ]
        weight_products(rows, grad.reshape(-1, c), turn(wide, across), acc_ref, s == 0)

    share = 1.0 / group
    small = [
        small_rows([bias.sum(0, keepdims=True), gain_sum * share, shift_sum * share], c),
        small_rows([b2_ref[0:1], c2_ref[2:3] * share, c2_ref[3:4] * share], c),
    ]

    def put(target, which):
        size = 9 * c // leads
        for j in range(leads):
            slot = j ^ lead
            if which == 1:
                target[slot, :size] = w2_ref[j * size : (j + 1) * size]
            else:
                at = j * size
                while at < (j + 1) * size:
                    tap, low = at // c, at % c
                    step = min(c - low, (j + 1) * size - at)
                    a, b = tap // 3, tap % 3
                    target[slot, at - j * size : at - j * size + step] = acc_ref[
                        a * c + low : a * c + low + step, b * c : (b + 1) * c
                    ].astype(BF16)
                    at += step
            target[slot, size:] = small[which]

    @pl.when(core == 0)
    def _():
        put(keep_ref, 0)
        put(send_ref, 1)

    @pl.when(core != 0)
    def _():
        put(keep_ref, 1)
        put(send_ref, 0)


def input_grad_kernel(d_ref, ex_ref, ep_ref, u_ref, w_ref, after_ref, o_ref, done_ref, k_ref):
    samples, height, across, c = u_ref.shape
    even = lax.axis_index("lat") % 2 == 0
    fill_toeplitz_transposed(w_ref, k_ref)
    for s in range(samples):

        def row(r):
            if r < 0:
                return pick(even, ep_ref[s], ex_ref[s])
            if r >= height:
                return pick(even, ex_ref[s], ep_ref[s])
            return d_ref[s, r]

        piece = convolve_rows(row, range(0, height, 2), k_ref, across, True)
        for r in range(height):
            o_ref[s, r] = (u_ref[s, r].astype(F32) + piece(r // 2, r % 2)).astype(BF16)
    done_ref[...] = jnp.zeros(done_ref.shape, F32)


def finish_kernel(leads, mine_ref, *refs):
    got_refs, other_ref = refs[: leads - 1], refs[leads - 1]
    first, second = refs[leads + 1 : leads + 5], refs[leads + 5 :]
    core = lax.axis_index("dp") % 2
    lead = lax.axis_index("lead")
    size = mine_ref.shape[0] - SMALL

    def put(outs, chunk, small):
        for k in range(leads):
            at = pl.multiple_of((k ^ lead) * size, 16)
            outs[0][pl.ds(at, size)] = chunk(k).astype(F32)
        total = small[:8].astype(F32) + small[8:].astype(F32)
        for i in range(3):
            outs[i + 1][...] = total[i : i + 1]

    def own(outs):
        put(outs, lambda k: got_refs[k - 1][...] if k else mine_ref[:size], mine_ref[size:])

    def other(outs):
        put(
            outs,
            lambda k: other_ref[k * size : (k + 1) * size],
            other_ref[leads * size :],
        )

    @pl.when(core == 0)
    def _():
        own(first)
        other(second)

    @pl.when(core != 0)
    def _():
        other(first)
        own(second)


def add_kernel(parts, waits, *refs):
    outs = refs[parts + waits :]
    size = outs[0].shape[0] - SMALL
    for k, out in enumerate(outs):
        chunk = [r.at[k] if len(r.shape) == 3 else r for r in refs[:parts]]
        total = functools.reduce(lambda a, b: a + b, [r[...].astype(F32) for r in chunk])
        out[:size] = total[:size].astype(BF16)
        small = total[size : size + 8] + total[size + 8 :]
        high = small.astype(BF16)
        out[size:] = jnp.concatenate([high, (small - high.astype(F32)).astype(BF16)], 0)


def call(kernel, outs, scratch, operands, name, flops=0, waits=(), space=VMEM):
    size = sum(o.size * o.dtype.itemsize for o in operands)
    return pl.pallas_call(
        kernel,
        out_shape=outs,
        in_specs=[space] * len(operands) + [pl.BlockSpec(memory_space=pl.ANY)] * len(waits),
        out_specs=jax.tree.map(lambda _: space, outs),
        scratch_shapes=scratch,
        compiler_params=pltpu.CompilerParams(vmem_limit_bytes=16 * 2**20),
        cost_estimate=pl.CostEstimate(flops=flops, bytes_accessed=size, transcendentals=0),
        name=name,
    )(*operands, *waits)


def swap(value, axis, k):
    return lax.ppermute(value, axis, [(i, i ^ k) for i in range(lax.axis_size(axis))])


def neighbours(value_x, value_p, axis):
    n = lax.axis_size(axis)
    first = [(i, i ^ 1) for i in range(n) if i ^ 1 < n]
    second = [(i, i + 1) for i in range(1, n - 1, 2)]
    second += [(j, i) for i, j in second]
    return lax.ppermute(value_x, axis, first), lax.ppermute(value_p, axis, second)


def spread(stats):
    blocks, k = stats[None], 1
    while k < lax.axis_size("dp"):
        blocks = jnp.concatenate([blocks, swap(blocks, "dp", k)], 0)
        k *= 2
    return [blocks] + [swap(blocks, "lat", k) for k in range(1, lax.axis_size("lat"))]


def add_chunks(parts, name, outs=1, waits=()):
    shape = jax.ShapeDtypeStruct(parts[0].shape[-2:], BF16)
    return call(
        functools.partial(add_kernel, len(parts), len(waits)),
        [shape] * outs,
        [],
        parts,
        name,
        waits=waits,
    )


def sum_everywhere(send, keep, beside_lat, beside_last):
    leads, lats = lax.axis_size("lead"), lax.axis_size("lat")
    chunks = add_chunks([keep, swap(send, "dp", 1)], "add_dp", leads)
    got = [swap(chunks[k], "lead", k) for k in range(1, leads)]
    (mine,) = add_chunks([chunks[0]] + got, "add_lead")
    got = [swap(mine, "lat", k) for k in range(1, lats)]
    first = beside_lat(chunks[0])
    (mine,) = add_chunks([mine] + got, "add_lat", waits=(first[1],))
    k = 2
    while k < lax.axis_size("dp"):
        (mine,) = add_chunks([mine, swap(mine, "dp", k)], "add_far_dp")
        k *= 2
    size, c = mine.shape[0] - SMALL, mine.shape[1]
    got = [swap(mine[:size], "lead", k) for k in range(1, leads)]
    other = swap(jnp.concatenate([mine[:size]] + got + [mine[size:]], 0), "dp", 1)
    last = beside_last(mine)
    one = [jax.ShapeDtypeStruct((leads * size, c), F32)] + [jax.ShapeDtypeStruct((1, c), F32)] * 3
    sums = call(
        functools.partial(finish_kernel, leads),
        one + one,
        [],
        (mine, *got, other),
        "finish",
        waits=(last[1],),
    )
    return sums[:4], sums[4:], first[0], last[0]


def shards(
    field,
    cotangent,
    land_sea,
    conv1_weight,
    conv1_bias,
    first_norm_scale,
    norm1_shift,
    conv2_weight,
    conv2_bias,
    second_norm_scale,
    norm2_shift,
):
    x, u, mask = field[0], cotangent[0], land_sea[0]
    samples, height, across, c = x.shape
    group = lax.axis_size("dp") * lax.axis_size("lat")
    leads = lax.axis_size("lead")
    slabs = -(-samples * height // 128)
    vec = lambda v: v.reshape(1, c)
    b1, g1, t1 = vec(conv1_bias), vec(first_norm_scale), vec(norm1_shift)
    b2, g2, t2 = vec(conv2_bias), vec(second_norm_scale), vec(norm2_shift)

    array = jax.ShapeDtypeStruct
    shape = lambda rows, dtype=F32: array((samples, rows, across, c), dtype)
    edge = array((samples, across, c), BF16)
    vector = array((8, c), F32)
    weights = array((3, 4 * c, 2 * c), BF16)
    turned = array((3, 2 * c, 4 * c), BF16)
    ext = lambda rows: pltpu.VMEM((2, rows, across, c), BF16)
    acc = pltpu.VMEM((3 * c, 3 * c), F32)
    conv_flops = 2 * 9 * c * c * samples * height * across

    near = call(
        near_rows_kernel,
        (shape(1, BF16), shape(1, BF16)),
        [pltpu.SemaphoreType.DMA((2,))],
        (x,),
        "near_rows",
        space=pl.BlockSpec(memory_space=pl.ANY),
    )
    gx, gp = neighbours(*near, "lat")
    a1, s1, wide_mask, bits, w1t, part = call(
        conv1_inner_kernel,
        (
            shape(height - 4),
            shape(height - 4),
            shape(height),
            array((slabs, across, 128), F32),
            weights,
            vector,
        ),
        [],
        (x, mask.reshape(samples * height, across), conv1_weight, b1),
        "conv1_inner",
        conv_flops,
    )
    packed = array((3 * samples + slabs, across, c), BF16)
    hx, hp = neighbours(
        *call(far_rows_kernel, (packed, packed), [], (x, u, bits), "far_rows", waits=(gx, gp)), "lat"
    )
    a1o, s1o, own1 = call(
        conv1_outer_kernel,
        (shape(4), shape(4), vector),
        [],
        (x, gx, gp, wide_mask, w1t, b1, part),
        "conv1_outer",
        conv_flops // 2,
    )
    a1h, halo_mask, mu, mu_sum, w2t, w2tt = call(
        conv1_edge_kernel,
        (shape(4), shape(4), shape(height + 2), vector, weights, turned),
        [],
        (x, gx, gp, hx, hp, u, wide_mask, own1, w1t, b1, conv2_weight),
        "conv1_edges",
        conv_flops // 2,
    )
    st1 = spread(own1)
    n1, a2, s2, c1, own2 = call(
        functools.partial(conv2_kernel, len(st1)),
        (shape(height + 2, BF16), shape(height + 2), shape(height + 2), vector, vector),
        [ext(height + 4)],
        (own1, a1, a1o, a1h, wide_mask, halo_mask, mu, mu_sum, w2t, b2, g1, t1, *st1),
        "conv2",
        conv_flops,
    )
    st2 = spread(own2)
    d2, dn1, c2, own3 = call(
        functools.partial(back2_kernel, len(st2)),
        (shape(height, BF16), shape(height), vector, vector),
        [ext(height + 2)],
        (own2, own1, c1, a2, s2, mu, wide_mask, a1, a1o, w2tt, g2, t2, *st2),
        "conv2_back",
        conv_flops,
    )
    st3 = spread(own3)
    w2, bias2 = call(
        weight2_kernel,
        (array((9 * c, c), BF16), vector),
        [acc],
        (n1, d2),
        "conv2_weight_grad",
        conv_flops,
        waits=(st3[0],),
    )
    chunks = array((leads, 9 * c // leads + SMALL, c), BF16)
    d1, dx, dp, send, keep = call(
        functools.partial(weight1_kernel, group, leads, len(st3)),
        (shape(height, BF16), edge, edge, chunks, chunks),
        [acc],
        (c1, c2, dn1, a1, a1o, s1, s1o, x, gx, gp, g1, w2, bias2, *st3),
        "conv1_weight_grad",
        conv_flops,
    )
    dx, dp = neighbours(dx, dp, "lat")
    first, second, grad_input, output = sum_everywhere(
        send,
        keep,
        lambda after: call(
            input_grad_kernel,
            (shape(height, BF16), vector),
            [pltpu.VMEM(turned.shape, BF16)],
            (d1, dx, dp, u, conv1_weight),
            "conv1_back",
            conv_flops,
            waits=(after,),
        ),
        lambda after: call(
            output_kernel,
            (shape(height, BF16), vector),
            [],
            (x, a2, wide_mask, c2),
            "output",
            conv_flops // 2,
            waits=(after,),
        ),
    )
    sums = []
    for part in (first, second):
        sums += [part[0].reshape(3, 3, c, c)] + [v.reshape(c) for v in part[1:]]
    return (output[None], grad_input[None], *sums)


def solution(mesh):
    tiles = P("lead", "dp", "lat", None, None)
    in_specs = (tiles, tiles, P("lead", "dp", "lat", None)) + (P(),) * 8
    out_specs = (tiles, tiles) + (P(),) * 8
    return jax.shard_map(shards, mesh=mesh, in_specs=in_specs, out_specs=out_specs, check_vma=False)
```

```python
import functools

import jax
import jax.numpy as jnp
from jax import lax
from jax.experimental import pallas as pl
from jax.experimental.pallas import tpu as pltpu
from jax.sharding import PartitionSpec as P

EPSILON = 1e-05
BF16 = jnp.bfloat16
F32 = jnp.float32
VMEM = pl.BlockSpec(memory_space=pltpu.VMEM)
HIDE = 10**11
SMALL = 16


def fill_toeplitz(taps_ref, out_ref):
    c = taps_ref.shape[-1]
    zero = jnp.zeros((c, c), BF16)
    for b in range(3):
        for i in range(4):
            for j in range(2):
                block = taps_ref[i - j, b] if 0 <= i - j < 3 else zero
                out_ref[b, i * c : (i + 1) * c, j * c : (j + 1) * c] = block


def fill_toeplitz_transposed(taps_ref, out_ref):
    c = taps_ref.shape[-1]
    zero = jnp.zeros((c, c), BF16)
    for b in range(3):
        for i in range(4):
            for j in range(2):
                block = taps_ref[2 - (i - j), 2 - b] if 0 <= i - j < 3 else zero
                out_ref[b, j * c : (j + 1) * c, i * c : (i + 1) * c] = block


def convolve_rows(row, starts, weights_ref, across, transposed):
    left = jnp.concatenate(
        [jnp.concatenate([row(r - 1 + i) for r in starts], 0) for i in range(4)], 1
    )
    c = left.shape[1] // 4
    dims = (((1,), (1 if transposed else 0,)), ((), ()))
    taps = [
        lax.dot_general(left, weights_ref[b], dims, preferred_element_type=F32)
        for b in range(3)
    ]

    def piece(pair, j):
        part = [t[pair * across : (pair + 1) * across, j * c : (j + 1) * c] for t in taps]
        return pltpu.roll(part[0], 1, 0) + part[1] + pltpu.roll(part[2], across - 1, 0)

    return piece


def silu_and_slope(hidden):
    gate = 0.5 + 0.5 * jnp.tanh(0.5 * hidden)
    active = hidden * gate
    return active, gate + active * (1.0 - gate)


def silu(value):
    return value * (0.5 + 0.5 * jnp.tanh(0.5 * value))


def fold(value):
    return value.reshape(-1, 8, value.shape[-1]).sum(0)


def join(stats, count, at, sums):
    centres = stats[:, at + 2 : at + 3]
    mean = (stats[:, at : at + 1] + sums * centres).sum(0) / count
    away = centres - mean
    squares = stats[:, at + 1 : at + 2] + away * (2.0 * stats[:, at : at + 1] + sums * away)
    variance = jnp.maximum(squares.sum(0) / count, 0.0)
    return mean, lax.rsqrt(variance + EPSILON)


def pick(even, when_even, when_odd):
    return jnp.where(even, when_even, when_odd)


def column_mask(bits, k, c):
    tile = bits[k // 128]
    return jnp.broadcast_to(tile[:, k % 128 : k % 128 + 1].astype(F32), (tile.shape[0], c))


def near_rows_kernel(x_ref, gx_ref, gp_ref, sems):
    height = x_ref.shape[1]
    even = lax.axis_index("lat") % 2 == 0
    last = jnp.where(even, height - 1, 0)
    copies = [
        pltpu.make_async_copy(x_ref.at[:, pl.ds(at, 1)], out, sems.at[i])
        for i, (at, out) in enumerate(((last, gx_ref), (height - 1 - last, gp_ref)))
    ]
    for copy in copies:
        copy.start()
    for copy in copies:
        copy.wait()


def far_rows_kernel(x_ref, u_ref, mask_ref, hx_ref, hp_ref, m_ref, count_ref, bits_ref):
    samples, height, across, c = x_ref.shape
    even = lax.axis_index("lat") % 2 == 0
    for k in range(bits_ref.shape[0]):
        bits = mask_ref[k * 128 : (k + 1) * 128].astype(F32)
        bits = jnp.concatenate([bits, jnp.zeros((bits.shape[0], 128 - across), F32)], 1)
        if bits.shape[0] < 128:
            bits = jnp.concatenate([bits, jnp.zeros((128 - bits.shape[0], 128), F32)], 0)
        bits_ref[k] = bits.T[:across]
    for out, down in ((hx_ref, even), (hp_ref, jnp.logical_not(even))):
        first = jnp.where(down, height - 3, 1)
        edge = jnp.where(down, height - 1, 0)
        for s in range(samples):
            out[2 * s] = x_ref[s, first]
            out[2 * s + 1] = x_ref[s, first + 1]
            out[2 * samples + s] = u_ref[s, edge]
        for k in range(bits_ref.shape[0]):
            out[3 * samples + k] = bits_ref[k].astype(BF16)
    count = jnp.zeros((8, c), F32)
    for s in range(samples):
        for r in range(height):
            mask = column_mask(bits_ref, s * height + r, c)
            m_ref[s, r] = mask
            count += fold(mask)
    count_ref[...] = stats_block([count.sum(0, keepdims=True)], c)


def stats_block(rows, c):
    return jnp.concatenate(rows + [jnp.zeros((8 - len(rows), c), F32)], 0)


def gather(refs):
    return jnp.concatenate([r[...] for r in refs], 0)


def middle(value):
    return value.mean(0, keepdims=True)


def add_moments(sums, active, mask):
    masked = active * mask
    sums[0] += fold(masked)
    sums[1] += fold(masked * active)
    return masked


def conv1_kernel(gp_ref, gx_ref, x_ref, m_ref, count_ref, w_ref, b_ref, a_ref, s_ref, t_ref, st_ref):
    samples, height, across, c = x_ref.shape
    even = lax.axis_index("lat") % 2 == 0
    fill_toeplitz(w_ref, t_ref)
    bias = b_ref[...]
    sums = [jnp.zeros((8, c), F32) for _ in range(2)]
    centre = None
    for s in range(samples):

        def row(r):
            if r < 0:
                return pick(even, gp_ref[s, 0], gx_ref[s, 0])
            if r >= height:
                return pick(even, gx_ref[s, 0], gp_ref[s, 0])
            return x_ref[s, r]

        piece = convolve_rows(row, range(0, height, 2), t_ref, across, False)
        for r in range(height):
            active, slope = silu_and_slope(piece(r // 2, r % 2) + bias)
            if centre is None:
                centre = middle(active)
            active = active - centre
            mask = m_ref[s, r]
            a_ref[s, r] = active
            s_ref[s, r] = slope * mask
            add_moments(sums, active, mask)
    rows = [v.sum(0, keepdims=True) for v in sums]
    st_ref[...] = stats_block([rows[0], rows[1], centre, count_ref[0:1]], c)


def conv1_edge_kernel(
    hp_ref, hx_ref, gp_ref, gx_ref, x_ref, u_ref, m_ref, st_ref, t_ref, b_ref, w2_ref,
    a_ref, mh_ref, mu_ref, su_ref, t2_ref, tt2_ref,
):
    samples, height, across, c = x_ref.shape
    even = lax.axis_index("lat") % 2 == 0
    fill_toeplitz(w2_ref, t2_ref)
    fill_toeplitz_transposed(w2_ref, tt2_ref)
    bias = b_ref[...]
    centre = st_ref[2:3]

    def row(r):
        parts = []
        for s in range(samples):
            if r < -1:
                parts.append(pick(even, hp_ref[2 * s + r + 3], hx_ref[2 * s + r + 3]))
            elif r == -1:
                parts.append(pick(even, gp_ref[s, 0], gx_ref[s, 0]))
            elif r < height:
                parts.append(x_ref[s, r])
            elif r == height:
                parts.append(pick(even, gx_ref[s, 0], gp_ref[s, 0]))
            else:
                j = r - height - 1
                parts.append(pick(even, hx_ref[2 * s + j], hp_ref[2 * s + j]))
        return jnp.concatenate(parts, 0)

    slabs = slice(3 * samples, hx_ref.shape[0])
    above = pick(even, hp_ref[slabs], hx_ref[slabs])
    below = pick(even, hx_ref[slabs], hp_ref[slabs])
    total = jnp.zeros((8, c), F32)
    for slot, start in ((0, -2), (2, height)):
        piece = convolve_rows(row, (start,), t_ref, across, False)
        for s in range(samples):
            for j in range(2):
                a_ref[s, slot + j] = silu(piece(s, j) + bias) - centre
                if start < 0:
                    mask = column_mask(above, s * height + height - 2 + j, c)
                else:
                    mask = column_mask(below, s * height + j, c)
                mh_ref[s, slot + j] = mask
    for s in range(samples):
        up = pick(even, hp_ref[2 * samples + s], hx_ref[2 * samples + s])
        mu_ref[s, 0] = up.astype(F32) * mh_ref[s, 1]
        for r in range(height):
            value = u_ref[s, r].astype(F32) * m_ref[s, r]
            mu_ref[s, r + 1] = value
            total += fold(value)
        down = pick(even, hx_ref[2 * samples + s], hp_ref[2 * samples + s])
        mu_ref[s, height + 1] = down.astype(F32) * mh_ref[s, 2]
    su_ref[...] = stats_block([total.sum(0, keepdims=True)], c)


def conv2_kernel(
    pieces,
    own_ref, a_ref, ah_ref, m_ref, mh_ref, mu_ref, su_ref, k_ref, b_ref, g_ref, t_ref, *refs,
):
    stats, (n_ref, a2_ref, s2_ref, c1_ref, st2_ref, ext_ref) = gather(refs[:pieces]), refs[pieces:]
    samples, height, across, c = m_ref.shape
    counts = stats[:, 3:4]
    count = counts.sum(0)
    mean, inverse = join(stats, count, 0, counts)
    offset = mean - own_ref[2:3]
    scale = inverse * g_ref[...]
    shift = t_ref[...] - offset * scale
    c1_ref[...] = stats_block([offset, inverse, count, mean], c)
    bias = b_ref[...]
    sums = [jnp.zeros((8, c), F32) for _ in range(3)]
    centre = None
    for s in range(samples):
        ext = ext_ref.at[s % 2]
        for i in range(height + 4):
            r = i - 2
            if 0 <= r < height:
                value, mask = a_ref[s, r], m_ref[s, r]
            else:
                j = i if r < 0 else r - height + 2
                value, mask = ah_ref[s, j], mh_ref[s, j]
            ext[i] = ((value * scale + shift) * mask).astype(BF16)
            if 1 <= i < height + 3:
                n_ref[s, i - 1] = ext[i]

        piece = convolve_rows(
            lambda r: ext[r + 2], range(-1, height + 1, 2), k_ref, across, False
        )
        for i in range(height + 2):
            r = i - 1
            active, slope = silu_and_slope(piece(i // 2, i % 2) + bias)
            if centre is None:
                centre = middle(active)
            active = active - centre
            if 0 <= r < height:
                mask = m_ref[s, r]
                add_moments(sums, active, mask)
                sums[2] += fold(active * mu_ref[s, i])
            else:
                mask = mh_ref[s, 1 if r < 0 else 2]
            a2_ref[s, i] = active
            s2_ref[s, i] = slope * mask
    rows = [v.sum(0, keepdims=True) for v in sums]
    st2_ref[...] = stats_block(
        [rows[0], rows[1], centre, rows[2], su_ref[0:1], own_ref[3:4]], c
    )


def back_terms(scale, inverse, offset, gain_sum, shift_sum, count):
    by_active = -scale * gain_sum * inverse / count
    constant = -scale * (shift_sum - offset * inverse * gain_sum) / count
    return by_active, constant


def back2_kernel(
    pieces,
    own_ref, st1_ref, c1_ref, a2_ref, s2_ref, mu_ref, m_ref, a_ref, k_ref, g_ref, t_ref, *refs,
):
    stats, (d_ref, dn_ref, c2_ref, st3_ref, ext_ref) = gather(refs[:pieces]), refs[pieces:]
    samples, height, across, c = m_ref.shape
    count = c1_ref[2:3]
    mean, inverse = join(stats, count, 0, stats[:, 5:6])
    offset = mean - own_ref[2:3]
    shift_sum = stats[:, 4:5].sum(0)
    away = stats[:, 2:3] - mean
    gain_sum = inverse * (stats[:, 3:4] + away * stats[:, 4:5]).sum(0)
    scale = inverse * g_ref[...]
    by_active, constant = back_terms(scale, inverse, offset, gain_sum, shift_sum, count)
    c2_ref[...] = stats_block([scale, t_ref[...] - offset * scale, gain_sum, shift_sum], c)
    sums = [jnp.zeros((8, c), F32) for _ in range(2)]
    for s in range(samples):
        ext = ext_ref.at[s % 2]
        for i in range(height + 2):
            grad = mu_ref[s, i] * scale + (a2_ref[s, i] * by_active + constant)
            ext[i] = (grad * s2_ref[s, i]).astype(BF16)
            if 0 < i <= height:
                d_ref[s, i - 1] = ext[i]
        piece = convolve_rows(
            lambda r: ext[r + 1], range(0, height, 2), k_ref, across, True
        )
        for r in range(height):
            part = piece(r // 2, r % 2)
            dn_ref[s, r] = part
            masked = part * m_ref[s, r]
            sums[0] += fold(masked)
            sums[1] += fold(masked * a_ref[s, r])
    rows = [v.sum(0, keepdims=True) for v in sums]
    st3_ref[...] = stats_block([rows[0], rows[1], st1_ref[2:3]], c)


def weight_products(rows, centre, turned, total_ref, first):
    windows = jnp.concatenate(rows, 1)
    product = lax.dot_general(
        windows,
        jnp.concatenate([turned[0], centre, turned[1]], 1),
        (((0,), (0,)), ((), ())),
        preferred_element_type=F32,
    )
    if first:
        total_ref[...] = product
    else:
        total_ref[...] += product


def turn(value, across):
    c = value.shape[-1]
    return [
        pltpu.roll(value, k, 1).astype(BF16).reshape(-1, c) for k in (across - 1, 1)
    ]


def weight2_kernel(n_ref, d_ref, after_ref, w_ref, b_ref, acc_ref):
    samples, height, across, c = d_ref.shape
    bias = jnp.zeros((8, c), F32)
    for s in range(samples):
        grad = d_ref[s]
        wide = grad.astype(F32)
        bias += fold(wide)
        rows = [n_ref[s, a : a + height].reshape(-1, c) for a in range(3)]
        weight_products(rows, grad.reshape(-1, c), turn(wide, across), acc_ref, s == 0)
    b_ref[...] = jnp.broadcast_to(bias.sum(0, keepdims=True), b_ref.shape)
    for a in range(3):
        for b in range(3):
            at = (a * 3 + b) * c
            w_ref[at : at + c] = acc_ref[a * c : (a + 1) * c, b * c : (b + 1) * c].astype(BF16)


def output_kernel(x_ref, a2_ref, m_ref, c2_ref, after_ref, o_ref, done_ref):
    samples, height, across, c = x_ref.shape
    scale, shift = c2_ref[0:1], c2_ref[1:2]
    for s in range(samples):
        for r in range(height):
            normed = (a2_ref[s, r + 1] * scale + shift) * m_ref[s, r]
            o_ref[s, r] = (x_ref[s, r].astype(F32) + normed).astype(BF16)
    done_ref[...] = jnp.zeros(done_ref.shape, F32)


def small_rows(rows, c):
    high = jnp.concatenate(rows + [jnp.zeros((8 - len(rows), c), F32)], 0)
    first = high.astype(BF16)
    return jnp.concatenate([first, (high - first.astype(F32)).astype(BF16)], 0)


def weight1_kernel(
    group, leads, pieces,
    c1_ref, c2_ref, dn_ref, a_ref, s_ref, x_ref, gx_ref, gp_ref, g_ref, w2_ref, b2_ref, *refs,
):
    stats = gather(refs[:pieces])
    d_ref, send_ref, keep_ref, acc_ref = refs[pieces:]
    samples, height, across, c = x_ref.shape
    even = lax.axis_index("lat") % 2 == 0
    lead = lax.axis_index("lead")
    core = lax.axis_index("dp") % 2
    offset, inverse, count, mean = (c1_ref[i : i + 1] for i in range(4))
    shift_sum = stats[:, 0:1].sum(0)
    away = stats[:, 2:3] - mean
    gain_sum = inverse * (stats[:, 1:2] + away * stats[:, 0:1]).sum(0)
    scale = inverse * g_ref[...]
    by_active, constant = back_terms(scale, inverse, offset, gain_sum, shift_sum, count)
    bias = jnp.zeros((8, c), F32)
    for s in range(samples):
        for r in range(height):
            active = a_ref[s, r]
            grad = dn_ref[s, r] * scale + (active * by_active + constant)
            d_ref[s, r] = (grad * s_ref[s, r]).astype(BF16)
        grad = d_ref[s]
        wide = grad.astype(F32)
        bias += fold(wide)
        above = pick(even, gp_ref[s, 0], gx_ref[s, 0])
        below = pick(even, gx_ref[s, 0], gp_ref[s, 0])
        body = x_ref[s].reshape(-1, c)
        rows = [
            jnp.concatenate([above, body[: (height - 1) * across]], 0),
            body,
            jnp.concatenate([body[across:], below], 0),
        ]
        weight_products(rows, grad.reshape(-1, c), turn(wide, across), acc_ref, s == 0)

    share = 1.0 / group
    small = [
        small_rows([bias.sum(0, keepdims=True), gain_sum * share, shift_sum * share], c),
        small_rows([b2_ref[0:1], c2_ref[2:3] * share, c2_ref[3:4] * share], c),
    ]

    def put(target, which):
        size = 9 * c // leads
        for j in range(leads):
            slot = j ^ lead
            if which == 1:
                target[slot, :size] = w2_ref[j * size : (j + 1) * size]
            else:
                at = j * size
                while at < (j + 1) * size:
                    tap, low = at // c, at % c
                    step = min(c - low, (j + 1) * size - at)
                    a, b = tap // 3, tap % 3
                    target[slot, at - j * size : at - j * size + step] = acc_ref[
                        a * c + low : a * c + low + step, b * c : (b + 1) * c
                    ].astype(BF16)
                    at += step
            target[slot, size:] = small[which]

    @pl.when(core == 0)
    def _():
        put(keep_ref, 0)
        put(send_ref, 1)

    @pl.when(core != 0)
    def _():
        put(keep_ref, 1)
        put(send_ref, 0)


def edge_rows_kernel(d_ref, after_ref, dx_ref, dp_ref):
    samples, height = d_ref.shape[:2]
    even = lax.axis_index("lat") % 2 == 0
    for s in range(samples):
        dx_ref[s] = pick(even, d_ref[s, height - 1], d_ref[s, 0])
        dp_ref[s] = pick(even, d_ref[s, 0], d_ref[s, height - 1])


def input_grad_kernel(ep_ref, ex_ref, d_ref, u_ref, w_ref, o_ref, done_ref, k_ref):
    samples, height, across, c = u_ref.shape
    even = lax.axis_index("lat") % 2 == 0
    fill_toeplitz_transposed(w_ref, k_ref)
    for s in range(samples):

        def row(r):
            if r < 0:
                return pick(even, ep_ref[s], ex_ref[s])
            if r >= height:
                return pick(even, ex_ref[s], ep_ref[s])
            return d_ref[s, r]

        piece = convolve_rows(row, range(0, height, 2), k_ref, across, True)
        for r in range(height):
            o_ref[s, r] = (u_ref[s, r].astype(F32) + piece(r // 2, r % 2)).astype(BF16)
    done_ref[...] = jnp.zeros(done_ref.shape, F32)


def join_kernel(leads, *refs):
    out_ref = refs[-1]
    size = refs[0].shape[0] - SMALL
    for k in range(leads):
        out_ref[k * size : (k + 1) * size] = refs[k][:size]
    out_ref[leads * size :] = refs[0][size:]


def finish_kernel(leads, own_ref, other_ref, *refs):
    first, second = refs[:4], refs[4:]
    core = lax.axis_index("dp") % 2
    lead = lax.axis_index("lead")
    size = (own_ref.shape[0] - SMALL) // leads

    def put(outs, ref):
        for k in range(leads):
            at = pl.multiple_of((k ^ lead) * size, 16)
            outs[0][pl.ds(at, size)] = ref[k * size : (k + 1) * size].astype(F32)
        small = ref[leads * size :].astype(F32)
        total = small[:8] + small[8:]
        for i in range(3):
            outs[i + 1][...] = total[i : i + 1]

    @pl.when(core == 0)
    def _():
        put(first, own_ref)
        put(second, other_ref)

    @pl.when(core != 0)
    def _():
        put(first, other_ref)
        put(second, own_ref)


def add_kernel(parts, waits, *refs):
    outs = refs[parts + waits :]
    size = outs[0].shape[0] - SMALL
    for k, out in enumerate(outs):
        chunk = [r.at[k] if len(r.shape) == 3 else r for r in refs[:parts]]
        total = functools.reduce(lambda a, b: a + b, [r[...].astype(F32) for r in chunk])
        out[:size] = total[:size].astype(BF16)
        small = total[size : size + 8] + total[size + 8 :]
        high = small.astype(BF16)
        out[size:] = jnp.concatenate([high, (small - high.astype(F32)).astype(BF16)], 0)


def call(kernel, outs, scratch, operands, name, flops=0, waits=(), spaces=(VMEM, VMEM)):
    size = sum(o.size * o.dtype.itemsize for o in operands)
    return pl.pallas_call(
        kernel,
        out_shape=outs,
        in_specs=[spaces[0]] * len(operands) + [pl.BlockSpec(memory_space=pl.ANY)] * len(waits),
        out_specs=jax.tree.map(lambda _: spaces[1], outs),
        scratch_shapes=scratch,
        compiler_params=pltpu.CompilerParams(vmem_limit_bytes=16 * 2**20),
        cost_estimate=pl.CostEstimate(flops=flops, bytes_accessed=size, transcendentals=0),
        name=name,
    )(*operands, *waits)


def swap(value, axis, k):
    return lax.ppermute(value, axis, [(i, i ^ k) for i in range(lax.axis_size(axis))])


def neighbours(value_x, value_p, axis):
    n = lax.axis_size(axis)
    first = [(i, i ^ 1) for i in range(n) if i ^ 1 < n]
    second = [(i, i + 1) for i in range(1, n - 1, 2)]
    second += [(j, i) for i, j in second]
    got_p = lax.ppermute(value_p, axis, second)
    return lax.ppermute(value_x, axis, first), got_p


def spread(stats):
    blocks, k = stats[None], 1
    while k < lax.axis_size("dp"):
        blocks = jnp.concatenate([blocks, swap(blocks, "dp", k)], 0)
        k *= 2
    return [blocks] + [swap(blocks, "lat", k) for k in range(1, lax.axis_size("lat"))]


def add_chunks(parts, name, outs=1, waits=(), flops=0):
    shape = jax.ShapeDtypeStruct(parts[0].shape[-2:], BF16)
    return call(
        functools.partial(add_kernel, len(parts), len(waits)),
        [shape] * outs,
        [],
        parts,
        name,
        flops,
        waits,
    )


def sum_everywhere(send, keep, block_output, input_grad):
    leads, lats = lax.axis_size("lead"), lax.axis_size("lat")
    chunks = add_chunks([keep, swap(send, "dp", 1)], "add_dp", leads)
    got = [swap(chunks[k], "lead", k) for k in reversed(range(1, leads))]
    (mine,) = add_chunks([chunks[0]] + got, "add_lead", flops=HIDE)
    got = [swap(mine, "lat", k) for k in range(1, lats)]
    grad_input = input_grad(chunks[0])
    (mine,) = add_chunks([mine] + got, "add_lat", waits=(grad_input[1],))
    k = 2
    while k < lax.axis_size("dp"):
        (mine,) = add_chunks([mine, swap(mine, "dp", k)], "add_far_dp")
        k *= 2
    size, c = mine.shape[0] - SMALL, mine.shape[1]
    got = [swap(mine, "lead", k) for k in range(1, leads)]
    output = block_output(mine)
    own = call(
        functools.partial(join_kernel, leads),
        jax.ShapeDtypeStruct((leads * size + SMALL, c), BF16),
        [],
        (mine, *got),
        "join",
        waits=(output[1],),
    )
    one = [jax.ShapeDtypeStruct((leads * size, c), F32)] + [jax.ShapeDtypeStruct((1, c), F32)] * 3
    sums = call(
        functools.partial(finish_kernel, leads), one + one, [], (own, swap(own, "dp", 1)), "finish"
    )
    return sums[:4], sums[4:], output[0], grad_input[0]


def shards(
    field,
    cotangent,
    land_sea,
    conv1_weight,
    conv1_bias,
    first_norm_scale,
    norm1_shift,
    conv2_weight,
    conv2_bias,
    second_norm_scale,
    norm2_shift,
):
    x, u, mask = field[0], cotangent[0], land_sea[0]
    samples, height, across, c = x.shape
    group = lax.axis_size("dp") * lax.axis_size("lat")
    leads = lax.axis_size("lead")
    slabs = -(-samples * height // 128)
    vec = lambda v: v.reshape(1, c)
    b1, g1, t1 = vec(conv1_bias), vec(first_norm_scale), vec(norm1_shift)
    b2, g2, t2 = vec(conv2_bias), vec(second_norm_scale), vec(norm2_shift)

    array = jax.ShapeDtypeStruct
    shape = lambda rows, dtype=F32: array((samples, rows, across, c), dtype)
    edge = array((samples, across, c), BF16)
    vector = array((8, c), F32)
    weights = array((3, 4 * c, 2 * c), BF16)
    turned = array((3, 2 * c, 4 * c), BF16)
    ext = lambda rows: pltpu.VMEM((2, rows, across, c), BF16)
    acc = pltpu.VMEM((3 * c, 3 * c), F32)
    conv_flops = 2 * 9 * c * c * samples * height * across

    near = call(
        near_rows_kernel,
        (shape(1, BF16), shape(1, BF16)),
        [pltpu.SemaphoreType.DMA((2,))],
        (x,),
        "near_rows",
        conv_flops,
        spaces=(pl.BlockSpec(memory_space=pl.ANY),) * 2,
    )
    gx, gp = neighbours(*near, "lat")
    packed = array((3 * samples + slabs, across, c), BF16)
    far_x, far_p, wide_mask, count = call(
        far_rows_kernel,
        (packed, packed, shape(height), vector),
        [pltpu.VMEM((slabs, across, 128), F32)],
        (x, u, mask.reshape(samples * height, across)),
        "far_rows",
        conv_flops,
    )
    hx, hp = neighbours(far_x, far_p, "lat")
    a1, s1, w1t, own1 = call(
        conv1_kernel,
        (shape(height), shape(height), weights, vector),
        [],
        (gp, gx, x, wide_mask, count, conv1_weight, b1),
        "conv1",
        16 * conv_flops,
    )
    a1h, halo_mask, mu, mu_sum, w2t, w2tt = call(
        conv1_edge_kernel,
        (shape(4), shape(4), shape(height + 2), vector, weights, turned),
        [],
        (hp, hx, gp, gx, x, u, wide_mask, own1, w1t, b1, conv2_weight),
        "conv1_edges",
        conv_flops // 2,
    )
    st1 = spread(own1)
    n1, a2, s2, c1, own2 = call(
        functools.partial(conv2_kernel, len(st1)),
        (shape(height + 2, BF16), shape(height + 2), shape(height + 2), vector, vector),
        [ext(height + 4)],
        (own1, a1, a1h, wide_mask, halo_mask, mu, mu_sum, w2t, b2, g1, t1, *st1),
        "conv2",
        conv_flops,
    )
    st2 = spread(own2)
    d2, dn1, c2, own3 = call(
        functools.partial(back2_kernel, len(st2)),
        (shape(height, BF16), shape(height), vector, vector),
        [ext(height + 2)],
        (own2, own1, c1, a2, s2, mu, wide_mask, a1, w2tt, g2, t2, *st2),
        "conv2_back",
        conv_flops,
    )
    st3 = spread(own3)
    w2, bias2 = call(
        weight2_kernel,
        (array((9 * c, c), BF16), vector),
        [acc],
        (n1, d2),
        "conv2_weight_grad",
        conv_flops,
        waits=(st3[0],),
    )
    chunks = array((leads, 9 * c // leads + SMALL, c), BF16)
    d1, send, keep = call(
        functools.partial(weight1_kernel, group, leads, len(st3)),
        (shape(height, BF16), chunks, chunks),
        [acc],
        (c1, c2, dn1, a1, s1, x, gx, gp, g1, w2, bias2, *st3),
        "conv1_weight_grad",
        conv_flops,
    )

    def input_grad(after):
        rows = call(edge_rows_kernel, (edge, edge), [], (d1,), "edge_rows", waits=(after,))
        rows = neighbours(*rows, "lat")
        return call(
            input_grad_kernel,
            (shape(height, BF16), vector),
            [pltpu.VMEM(turned.shape, BF16)],
            (rows[1], rows[0], d1, u, conv1_weight),
            "conv1_back",
            conv_flops,
        )

    def block_output(after):
        return call(
            output_kernel,
            (shape(height, BF16), vector),
            [],
            (x, a2, wide_mask, c2),
            "output",
            conv_flops // 2,
            waits=(after,),
        )

    first, second, output, grad_input = sum_everywhere(send, keep, block_output, input_grad)
    sums = []
    for part in (first, second):
        sums += [part[0].reshape(3, 3, c, c)] + [v.reshape(c) for v in part[1:]]
    return (output[None], grad_input[None], *sums)


def solution(mesh):
    tiles = P("lead", "dp", "lat", None, None)
    in_specs = (tiles, tiles, P("lead", "dp", "lat", None)) + (P(),) * 8
    out_specs = (tiles, tiles) + (P(),) * 8
    return jax.shard_map(shards, mesh=mesh, in_specs=in_specs, out_specs=out_specs, check_vma=False)
```

```python
import functools

import jax
import jax.numpy as jnp
from jax import lax
from jax.experimental import pallas as pl
from jax.experimental.pallas import tpu as pltpu
from jax.sharding import PartitionSpec as P

EPSILON = 1e-05
BF16 = jnp.bfloat16
F32 = jnp.float32
VMEM = pl.BlockSpec(memory_space=pltpu.VMEM)
HIDE = 10**11
SMALL = 16


def fill_toeplitz(taps_ref, out_ref):
    c = taps_ref.shape[-1]
    zero = jnp.zeros((c, c), BF16)
    half = jnp.asarray(0.5, BF16)
    for b in range(3):
        for i in range(4):
            for j in range(2):
                block = taps_ref[i - j, b] * half if 0 <= i - j < 3 else zero
                out_ref[b, i * c : (i + 1) * c, j * c : (j + 1) * c] = block


def fill_toeplitz_transposed(taps_ref, out_ref):
    c = taps_ref.shape[-1]
    zero = jnp.zeros((c, c), BF16)
    for b in range(3):
        for i in range(4):
            for j in range(2):
                block = taps_ref[2 - (i - j), 2 - b] if 0 <= i - j < 3 else zero
                out_ref[b, j * c : (j + 1) * c, i * c : (i + 1) * c] = block


def convolve_rows(row, starts, weights_ref, across, transposed):
    left = jnp.concatenate(
        [jnp.concatenate([row(r - 1 + i) for r in starts], 0) for i in range(4)], 1
    )
    c = left.shape[1] // 4
    dims = (((1,), (1 if transposed else 0,)), ((), ()))
    taps = [
        lax.dot_general(left, weights_ref[b], dims, preferred_element_type=F32)
        for b in range(3)
    ]

    def piece(pair, j):
        part = [t[pair * across : (pair + 1) * across, j * c : (j + 1) * c] for t in taps]
        return pltpu.roll(part[0], 1, 0) + part[1] + pltpu.roll(part[2], across - 1, 0)

    return piece


def silu(half):
    return half + half * jnp.tanh(half)


def silu_slope(half):
    t = jnp.tanh(half)
    return (0.5 + 0.5 * t) * (1.0 + half * (1.0 - t))


def fold(value):
    return value.reshape(-1, 8, value.shape[-1]).sum(0)


def join(stats, count, at, sums):
    centres = stats[:, at + 2 : at + 3]
    mean = (stats[:, at : at + 1] + sums * centres).sum(0) / count
    away = centres - mean
    squares = stats[:, at + 1 : at + 2] + away * (2.0 * stats[:, at : at + 1] + sums * away)
    variance = jnp.maximum(squares.sum(0) / count, 0.0)
    return mean, lax.rsqrt(variance + EPSILON)


def pick(even, when_even, when_odd):
    return jnp.where(even, when_even, when_odd)


def column_mask(bits, k, c):
    tile = bits[k // 128]
    return jnp.broadcast_to(tile[:, k % 128 : k % 128 + 1].astype(F32), (tile.shape[0], c))


def near_rows_kernel(x_ref, gx_ref, gp_ref, sems):
    height = x_ref.shape[1]
    even = lax.axis_index("lat") % 2 == 0
    last = jnp.where(even, height - 1, 0)
    copies = [
        pltpu.make_async_copy(x_ref.at[:, pl.ds(at, 1)], out, sems.at[i])
        for i, (at, out) in enumerate(((last, gx_ref), (height - 1 - last, gp_ref)))
    ]
    for copy in copies:
        copy.start()
    for copy in copies:
        copy.wait()


def far_rows_kernel(x_ref, u_ref, mask_ref, hx_ref, hp_ref, bits_ref):
    samples, height, across, c = x_ref.shape
    even = lax.axis_index("lat") % 2 == 0
    for k in range(bits_ref.shape[0]):
        bits = mask_ref[k * 128 : (k + 1) * 128].astype(F32)
        bits = jnp.concatenate([bits, jnp.zeros((bits.shape[0], 128 - across), F32)], 1)
        if bits.shape[0] < 128:
            bits = jnp.concatenate([bits, jnp.zeros((128 - bits.shape[0], 128), F32)], 0)
        bits_ref[k] = bits.T[:across]
    for out, down in ((hx_ref, even), (hp_ref, jnp.logical_not(even))):
        first = jnp.where(down, height - 3, 1)
        edge = jnp.where(down, height - 1, 0)
        for s in range(samples):
            out[2 * s] = x_ref[s, first]
            out[2 * s + 1] = x_ref[s, first + 1]
            out[2 * samples + s] = u_ref[s, edge]
        for k in range(bits_ref.shape[0]):
            out[3 * samples + k] = bits_ref[k].astype(BF16)


def masks_kernel(bits_ref, m_ref, count_ref):
    samples, height, across, c = m_ref.shape
    count = jnp.zeros((8, c), F32)
    for s in range(samples):
        for r in range(height):
            mask = column_mask(bits_ref, s * height + r, c)
            m_ref[s, r] = mask
            count += fold(mask)
    count_ref[...] = stats_block([count.sum(0, keepdims=True)], c)


def stats_block(rows, c):
    return jnp.concatenate(rows + [jnp.zeros((8 - len(rows), c), F32)], 0)


def gather(refs):
    return jnp.concatenate([r[...] for r in refs], 0)


def middle(value):
    return value.mean(0, keepdims=True)


def add_moments(sums, active, mask):
    masked = active * mask
    sums[0] += fold(masked)
    sums[1] += fold(masked * active)
    return masked


def conv1_kernel(gp_ref, gx_ref, x_ref, m_ref, count_ref, w_ref, b_ref, a_ref, z_ref, t_ref, st_ref):
    samples, height, across, c = x_ref.shape
    even = lax.axis_index("lat") % 2 == 0
    fill_toeplitz(w_ref, t_ref)
    bias = 0.5 * b_ref[...]
    sums = [jnp.zeros((8, c), F32) for _ in range(2)]
    centre = None
    for s in range(samples):

        def row(r):
            if r < 0:
                return pick(even, gp_ref[s, 0], gx_ref[s, 0])
            if r >= height:
                return pick(even, gx_ref[s, 0], gp_ref[s, 0])
            return x_ref[s, r]

        piece = convolve_rows(row, range(0, height, 2), t_ref, across, False)
        for r in range(height):
            half = piece(r // 2, r % 2) + bias
            active = silu(half)
            if centre is None:
                centre = middle(active)
            active = active - centre
            a_ref[s, r] = active
            z_ref[s, r] = half
            add_moments(sums, active, m_ref[s, r])
    rows = [v.sum(0, keepdims=True) for v in sums]
    st_ref[...] = stats_block([rows[0], rows[1], centre, count_ref[0:1]], c)


def prepare_kernel(u_ref, m_ref, w2_ref, mu_ref, su_ref, t2_ref, tt2_ref):
    samples, height, across, c = u_ref.shape
    fill_toeplitz(w2_ref, t2_ref)
    fill_toeplitz_transposed(w2_ref, tt2_ref)
    total = jnp.zeros((8, c), F32)
    for s in range(samples):
        for r in range(height):
            value = u_ref[s, r].astype(F32) * m_ref[s, r]
            mu_ref[s, r] = value
            total += fold(value)
    su_ref[...] = stats_block([total.sum(0, keepdims=True)], c)


def conv1_edge_kernel(
    hp_ref, hx_ref, gp_ref, gx_ref, x_ref, st_ref, t_ref, b_ref, a_ref, mh_ref, muh_ref
):
    samples, height, across, c = x_ref.shape
    even = lax.axis_index("lat") % 2 == 0
    bias = 0.5 * b_ref[...]
    centre = st_ref[2:3]

    def row(r):
        parts = []
        for s in range(samples):
            if r < -1:
                parts.append(pick(even, hp_ref[2 * s + r + 3], hx_ref[2 * s + r + 3]))
            elif r == -1:
                parts.append(pick(even, gp_ref[s, 0], gx_ref[s, 0]))
            elif r < height:
                parts.append(x_ref[s, r])
            elif r == height:
                parts.append(pick(even, gx_ref[s, 0], gp_ref[s, 0]))
            else:
                j = r - height - 1
                parts.append(pick(even, hx_ref[2 * s + j], hp_ref[2 * s + j]))
        return jnp.concatenate(parts, 0)

    slabs = slice(3 * samples, hx_ref.shape[0])
    above = pick(even, hp_ref[slabs], hx_ref[slabs])
    below = pick(even, hx_ref[slabs], hp_ref[slabs])
    for slot, start in ((0, -2), (2, height)):
        piece = convolve_rows(row, (start,), t_ref, across, False)
        for s in range(samples):
            for j in range(2):
                a_ref[s, slot + j] = silu(piece(s, j) + bias) - centre
                if start < 0:
                    mask = column_mask(above, s * height + height - 2 + j, c)
                else:
                    mask = column_mask(below, s * height + j, c)
                mh_ref[s, slot + j] = mask
    for s in range(samples):
        up = pick(even, hp_ref[2 * samples + s], hx_ref[2 * samples + s])
        muh_ref[s, 0] = up.astype(F32) * mh_ref[s, 1]
        down = pick(even, hx_ref[2 * samples + s], hp_ref[2 * samples + s])
        muh_ref[s, 1] = down.astype(F32) * mh_ref[s, 2]


def conv2_kernel(
    pieces,
    own_ref, a_ref, ah_ref, m_ref, mh_ref, mu_ref, su_ref, k_ref, b_ref, g_ref, t_ref, *refs,
):
    stats, (n_ref, a2_ref, z2_ref, c1_ref, st2_ref, ext_ref) = gather(refs[:pieces]), refs[pieces:]
    samples, height, across, c = m_ref.shape
    counts = stats[:, 3:4]
    count = counts.sum(0)
    mean, inverse = join(stats, count, 0, counts)
    offset = mean - own_ref[2:3]
    scale = inverse * g_ref[...]
    shift = t_ref[...] - offset * scale
    c1_ref[...] = stats_block([offset, inverse, count, mean], c)
    bias = 0.5 * b_ref[...]
    sums = [jnp.zeros((8, c), F32) for _ in range(3)]
    centre = None
    for s in range(samples):
        ext = ext_ref.at[s % 2]
        for i in range(height + 4):
            r = i - 2
            if 0 <= r < height:
                value, mask = a_ref[s, r], m_ref[s, r]
            else:
                j = i if r < 0 else r - height + 2
                value, mask = ah_ref[s, j], mh_ref[s, j]
            ext[i] = ((value * scale + shift) * mask).astype(BF16)
            if 1 <= i < height + 3:
                n_ref[s, i - 1] = ext[i]

        piece = convolve_rows(
            lambda r: ext[r + 2], range(-1, height + 1, 2), k_ref, across, False
        )
        for i in range(height + 2):
            r = i - 1
            half = piece(i // 2, i % 2) + bias
            active = silu(half)
            if centre is None:
                centre = middle(active)
            active = active - centre
            if 0 <= r < height:
                add_moments(sums, active, m_ref[s, r])
                sums[2] += fold(active * mu_ref[s, r])
            a2_ref[s, i] = active
            z2_ref[s, i] = half
    rows = [v.sum(0, keepdims=True) for v in sums]
    st2_ref[...] = stats_block(
        [rows[0], rows[1], centre, rows[2], su_ref[0:1], own_ref[3:4]], c
    )


def slopes_kernel(z_ref, z2_ref, m_ref, mh_ref, after_ref, s_ref, s2_ref):
    samples, height = m_ref.shape[:2]
    for s in range(samples):
        for r in range(-1, height + 1):
            mask = mh_ref[s, 1 if r < 0 else 2]
            if 0 <= r < height:
                mask = m_ref[s, r]
                s_ref[s, r] = silu_slope(z_ref[s, r]) * mask
            s2_ref[s, r + 1] = silu_slope(z2_ref[s, r + 1]) * mask


def back_terms(scale, inverse, offset, gain_sum, shift_sum, count):
    by_active = -scale * gain_sum * inverse / count
    constant = -scale * (shift_sum - offset * inverse * gain_sum) / count
    return by_active, constant


def back2_kernel(
    pieces,
    own_ref, st1_ref, c1_ref, a2_ref, s2_ref, mu_ref, muh_ref, m_ref, a_ref, k_ref, g_ref, t_ref, *refs,
):
    stats, (d_ref, dn_ref, c2_ref, st3_ref, ext_ref) = gather(refs[:pieces]), refs[pieces:]
    samples, height, across, c = m_ref.shape
    count = c1_ref[2:3]
    mean, inverse = join(stats, count, 0, stats[:, 5:6])
    offset = mean - own_ref[2:3]
    shift_sum = stats[:, 4:5].sum(0)
    away = stats[:, 2:3] - mean
    gain_sum = inverse * (stats[:, 3:4] + away * stats[:, 4:5]).sum(0)
    scale = inverse * g_ref[...]
    by_active, constant = back_terms(scale, inverse, offset, gain_sum, shift_sum, count)
    c2_ref[...] = stats_block([scale, t_ref[...] - offset * scale, gain_sum, shift_sum], c)
    sums = [jnp.zeros((8, c), F32) for _ in range(2)]
    for s in range(samples):
        ext = ext_ref.at[s % 2]
        for i in range(height + 2):
            upstream = mu_ref[s, i - 1] if 0 < i <= height else muh_ref[s, 0 if i == 0 else 1]
            grad = upstream * scale + (a2_ref[s, i] * by_active + constant)
            ext[i] = (grad * s2_ref[s, i]).astype(BF16)
            if 0 < i <= height:
                d_ref[s, i - 1] = ext[i]
        piece = convolve_rows(
            lambda r: ext[r + 1], range(0, height, 2), k_ref, across, True
        )
        for r in range(height):
            part = piece(r // 2, r % 2)
            dn_ref[s, r] = part
            masked = part * m_ref[s, r]
            sums[0] += fold(masked)
            sums[1] += fold(masked * a_ref[s, r])
    rows = [v.sum(0, keepdims=True) for v in sums]
    st3_ref[...] = stats_block([rows[0], rows[1], st1_ref[2:3]], c)


def weight_products(rows, centre, turned, total_ref, first):
    windows = jnp.concatenate(rows, 1)
    product = lax.dot_general(
        windows,
        jnp.concatenate([turned[0], centre, turned[1]], 1),
        (((0,), (0,)), ((), ())),
        preferred_element_type=F32,
    )
    if first:
        total_ref[...] = product
    else:
        total_ref[...] += product


def turn(value, across):
    c = value.shape[-1]
    return [
        pltpu.roll(value, k, 1).astype(BF16).reshape(-1, c) for k in (across - 1, 1)
    ]


def weight2_kernel(n_ref, d_ref, after_ref, w_ref, b_ref, acc_ref):
    samples, height, across, c = d_ref.shape
    bias = jnp.zeros((8, c), F32)
    for s in range(samples):
        grad = d_ref[s]
        wide = grad.astype(F32)
        bias += fold(wide)
        rows = [n_ref[s, a : a + height].reshape(-1, c) for a in range(3)]
        weight_products(rows, grad.reshape(-1, c), turn(wide, across), acc_ref, s == 0)
    b_ref[...] = jnp.broadcast_to(bias.sum(0, keepdims=True), b_ref.shape)
    for a in range(3):
        for b in range(3):
            at = (a * 3 + b) * c
            w_ref[at : at + c] = acc_ref[a * c : (a + 1) * c, b * c : (b + 1) * c].astype(BF16)


def output_kernel(x_ref, a2_ref, m_ref, c2_ref, after_ref, o_ref, done_ref):
    samples, height, across, c = x_ref.shape
    scale, shift = c2_ref[0:1], c2_ref[1:2]
    for s in range(samples):
        for r in range(height):
            normed = (a2_ref[s, r + 1] * scale + shift) * m_ref[s, r]
            o_ref[s, r] = (x_ref[s, r].astype(F32) + normed).astype(BF16)
    done_ref[...] = jnp.zeros(done_ref.shape, F32)


def small_rows(rows, c):
    high = jnp.concatenate(rows + [jnp.zeros((8 - len(rows), c), F32)], 0)
    first = high.astype(BF16)
    return jnp.concatenate([first, (high - first.astype(F32)).astype(BF16)], 0)


def weight1_kernel(
    group, leads, pieces,
    c1_ref, c2_ref, dn_ref, a_ref, s_ref, x_ref, gx_ref, gp_ref, g_ref, w2_ref, b2_ref, *refs,
):
    stats = gather(refs[:pieces])
    d_ref, send_ref, keep_ref, acc_ref = refs[pieces:]
    samples, height, across, c = x_ref.shape
    even = lax.axis_index("lat") % 2 == 0
    lead = lax.axis_index("lead")
    core = lax.axis_index("dp") % 2
    offset, inverse, count, mean = (c1_ref[i : i + 1] for i in range(4))
    shift_sum = stats[:, 0:1].sum(0)
    away = stats[:, 2:3] - mean
    gain_sum = inverse * (stats[:, 1:2] + away * stats[:, 0:1]).sum(0)
    scale = inverse * g_ref[...]
    by_active, constant = back_terms(scale, inverse, offset, gain_sum, shift_sum, count)
    bias = jnp.zeros((8, c), F32)
    for s in range(samples):
        for r in range(height):
            active = a_ref[s, r]
            grad = dn_ref[s, r] * scale + (active * by_active + constant)
            d_ref[s, r] = (grad * s_ref[s, r]).astype(BF16)
        grad = d_ref[s]
        wide = grad.astype(F32)
        bias += fold(wide)
        above = pick(even, gp_ref[s, 0], gx_ref[s, 0])
        below = pick(even, gx_ref[s, 0], gp_ref[s, 0])
        body = x_ref[s].reshape(-1, c)
        rows = [
            jnp.concatenate([above, body[: (height - 1) * across]], 0),
            body,
            jnp.concatenate([body[across:], below], 0),
        ]
        weight_products(rows, grad.reshape(-1, c), turn(wide, across), acc_ref, s == 0)

    share = 1.0 / group
    small = [
        small_rows([bias.sum(0, keepdims=True), gain_sum * share, shift_sum * share], c),
        small_rows([b2_ref[0:1], c2_ref[2:3] * share, c2_ref[3:4] * share], c),
    ]

    def put(target, which):
        size = 9 * c // leads
        for j in range(leads):
            slot = j ^ lead
            if which == 1:
                target[slot, :size] = w2_ref[j * size : (j + 1) * size]
            else:
                at = j * size
                while at < (j + 1) * size:
                    tap, low = at // c, at % c
                    step = min(c - low, (j + 1) * size - at)
                    a, b = tap // 3, tap % 3
                    target[slot, at - j * size : at - j * size + step] = acc_ref[
                        a * c + low : a * c + low + step, b * c : (b + 1) * c
                    ].astype(BF16)
                    at += step
            target[slot, size:] = small[which]

    @pl.when(core == 0)
    def _():
        put(keep_ref, 0)
        put(send_ref, 1)

    @pl.when(core != 0)
    def _():
        put(keep_ref, 1)
        put(send_ref, 0)


def edge_rows_kernel(d_ref, after_ref, dx_ref, dp_ref):
    samples, height = d_ref.shape[:2]
    even = lax.axis_index("lat") % 2 == 0
    for s in range(samples):
        dx_ref[s] = pick(even, d_ref[s, height - 1], d_ref[s, 0])
        dp_ref[s] = pick(even, d_ref[s, 0], d_ref[s, height - 1])


def input_grad_kernel(ep_ref, ex_ref, d_ref, u_ref, w_ref, o_ref, done_ref, k_ref):
    samples, height, across, c = u_ref.shape
    even = lax.axis_index("lat") % 2 == 0
    fill_toeplitz_transposed(w_ref, k_ref)
    for s in range(samples):

        def row(r):
            if r < 0:
                return pick(even, ep_ref[s], ex_ref[s])
            if r >= height:
                return pick(even, ex_ref[s], ep_ref[s])
            return d_ref[s, r]

        piece = convolve_rows(row, range(0, height, 2), k_ref, across, True)
        for r in range(height):
            o_ref[s, r] = (u_ref[s, r].astype(F32) + piece(r // 2, r % 2)).astype(BF16)
    done_ref[...] = jnp.zeros(done_ref.shape, F32)


def join_kernel(leads, *refs):
    out_ref = refs[-1]
    size = refs[0].shape[0] - SMALL
    for k in range(leads):
        out_ref[k * size : (k + 1) * size] = refs[k][:size]
    out_ref[leads * size :] = refs[0][size:]


def finish_kernel(leads, own_ref, other_ref, *refs):
    first, second = refs[:4], refs[4:]
    core = lax.axis_index("dp") % 2
    lead = lax.axis_index("lead")
    size = (own_ref.shape[0] - SMALL) // leads

    def put(outs, ref):
        for k in range(leads):
            at = pl.multiple_of((k ^ lead) * size, 16)
            outs[0][pl.ds(at, size)] = ref[k * size : (k + 1) * size].astype(F32)
        small = ref[leads * size :].astype(F32)
        total = small[:8] + small[8:]
        for i in range(3):
            outs[i + 1][...] = total[i : i + 1]

    @pl.when(core == 0)
    def _():
        put(first, own_ref)
        put(second, other_ref)

    @pl.when(core != 0)
    def _():
        put(first, other_ref)
        put(second, own_ref)


def add_kernel(parts, waits, *refs):
    outs = refs[parts + waits :]
    size = outs[0].shape[0] - SMALL
    for k, out in enumerate(outs):
        chunk = [r.at[k] if len(r.shape) == 3 else r for r in refs[:parts]]
        total = functools.reduce(lambda a, b: a + b, [r[...].astype(F32) for r in chunk])
        out[:size] = total[:size].astype(BF16)
        small = total[size : size + 8] + total[size + 8 :]
        high = small.astype(BF16)
        out[size:] = jnp.concatenate([high, (small - high.astype(F32)).astype(BF16)], 0)


def call(kernel, outs, scratch, operands, name, flops=0, waits=(), spaces=(VMEM, VMEM)):
    size = sum(o.size * o.dtype.itemsize for o in operands)
    return pl.pallas_call(
        kernel,
        out_shape=outs,
        in_specs=[spaces[0]] * len(operands) + [pl.BlockSpec(memory_space=pl.ANY)] * len(waits),
        out_specs=jax.tree.map(lambda _: spaces[1], outs),
        scratch_shapes=scratch,
        compiler_params=pltpu.CompilerParams(vmem_limit_bytes=16 * 2**20),
        cost_estimate=pl.CostEstimate(flops=flops, bytes_accessed=size, transcendentals=0),
        name=name,
    )(*operands, *waits)


def swap(value, axis, k):
    return lax.ppermute(value, axis, [(i, i ^ k) for i in range(lax.axis_size(axis))])


def neighbours(value_x, value_p, axis):
    n = lax.axis_size(axis)
    first = [(i, i ^ 1) for i in range(n) if i ^ 1 < n]
    second = [(i, i + 1) for i in range(1, n - 1, 2)]
    second += [(j, i) for i, j in second]
    got_p = lax.ppermute(value_p, axis, second)
    return lax.ppermute(value_x, axis, first), got_p


def spread(stats):
    blocks, k = stats[None], 1
    while k < lax.axis_size("dp"):
        blocks = jnp.concatenate([blocks, swap(blocks, "dp", k)], 0)
        k *= 2
    return [blocks] + [swap(blocks, "lat", k) for k in range(1, lax.axis_size("lat"))]


def add_chunks(parts, name, outs=1, waits=(), flops=0):
    shape = jax.ShapeDtypeStruct(parts[0].shape[-2:], BF16)
    return call(
        functools.partial(add_kernel, len(parts), len(waits)),
        [shape] * outs,
        [],
        parts,
        name,
        flops,
        waits,
    )


def sum_everywhere(send, keep, edges, block_output, input_grad):
    leads, lats = lax.axis_size("lead"), lax.axis_size("lat")
    chunks = add_chunks([keep, swap(send, "dp", 1)], "add_dp", leads)
    got = [swap(chunks[k], "lead", k) for k in reversed(range(1, leads))]
    output = block_output(chunks[0])
    (mine,) = add_chunks([chunks[0]] + got, "add_lead", waits=(output[1],))
    got = [swap(mine, "lat", k) for k in range(1, lats)]
    rows = edges(mine)
    (mine,) = add_chunks([mine] + got, "add_lat", flops=HIDE)
    k = 2
    while k < lax.axis_size("dp"):
        (mine,) = add_chunks([mine, swap(mine, "dp", k)], "add_far_dp")
        k *= 2
    size, c = mine.shape[0] - SMALL, mine.shape[1]
    got = [swap(mine, "lead", k) for k in range(1, leads)]
    grad_input = input_grad(rows)
    own = call(
        functools.partial(join_kernel, leads),
        jax.ShapeDtypeStruct((leads * size + SMALL, c), BF16),
        [],
        (mine, *got),
        "join",
        waits=(grad_input[1],),
    )
    one = [jax.ShapeDtypeStruct((leads * size, c), F32)] + [jax.ShapeDtypeStruct((1, c), F32)] * 3
    sums = call(
        functools.partial(finish_kernel, leads), one + one, [], (own, swap(own, "dp", 1)), "finish"
    )
    return sums[:4], sums[4:], output[0], grad_input[0]


def shards(
    field,
    cotangent,
    land_sea,
    conv1_weight,
    conv1_bias,
    first_norm_scale,
    norm1_shift,
    conv2_weight,
    conv2_bias,
    second_norm_scale,
    norm2_shift,
):
    x, u, mask = field[0], cotangent[0], land_sea[0]
    samples, height, across, c = x.shape
    group = lax.axis_size("dp") * lax.axis_size("lat")
    leads = lax.axis_size("lead")
    slabs = -(-samples * height // 128)
    vec = lambda v: v.reshape(1, c)
    b1, g1, t1 = vec(conv1_bias), vec(first_norm_scale), vec(norm1_shift)
    b2, g2, t2 = vec(conv2_bias), vec(second_norm_scale), vec(norm2_shift)

    array = jax.ShapeDtypeStruct
    shape = lambda rows, dtype=F32: array((samples, rows, across, c), dtype)
    edge = array((samples, across, c), BF16)
    vector = array((8, c), F32)
    weights = array((3, 4 * c, 2 * c), BF16)
    turned = array((3, 2 * c, 4 * c), BF16)
    ext = lambda rows: pltpu.VMEM((2, rows, across, c), BF16)
    acc = pltpu.VMEM((3 * c, 3 * c), F32)
    conv_flops = 2 * 9 * c * c * samples * height * across

    near = call(
        near_rows_kernel,
        (shape(1, BF16), shape(1, BF16)),
        [pltpu.SemaphoreType.DMA((2,))],
        (x,),
        "near_rows",
        conv_flops,
        spaces=(pl.BlockSpec(memory_space=pl.ANY),) * 2,
    )
    gx, gp = neighbours(*near, "lat")
    packed = array((3 * samples + slabs, across, c), BF16)
    far_x, far_p, bits = call(
        far_rows_kernel,
        (packed, packed, array((slabs, across, 128), F32)),
        [],
        (x, u, mask.reshape(samples * height, across)),
        "far_rows",
        conv_flops,
    )
    hx, hp = neighbours(far_x, far_p, "lat")
    wide_mask, count = call(masks_kernel, (shape(height), vector), [], (bits,), "masks", conv_flops)
    a1, z1, w1t, own1 = call(
        conv1_kernel,
        (shape(height), shape(height), weights, vector),
        [],
        (gp, gx, x, wide_mask, count, conv1_weight, b1),
        "conv1",
        16 * conv_flops,
    )
    mu, mu_sum, w2t, w2tt = call(
        prepare_kernel,
        (shape(height), vector, weights, turned),
        [],
        (u, wide_mask, conv2_weight),
        "prepare",
        conv_flops,
    )
    a1h, halo_mask, mu_halo = call(
        conv1_edge_kernel,
        (shape(4), shape(4), shape(2)),
        [],
        (hp, hx, gp, gx, x, own1, w1t, b1),
        "conv1_edges",
        conv_flops // 2,
    )
    st1 = spread(own1)
    n1, a2, z2, c1, own2 = call(
        functools.partial(conv2_kernel, len(st1)),
        (shape(height + 2, BF16), shape(height + 2), shape(height + 2), vector, vector),
        [ext(height + 4)],
        (own1, a1, a1h, wide_mask, halo_mask, mu, mu_sum, w2t, b2, g1, t1, *st1),
        "conv2",
        conv_flops,
    )
    st2 = spread(own2)
    s1, s2 = call(
        slopes_kernel,
        (shape(height), shape(height + 2)),
        [],
        (z1, z2, wide_mask, halo_mask),
        "slopes",
        conv_flops,
        waits=(st2[0],),
    )
    d2, dn1, c2, own3 = call(
        functools.partial(back2_kernel, len(st2)),
        (shape(height, BF16), shape(height), vector, vector),
        [ext(height + 2)],
        (own2, own1, c1, a2, s2, mu, mu_halo, wide_mask, a1, w2tt, g2, t2, *st2),
        "conv2_back",
        conv_flops,
    )
    st3 = spread(own3)
    w2, bias2 = call(
        weight2_kernel,
        (array((9 * c, c), BF16), vector),
        [acc],
        (n1, d2),
        "conv2_weight_grad",
        conv_flops,
        waits=(st3[0],),
    )
    chunks = array((leads, 9 * c // leads + SMALL, c), BF16)
    d1, send, keep = call(
        functools.partial(weight1_kernel, group, leads, len(st3)),
        (shape(height, BF16), chunks, chunks),
        [acc],
        (c1, c2, dn1, a1, s1, x, gx, gp, g1, w2, bias2, *st3),
        "conv1_weight_grad",
        conv_flops,
    )

    def edges(after):
        rows = call(edge_rows_kernel, (edge, edge), [], (d1,), "edge_rows", waits=(after,))
        return neighbours(*rows, "lat")[::-1]

    def input_grad(rows):
        return call(
            input_grad_kernel,
            (shape(height, BF16), vector),
            [pltpu.VMEM(turned.shape, BF16)],
            (*rows, d1, u, conv1_weight),
            "conv1_back",
            conv_flops,
        )

    def block_output(after):
        return call(
            output_kernel,
            (shape(height, BF16), vector),
            [],
            (x, a2, wide_mask, c2),
            "output",
            conv_flops // 2,
            waits=(after,),
        )

    first, second, output, grad_input = sum_everywhere(
        send, keep, edges, block_output, input_grad
    )
    sums = []
    for part in (first, second):
        sums += [part[0].reshape(3, 3, c, c)] + [v.reshape(c) for v in part[1:]]
    return (output[None], grad_input[None], *sums)


def solution(mesh):
    tiles = P("lead", "dp", "lat", None, None)
    in_specs = (tiles, tiles, P("lead", "dp", "lat", None)) + (P(),) * 8
    out_specs = (tiles, tiles) + (P(),) * 8
    return jax.shard_map(shards, mesh=mesh, in_specs=in_specs, out_specs=out_specs, check_vma=False)
```

```python
import functools

import jax
import jax.numpy as jnp
from jax import lax
from jax.experimental import pallas as pl
from jax.experimental.pallas import tpu as pltpu
from jax.sharding import PartitionSpec as P

EPSILON = 1e-05
BF16 = jnp.bfloat16
F32 = jnp.float32
VMEM = pl.BlockSpec(memory_space=pltpu.VMEM)
ANY = pl.BlockSpec(memory_space=pl.ANY)
HIDE = 10**11
SMALL = 16


def fill_toeplitz(taps_ref, out_ref):
    c = taps_ref.shape[-1]
    zero = jnp.zeros((c, c), BF16)
    half = jnp.asarray(0.5, BF16)
    for b in range(3):
        for i in range(4):
            for j in range(2):
                block = taps_ref[i - j, b] * half if 0 <= i - j < 3 else zero
                out_ref[b, i * c : (i + 1) * c, j * c : (j + 1) * c] = block


def fill_toeplitz_transposed(taps_ref, out_ref):
    c = taps_ref.shape[-1]
    zero = jnp.zeros((c, c), BF16)
    for b in range(3):
        for i in range(4):
            for j in range(2):
                block = taps_ref[2 - (i - j), 2 - b] if 0 <= i - j < 3 else zero
                out_ref[b, j * c : (j + 1) * c, i * c : (i + 1) * c] = block


def convolve_rows(row, starts, weights_ref, across, transposed):
    left = jnp.concatenate(
        [jnp.concatenate([row(r - 1 + i) for r in starts], 0) for i in range(4)], 1
    )
    c = left.shape[1] // 4
    dims = (((1,), (1 if transposed else 0,)), ((), ()))
    taps = [
        lax.dot_general(left, weights_ref[b], dims, preferred_element_type=F32)
        for b in range(3)
    ]

    def piece(pair, j):
        part = [t[pair * across : (pair + 1) * across, j * c : (j + 1) * c] for t in taps]
        return pltpu.roll(part[0], 1, 0) + part[1] + pltpu.roll(part[2], across - 1, 0)

    return piece


def silu(half):
    return half + half * jnp.tanh(half)


def silu_slope(half):
    t = jnp.tanh(half)
    return (0.5 + 0.5 * t) * (1.0 + half * (1.0 - t))


def fold(value):
    return value.reshape(-1, 8, value.shape[-1]).sum(0)


def join(stats, count, at, sums):
    centres = stats[:, at + 2 : at + 3]
    mean = (stats[:, at : at + 1] + sums * centres).sum(0) / count
    away = centres - mean
    squares = stats[:, at + 1 : at + 2] + away * (2.0 * stats[:, at : at + 1] + sums * away)
    variance = jnp.maximum(squares.sum(0) / count, 0.0)
    return mean, lax.rsqrt(variance + EPSILON)


def pick(even, when_even, when_odd):
    return jnp.where(even, when_even, when_odd)


def column_mask(bits, k, c):
    tile = bits[k // 128]
    return jnp.broadcast_to(tile[:, k % 128 : k % 128 + 1].astype(F32), (tile.shape[0], c))


def near_rows_kernel(x_ref, gx_ref, gp_ref, sems):
    height = x_ref.shape[1]
    even = lax.axis_index("lat") % 2 == 0
    last = jnp.where(even, height - 1, 0)
    copies = [
        pltpu.make_async_copy(x_ref.at[:, pl.ds(at, 1)], out, sems.at[i])
        for i, (at, out) in enumerate(((last, gx_ref), (height - 1 - last, gp_ref)))
    ]
    for copy in copies:
        copy.start()
    for copy in copies:
        copy.wait()


def far_rows_kernel(x_ref, u_ref, mask_ref, hx_ref, hp_ref, bits_ref):
    samples, height, across, c = x_ref.shape
    even = lax.axis_index("lat") % 2 == 0
    for k in range(bits_ref.shape[0]):
        bits = mask_ref[k * 128 : (k + 1) * 128].astype(F32)
        bits = jnp.concatenate([bits, jnp.zeros((bits.shape[0], 128 - across), F32)], 1)
        if bits.shape[0] < 128:
            bits = jnp.concatenate([bits, jnp.zeros((128 - bits.shape[0], 128), F32)], 0)
        bits_ref[k] = bits.T[:across]
    for out, down in ((hx_ref, even), (hp_ref, jnp.logical_not(even))):
        first = jnp.where(down, height - 3, 1)
        edge = jnp.where(down, height - 1, 0)
        for s in range(samples):
            out[2 * s] = x_ref[s, first]
            out[2 * s + 1] = x_ref[s, first + 1]
            out[2 * samples + s] = u_ref[s, edge]
        for k in range(bits_ref.shape[0]):
            out[3 * samples + k] = bits_ref[k].astype(BF16)


def masks_kernel(bits_ref, m_ref, count_ref):
    samples, height, across, c = m_ref.shape
    count = jnp.zeros((8, c), F32)
    for s in range(samples):
        for r in range(height):
            mask = column_mask(bits_ref, s * height + r, c)
            m_ref[s, r] = mask
            count += fold(mask)
    count_ref[...] = stats_block([count.sum(0, keepdims=True)], c)


def stats_block(rows, c):
    return jnp.concatenate(rows + [jnp.zeros((8 - len(rows), c), F32)], 0)


def gather(refs):
    return jnp.concatenate([r[...] for r in refs], 0)


def middle(value):
    return value.mean(0, keepdims=True)


def add_moments(sums, active, mask):
    masked = active * mask
    sums[0] += fold(masked)
    sums[1] += fold(masked * active)
    return masked


def conv1_kernel(gp_ref, gx_ref, x_ref, m_ref, count_ref, w_ref, b_ref, a_ref, z_ref, t_ref, st_ref):
    samples, height, across, c = x_ref.shape
    even = lax.axis_index("lat") % 2 == 0
    fill_toeplitz(w_ref, t_ref)
    bias = 0.5 * b_ref[...]
    sums = [jnp.zeros((8, c), F32) for _ in range(2)]
    centre = None
    for s in range(samples):

        def row(r):
            if r < 0:
                return pick(even, gp_ref[s, 0], gx_ref[s, 0])
            if r >= height:
                return pick(even, gx_ref[s, 0], gp_ref[s, 0])
            return x_ref[s, r]

        piece = convolve_rows(row, range(0, height, 2), t_ref, across, False)
        for r in range(height):
            half = piece(r // 2, r % 2) + bias
            active = silu(half)
            if centre is None:
                centre = middle(active)
            active = active - centre
            a_ref[s, r] = active
            z_ref[s, r] = half
            add_moments(sums, active, m_ref[s, r])
    rows = [v.sum(0, keepdims=True) for v in sums]
    st_ref[...] = stats_block([rows[0], rows[1], centre, count_ref[0:1]], c)


def prepare_kernel(u_ref, m_ref, w2_ref, mu_ref, su_ref, t2_ref, tt2_ref):
    samples, height, across, c = u_ref.shape
    fill_toeplitz(w2_ref, t2_ref)
    fill_toeplitz_transposed(w2_ref, tt2_ref)
    total = jnp.zeros((8, c), F32)
    for s in range(samples):
        for r in range(height):
            value = u_ref[s, r].astype(F32) * m_ref[s, r]
            mu_ref[s, r] = value
            total += fold(value)
    su_ref[...] = stats_block([total.sum(0, keepdims=True)], c)


def conv1_edge_kernel(
    hp_ref, hx_ref, gp_ref, gx_ref, x_ref, st_ref, t_ref, b_ref, a_ref, mh_ref, muh_ref
):
    samples, height, across, c = x_ref.shape
    even = lax.axis_index("lat") % 2 == 0
    bias = 0.5 * b_ref[...]
    centre = st_ref[2:3]

    def row(r):
        parts = []
        for s in range(samples):
            if r < -1:
                parts.append(pick(even, hp_ref[2 * s + r + 3], hx_ref[2 * s + r + 3]))
            elif r == -1:
                parts.append(pick(even, gp_ref[s, 0], gx_ref[s, 0]))
            elif r < height:
                parts.append(x_ref[s, r])
            elif r == height:
                parts.append(pick(even, gx_ref[s, 0], gp_ref[s, 0]))
            else:
                j = r - height - 1
                parts.append(pick(even, hx_ref[2 * s + j], hp_ref[2 * s + j]))
        return jnp.concatenate(parts, 0)

    slabs = slice(3 * samples, hx_ref.shape[0])
    above = pick(even, hp_ref[slabs], hx_ref[slabs])
    below = pick(even, hx_ref[slabs], hp_ref[slabs])
    for slot, start in ((0, -2), (2, height)):
        piece = convolve_rows(row, (start,), t_ref, across, False)
        for s in range(samples):
            for j in range(2):
                a_ref[s, slot + j] = silu(piece(s, j) + bias) - centre
                if start < 0:
                    mask = column_mask(above, s * height + height - 2 + j, c)
                else:
                    mask = column_mask(below, s * height + j, c)
                mh_ref[s, slot + j] = mask
    for s in range(samples):
        up = pick(even, hp_ref[2 * samples + s], hx_ref[2 * samples + s])
        muh_ref[s, 0] = up.astype(F32) * mh_ref[s, 1]
        down = pick(even, hx_ref[2 * samples + s], hp_ref[2 * samples + s])
        muh_ref[s, 1] = down.astype(F32) * mh_ref[s, 2]


def conv2_kernel(
    pieces,
    own_ref, a_ref, ah_ref, m_ref, mh_ref, mu_ref, su_ref, k_ref, b_ref, g_ref, t_ref, *refs,
):
    stats, (n_ref, a2_ref, z2_ref, c1_ref, st2_ref, ext_ref) = gather(refs[:pieces]), refs[pieces:]
    samples, height, across, c = m_ref.shape
    counts = stats[:, 3:4]
    count = counts.sum(0)
    mean, inverse = join(stats, count, 0, counts)
    offset = mean - own_ref[2:3]
    scale = inverse * g_ref[...]
    shift = t_ref[...] - offset * scale
    c1_ref[...] = stats_block([offset, inverse, count, mean], c)
    bias = 0.5 * b_ref[...]
    sums = [jnp.zeros((8, c), F32) for _ in range(3)]
    centre = None
    for s in range(samples):
        ext = ext_ref.at[s % 2]
        for i in range(height + 4):
            r = i - 2
            if 0 <= r < height:
                value, mask = a_ref[s, r], m_ref[s, r]
            else:
                j = i if r < 0 else r - height + 2
                value, mask = ah_ref[s, j], mh_ref[s, j]
            ext[i] = ((value * scale + shift) * mask).astype(BF16)
            if 1 <= i < height + 3:
                n_ref[s, i - 1] = ext[i]

        piece = convolve_rows(
            lambda r: ext[r + 2], range(-1, height + 1, 2), k_ref, across, False
        )
        for i in range(height + 2):
            r = i - 1
            half = piece(i // 2, i % 2) + bias
            active = silu(half)
            if centre is None:
                centre = middle(active)
            active = active - centre
            if 0 <= r < height:
                add_moments(sums, active, m_ref[s, r])
                sums[2] += fold(active * mu_ref[s, r])
            a2_ref[s, i] = active
            z2_ref[s, i] = half
    rows = [v.sum(0, keepdims=True) for v in sums]
    st2_ref[...] = stats_block(
        [rows[0], rows[1], centre, rows[2], su_ref[0:1], own_ref[3:4]], c
    )


def slopes_kernel(z_ref, z2_ref, m_ref, mh_ref, after_ref, s_ref, s2_ref):
    samples, height = m_ref.shape[:2]
    for s in range(samples):
        for r in range(-1, height + 1):
            mask = mh_ref[s, 1 if r < 0 else 2]
            if 0 <= r < height:
                mask = m_ref[s, r]
                s_ref[s, r] = silu_slope(z_ref[s, r]) * mask
            s2_ref[s, r + 1] = silu_slope(z2_ref[s, r + 1]) * mask


def back_terms(scale, inverse, offset, gain_sum, shift_sum, count):
    by_active = -scale * gain_sum * inverse / count
    constant = -scale * (shift_sum - offset * inverse * gain_sum) / count
    return by_active, constant


def back2_kernel(
    pieces,
    own_ref, st1_ref, c1_ref, a2_ref, s2_ref, mu_ref, muh_ref, m_ref, a_ref, k_ref, g_ref, t_ref, *refs,
):
    stats, (d_ref, dn_ref, c2_ref, st3_ref, ext_ref) = gather(refs[:pieces]), refs[pieces:]
    samples, height, across, c = m_ref.shape
    count = c1_ref[2:3]
    mean, inverse = join(stats, count, 0, stats[:, 5:6])
    offset = mean - own_ref[2:3]
    shift_sum = stats[:, 4:5].sum(0)
    away = stats[:, 2:3] - mean
    gain_sum = inverse * (stats[:, 3:4] + away * stats[:, 4:5]).sum(0)
    scale = inverse * g_ref[...]
    by_active, constant = back_terms(scale, inverse, offset, gain_sum, shift_sum, count)
    c2_ref[...] = stats_block([scale, t_ref[...] - offset * scale, gain_sum, shift_sum], c)
    sums = [jnp.zeros((8, c), F32) for _ in range(2)]
    for s in range(samples):
        ext = ext_ref.at[s % 2]
        for i in range(height + 2):
            upstream = mu_ref[s, i - 1] if 0 < i <= height else muh_ref[s, 0 if i == 0 else 1]
            grad = upstream * scale + (a2_ref[s, i] * by_active + constant)
            ext[i] = (grad * s2_ref[s, i]).astype(BF16)
            if 0 < i <= height:
                d_ref[s, i - 1] = ext[i]
        piece = convolve_rows(
            lambda r: ext[r + 1], range(0, height, 2), k_ref, across, True
        )
        for r in range(height):
            part = piece(r // 2, r % 2)
            dn_ref[s, r] = part
            masked = part * m_ref[s, r]
            sums[0] += fold(masked)
            sums[1] += fold(masked * a_ref[s, r])
    rows = [v.sum(0, keepdims=True) for v in sums]
    st3_ref[...] = stats_block([rows[0], rows[1], st1_ref[2:3]], c)


def weight_products(rows, centre, turned, total_ref, first):
    windows = jnp.concatenate(rows, 1)
    product = lax.dot_general(
        windows,
        jnp.concatenate([turned[0], centre, turned[1]], 1),
        (((0,), (0,)), ((), ())),
        preferred_element_type=F32,
    )
    if first:
        total_ref[...] = product
    else:
        total_ref[...] += product


def turn(value, across):
    c = value.shape[-1]
    return [
        pltpu.roll(value, k, 1).astype(BF16).reshape(-1, c) for k in (across - 1, 1)
    ]


def weight2_kernel(n_ref, d_ref, after_ref, w_ref, b_ref, acc_ref):
    samples, height, across, c = d_ref.shape
    bias = jnp.zeros((8, c), F32)
    for s in range(samples):
        grad = d_ref[s]
        wide = grad.astype(F32)
        bias += fold(wide)
        rows = [n_ref[s, a : a + height].reshape(-1, c) for a in range(3)]
        weight_products(rows, grad.reshape(-1, c), turn(wide, across), acc_ref, s == 0)
    b_ref[...] = jnp.broadcast_to(bias.sum(0, keepdims=True), b_ref.shape)
    for a in range(3):
        for b in range(3):
            at = (a * 3 + b) * c
            w_ref[at : at + c] = acc_ref[a * c : (a + 1) * c, b * c : (b + 1) * c].astype(BF16)


def output_kernel(x_ref, a2_ref, m_ref, c2_ref, after_ref, o_hbm, done_ref, o_ref, sems):
    samples, height, across, c = x_ref.shape
    scale, shift = c2_ref[0:1], c2_ref[1:2]
    for s in range(samples):
        for r in range(height):
            normed = (a2_ref[s, r + 1] * scale + shift) * m_ref[s, r]
            o_ref[s, r] = (x_ref[s, r].astype(F32) + normed).astype(BF16)
        pltpu.make_async_copy(o_ref.at[s], o_hbm.at[s], sems.at[s]).start()
    done_ref[...] = jnp.zeros(done_ref.shape, F32)
    for s in range(samples):
        pltpu.make_async_copy(o_ref.at[s], o_hbm.at[s], sems.at[s]).wait()


def small_rows(rows, c):
    high = jnp.concatenate(rows + [jnp.zeros((8 - len(rows), c), F32)], 0)
    first = high.astype(BF16)
    return jnp.concatenate([first, (high - first.astype(F32)).astype(BF16)], 0)


def weight1_kernel(
    group, leads, pieces,
    c1_ref, c2_ref, dn_ref, a_ref, s_ref, x_ref, gx_ref, gp_ref, g_ref, w2_ref, b2_ref, *refs,
):
    stats = gather(refs[:pieces])
    d_ref, send_ref, keep_ref, acc_ref = refs[pieces:]
    samples, height, across, c = x_ref.shape
    even = lax.axis_index("lat") % 2 == 0
    core = lax.axis_index("dp") % 2
    offset, inverse, count, mean = (c1_ref[i : i + 1] for i in range(4))
    shift_sum = stats[:, 0:1].sum(0)
    away = stats[:, 2:3] - mean
    gain_sum = inverse * (stats[:, 1:2] + away * stats[:, 0:1]).sum(0)
    scale = inverse * g_ref[...]
    by_active, constant = back_terms(scale, inverse, offset, gain_sum, shift_sum, count)
    bias = jnp.zeros((8, c), F32)
    for s in range(samples):
        for r in range(height):
            active = a_ref[s, r]
            grad = dn_ref[s, r] * scale + (active * by_active + constant)
            d_ref[s, r] = (grad * s_ref[s, r]).astype(BF16)
        grad = d_ref[s]
        wide = grad.astype(F32)
        bias += fold(wide)
        above = pick(even, gp_ref[s, 0], gx_ref[s, 0])
        below = pick(even, gx_ref[s, 0], gp_ref[s, 0])
        body = x_ref[s].reshape(-1, c)
        rows = [
            jnp.concatenate([above, body[: (height - 1) * across]], 0),
            body,
            jnp.concatenate([body[across:], below], 0),
        ]
        weight_products(rows, grad.reshape(-1, c), turn(wide, across), acc_ref, s == 0)

    share = 1.0 / group
    small = [
        small_rows([bias.sum(0, keepdims=True), gain_sum * share, shift_sum * share], c),
        small_rows([b2_ref[0:1], c2_ref[2:3] * share, c2_ref[3:4] * share], c),
    ]

    def put(target, which):
        size = 9 * c // leads
        for j in range(leads):
            slot = j ^ place(which, leads)
            if which == 1:
                target[slot, :size] = w2_ref[j * size : (j + 1) * size]
            else:
                at = j * size
                while at < (j + 1) * size:
                    tap, low = at // c, at % c
                    step = min(c - low, (j + 1) * size - at)
                    a, b = tap // 3, tap % 3
                    target[slot, at - j * size : at - j * size + step] = acc_ref[
                        a * c + low : a * c + low + step, b * c : (b + 1) * c
                    ].astype(BF16)
                    at += step
            target[slot, size:] = small[which]

    @pl.when(core == 0)
    def _():
        put(keep_ref, 0)
        put(send_ref, 1)

    @pl.when(core != 0)
    def _():
        put(keep_ref, 1)
        put(send_ref, 0)


def edge_rows_kernel(d_ref, after_ref, dx_ref, dp_ref):
    samples, height = d_ref.shape[:2]
    even = lax.axis_index("lat") % 2 == 0
    for s in range(samples):
        dx_ref[s] = pick(even, d_ref[s, height - 1], d_ref[s, 0])
        dp_ref[s] = pick(even, d_ref[s, 0], d_ref[s, height - 1])


def input_grad_kernel(ep_ref, ex_ref, d_ref, u_ref, w_ref, o_ref, done_ref, k_ref):
    samples, height, across, c = u_ref.shape
    even = lax.axis_index("lat") % 2 == 0
    fill_toeplitz_transposed(w_ref, k_ref)
    for s in range(samples):

        def row(r):
            if r < 0:
                return pick(even, ep_ref[s], ex_ref[s])
            if r >= height:
                return pick(even, ex_ref[s], ep_ref[s])
            return d_ref[s, r]

        piece = convolve_rows(row, range(0, height, 2), k_ref, across, True)
        for r in range(height):
            o_ref[s, r] = (u_ref[s, r].astype(F32) + piece(r // 2, r % 2)).astype(BF16)
    done_ref[...] = jnp.zeros(done_ref.shape, F32)


def join_kernel(leads, *refs):
    out_ref = refs[-1]
    size = refs[0].shape[0] - SMALL
    for k in range(leads):
        out_ref[k * size : (k + 1) * size] = refs[k][:size]
    out_ref[leads * size :] = refs[0][size:]


def write_chunks(leads, which, ref, out_hbm, sum_ref, sems):
    size = out_hbm.shape[0] // leads
    copies = []
    for k in range(leads):
        at = pl.multiple_of((k ^ place(which, leads)) * size, 16)
        rows = slice(k * size, (k + 1) * size)
        sum_ref[rows] = ref[rows].astype(F32)
        copies.append(
            pltpu.make_async_copy(sum_ref.at[rows], out_hbm.at[pl.ds(at, size)], sems.at[k])
        )
        copies[-1].start()
    for copy in copies:
        copy.wait()


def leave_kernel(leads, grad_ref, own_ref, grad_hbm, first_hbm, second_hbm, sum_ref, sems):
    core = lax.axis_index("dp") % 2
    grad = pltpu.make_async_copy(grad_ref, grad_hbm, sems.at[leads])
    grad.start()

    @pl.when(core == 0)
    def _():
        write_chunks(leads, 0, own_ref, first_hbm, sum_ref, sems)

    @pl.when(core != 0)
    def _():
        write_chunks(leads, 1, own_ref, second_hbm, sum_ref, sems)

    grad.wait()


def finish_kernel(leads, own_ref, other_ref, first_in, second_in, first_hbm, second_hbm, *refs):
    small_hbm, (sum_ref, small_ref, sems) = refs[:6], refs[6:]
    core = lax.axis_index("dp") % 2
    small = [r[sum_ref.shape[0] :].astype(F32) for r in (own_ref, other_ref)]
    small = [v[:8] + v[8:] for v in small]
    for which in range(2):
        total = jnp.where(core == which, small[0], small[1])
        for i in range(3):
            small_ref[3 * which + i] = total[i : i + 1]
    copies = [
        pltpu.make_async_copy(small_ref.at[i], small_hbm[i], sems.at[leads + i]) for i in range(6)
    ]
    for copy in copies:
        copy.start()

    @pl.when(core != 0)
    def _():
        write_chunks(leads, 0, other_ref, first_hbm, sum_ref, sems)

    @pl.when(core == 0)
    def _():
        write_chunks(leads, 1, other_ref, second_hbm, sum_ref, sems)

    for copy in copies:
        copy.wait()


def add_kernel(parts, waits, *refs):
    outs = refs[parts + waits :]
    size = outs[0].shape[0] - SMALL
    for k, out in enumerate(outs):
        chunk = [r.at[k] if len(r.shape) == 3 else r for r in refs[:parts]]
        total = functools.reduce(lambda a, b: a + b, [r[...].astype(F32) for r in chunk])
        out[:size] = total[:size].astype(BF16)
        small = total[size : size + 8] + total[size + 8 :]
        high = small.astype(BF16)
        out[size:] = jnp.concatenate([high, (small - high.astype(F32)).astype(BF16)], 0)


def call(
    kernel, outs, scratch, operands, name, flops=0, waits=(), spaces=(VMEM, VMEM), aliases={}
):
    size = sum(o.size * o.dtype.itemsize for o in operands)
    ins, to = (s if isinstance(s, list) else None for s in spaces)
    return pl.pallas_call(
        kernel,
        out_shape=outs,
        in_specs=(ins or [spaces[0]] * len(operands)) + [ANY] * len(waits),
        out_specs=to or jax.tree.map(lambda _: spaces[1], outs),
        scratch_shapes=scratch,
        input_output_aliases=aliases,
        compiler_params=pltpu.CompilerParams(vmem_limit_bytes=16 * 2**20),
        cost_estimate=pl.CostEstimate(flops=flops, bytes_accessed=size, transcendentals=0),
        name=name,
    )(*operands, *waits)


def swap(value, axis, k):
    return lax.ppermute(value, axis, [(i, i ^ k) for i in range(lax.axis_size(axis))])


def cross(value, k, first):
    leads, dps, lats = (lax.axis_size(a) for a in ("lead", "dp", "lat"))
    pairs = []
    for lead in range(leads):
        for dp in range(dps):
            for lat in range(lats):
                by_lead = first if leads != lats else (dp % 2 == 0) == first
                to = (lead ^ k, dp, lat) if by_lead else (lead, dp, lat ^ k)
                pairs.append(tuple((l * dps + d) * lats + t for l, d, t in ((lead, dp, lat), to)))
    return lax.ppermute(value, ("lead", "dp", "lat"), pairs)


def place(which, leads):
    if which == 1 and leads == lax.axis_size("lat"):
        return lax.axis_index("lat")
    return lax.axis_index("lead")


def neighbours(value_x, value_p, axis):
    n = lax.axis_size(axis)
    first = [(i, i ^ 1) for i in range(n) if i ^ 1 < n]
    second = [(i, i + 1) for i in range(1, n - 1, 2)]
    second += [(j, i) for i, j in second]
    got_p = lax.ppermute(value_p, axis, second)
    return lax.ppermute(value_x, axis, first), got_p


def spread(stats):
    blocks, k = stats[None], 1
    while k < lax.axis_size("dp"):
        blocks = jnp.concatenate([blocks, swap(blocks, "dp", k)], 0)
        k *= 2
    return [blocks] + [swap(blocks, "lat", k) for k in range(1, lax.axis_size("lat"))]


def add_chunks(parts, name, outs=1, waits=(), flops=0):
    shape = jax.ShapeDtypeStruct(parts[0].shape[-2:], BF16)
    return call(
        functools.partial(add_kernel, len(parts), len(waits)),
        [shape] * outs,
        [],
        parts,
        name,
        flops,
        waits,
    )


def sum_everywhere(send, keep, edges, block_output, input_grad):
    leads, lats = lax.axis_size("lead"), lax.axis_size("lat")
    chunks = add_chunks([keep, swap(send, "dp", 1)], "add_dp", leads)
    got = [cross(chunks[k], k, True) for k in reversed(range(1, leads))]
    output = block_output(chunks[0])
    (mine,) = add_chunks([chunks[0]] + got, "add_first", waits=(output[1],))
    got = [cross(mine, k, False) for k in range(1, lats)]
    rows = edges(mine)
    (mine,) = add_chunks([mine] + got, "add_second", flops=HIDE)
    k = 2
    while k < lax.axis_size("dp"):
        (mine,) = add_chunks([mine, swap(mine, "dp", k)], "add_far_dp")
        k *= 2
    size, c = mine.shape[0] - SMALL, mine.shape[1]
    got = [cross(mine, k, True) for k in range(1, leads)]
    grad_input = input_grad(rows)
    own = call(
        functools.partial(join_kernel, leads),
        jax.ShapeDtypeStruct((leads * size + SMALL, c), BF16),
        [],
        (mine, *got),
        "join",
        waits=(grad_input[1],),
    )
    whole = jax.ShapeDtypeStruct((leads * size, c), F32)
    row = jax.ShapeDtypeStruct((1, c), F32)
    dma = pltpu.SemaphoreType.DMA
    total = pltpu.VMEM(whole.shape, F32)
    other = swap(own, "dp", 1)
    grad_input, first, second = call(
        functools.partial(leave_kernel, leads),
        [jax.ShapeDtypeStruct(grad_input[0].shape, BF16), whole, whole],
        [total, dma((leads + 1,))],
        (grad_input[0], own),
        "leave",
        spaces=(VMEM, ANY),
    )
    first, second, *rows = call(
        functools.partial(finish_kernel, leads),
        [whole, whole] + [row] * 6,
        [total, pltpu.VMEM((6, 1, c), F32), dma((leads + 6,))],
        (own, other, first, second),
        "finish",
        spaces=([VMEM, VMEM, ANY, ANY], [ANY] * 8),
        aliases={2: 0, 3: 1},
    )
    return (first, *rows[:3]), (second, *rows[3:]), output[0], grad_input


def shards(
    field,
    cotangent,
    land_sea,
    conv1_weight,
    conv1_bias,
    first_norm_scale,
    norm1_shift,
    conv2_weight,
    conv2_bias,
    second_norm_scale,
    norm2_shift,
):
    x, u, mask = field[0], cotangent[0], land_sea[0]
    samples, height, across, c = x.shape
    group = lax.axis_size("dp") * lax.axis_size("lat")
    leads = lax.axis_size("lead")
    slabs = -(-samples * height // 128)
    vec = lambda v: v.reshape(1, c)
    b1, g1, t1 = vec(conv1_bias), vec(first_norm_scale), vec(norm1_shift)
    b2, g2, t2 = vec(conv2_bias), vec(second_norm_scale), vec(norm2_shift)

    array = jax.ShapeDtypeStruct
    shape = lambda rows, dtype=F32: array((samples, rows, across, c), dtype)
    edge = array((samples, across, c), BF16)
    vector = array((8, c), F32)
    weights = array((3, 4 * c, 2 * c), BF16)
    turned = array((3, 2 * c, 4 * c), BF16)
    ext = lambda rows: pltpu.VMEM((2, rows, across, c), BF16)
    acc = pltpu.VMEM((3 * c, 3 * c), F32)
    conv_flops = 2 * 9 * c * c * samples * height * across

    near = call(
        near_rows_kernel,
        (shape(1, BF16), shape(1, BF16)),
        [pltpu.SemaphoreType.DMA((2,))],
        (x,),
        "near_rows",
        conv_flops,
        spaces=(ANY, ANY),
    )
    gx, gp = neighbours(*near, "lat")
    packed = array((3 * samples + slabs, across, c), BF16)
    far_x, far_p, bits = call(
        far_rows_kernel,
        (packed, packed, array((slabs, across, 128), F32)),
        [],
        (x, u, mask.reshape(samples * height, across)),
        "far_rows",
        conv_flops,
    )
    hx, hp = neighbours(far_x, far_p, "lat")
    wide_mask, count = call(masks_kernel, (shape(height), vector), [], (bits,), "masks", conv_flops)
    a1, z1, w1t, own1 = call(
        conv1_kernel,
        (shape(height), shape(height), weights, vector),
        [],
        (gp, gx, x, wide_mask, count, conv1_weight, b1),
        "conv1",
        16 * conv_flops,
    )
    mu, mu_sum, w2t, w2tt = call(
        prepare_kernel,
        (shape(height), vector, weights, turned),
        [],
        (u, wide_mask, conv2_weight),
        "prepare",
        conv_flops,
    )
    a1h, halo_mask, mu_halo = call(
        conv1_edge_kernel,
        (shape(4), shape(4), shape(2)),
        [],
        (hp, hx, gp, gx, x, own1, w1t, b1),
        "conv1_edges",
        conv_flops // 2,
    )
    st1 = spread(own1)
    n1, a2, z2, c1, own2 = call(
        functools.partial(conv2_kernel, len(st1)),
        (shape(height + 2, BF16), shape(height + 2), shape(height + 2), vector, vector),
        [ext(height + 4)],
        (own1, a1, a1h, wide_mask, halo_mask, mu, mu_sum, w2t, b2, g1, t1, *st1),
        "conv2",
        conv_flops,
    )
    st2 = spread(own2)
    s1, s2 = call(
        slopes_kernel,
        (shape(height), shape(height + 2)),
        [],
        (z1, z2, wide_mask, halo_mask),
        "slopes",
        conv_flops,
        waits=(st2[0],),
    )
    d2, dn1, c2, own3 = call(
        functools.partial(back2_kernel, len(st2)),
        (shape(height, BF16), shape(height), vector, vector),
        [ext(height + 2)],
        (own2, own1, c1, a2, s2, mu, mu_halo, wide_mask, a1, w2tt, g2, t2, *st2),
        "conv2_back",
        conv_flops,
    )
    st3 = spread(own3)
    w2, bias2 = call(
        weight2_kernel,
        (array((9 * c, c), BF16), vector),
        [acc],
        (n1, d2),
        "conv2_weight_grad",
        conv_flops,
        waits=(st3[0],),
    )
    chunks = array((leads, 9 * c // leads + SMALL, c), BF16)
    d1, send, keep = call(
        functools.partial(weight1_kernel, group, leads, len(st3)),
        (shape(height, BF16), chunks, chunks),
        [acc],
        (c1, c2, dn1, a1, s1, x, gx, gp, g1, w2, bias2, *st3),
        "conv1_weight_grad",
        conv_flops,
    )

    def edges(after):
        rows = call(edge_rows_kernel, (edge, edge), [], (d1,), "edge_rows", waits=(after,))
        return neighbours(*rows, "lat")[::-1]

    def input_grad(rows):
        return call(
            input_grad_kernel,
            (shape(height, BF16), vector),
            [pltpu.VMEM(turned.shape, BF16)],
            (*rows, d1, u, conv1_weight),
            "conv1_back",
            conv_flops,
        )

    def block_output(after):
        return call(
            output_kernel,
            (shape(height, BF16), vector),
            [pltpu.VMEM(x.shape, BF16), pltpu.SemaphoreType.DMA((samples,))],
            (x, a2, wide_mask, c2),
            "output",
            conv_flops // 2,
            waits=(after,),
            spaces=(VMEM, [ANY, VMEM]),
        )

    first, second, output, grad_input = sum_everywhere(
        send, keep, edges, block_output, input_grad
    )
    sums = []
    for part in (first, second):
        sums += [part[0].reshape(3, 3, c, c)] + [v.reshape(c) for v in part[1:]]
    return (output[None], grad_input[None], *sums)


def solution(mesh):
    tiles = P("lead", "dp", "lat", None, None)
    in_specs = (tiles, tiles, P("lead", "dp", "lat", None)) + (P(),) * 8
    out_specs = (tiles, tiles) + (P(),) * 8
    return jax.shard_map(shards, mesh=mesh, in_specs=in_specs, out_specs=out_specs, check_vma=False)
```

```python
import functools

import jax
import jax.numpy as jnp
from jax import lax
from jax.experimental import pallas as pl
from jax.experimental.pallas import tpu as pltpu
from jax.sharding import PartitionSpec as P

EPSILON = 1e-05
BF16 = jnp.bfloat16
F32 = jnp.float32
VMEM = pl.BlockSpec(memory_space=pltpu.VMEM)
ANY = pl.BlockSpec(memory_space=pl.ANY)
HIDE = 10**11
SMALL = 16


def fill_toeplitz(taps_ref, out_ref):
    c = taps_ref.shape[-1]
    zero = jnp.zeros((c, c), BF16)
    half = jnp.asarray(0.5, BF16)
    for b in range(3):
        for i in range(4):
            for j in range(2):
                block = taps_ref[i - j, b] * half if 0 <= i - j < 3 else zero
                out_ref[b, i * c : (i + 1) * c, j * c : (j + 1) * c] = block


def fill_toeplitz_transposed(taps_ref, out_ref):
    c = taps_ref.shape[-1]
    zero = jnp.zeros((c, c), BF16)
    for b in range(3):
        for i in range(4):
            for j in range(2):
                block = taps_ref[2 - (i - j), 2 - b] if 0 <= i - j < 3 else zero
                out_ref[b, j * c : (j + 1) * c, i * c : (i + 1) * c] = block


def convolve_rows(row, starts, weights_ref, across, transposed):
    left = jnp.concatenate(
        [jnp.concatenate([row(r - 1 + i) for r in starts], 0) for i in range(4)], 1
    )
    c = left.shape[1] // 4
    dims = (((1,), (1 if transposed else 0,)), ((), ()))
    taps = [
        lax.dot_general(left, weights_ref[b], dims, preferred_element_type=F32)
        for b in range(3)
    ]

    def piece(pair, j):
        part = [t[pair * across : (pair + 1) * across, j * c : (j + 1) * c] for t in taps]
        return pltpu.roll(part[0], 1, 0) + part[1] + pltpu.roll(part[2], across - 1, 0)

    return piece


def silu(half):
    return half + half * jnp.tanh(half)


def silu_slope(half):
    t = jnp.tanh(half)
    return (0.5 + 0.5 * t) * (1.0 + half * (1.0 - t))


def fold(value):
    return value.reshape(-1, 8, value.shape[-1]).sum(0)


def join(stats, count, at, sums):
    centres = stats[:, at + 2 : at + 3]
    mean = (stats[:, at : at + 1] + sums * centres).sum(0) / count
    away = centres - mean
    squares = stats[:, at + 1 : at + 2] + away * (2.0 * stats[:, at : at + 1] + sums * away)
    variance = jnp.maximum(squares.sum(0) / count, 0.0)
    return mean, lax.rsqrt(variance + EPSILON)


def has_pair():
    count, me = lax.axis_size("lat"), lax.axis_index("lat")
    inside = jnp.logical_and(me != 0, me != count - 1)
    return (me == me, inside) if count % 2 == 0 else (me != count - 1, me != 0)


def pick(even, when_even, when_odd):
    return jnp.where(even, when_even, when_odd)


def column_mask(bits, k, c):
    tile = bits[k // 128]
    return jnp.broadcast_to(tile[:, k % 128 : k % 128 + 1].astype(F32), (tile.shape[0], c))


def near_rows_kernel(top_ref, bottom_ref, gx_ref, gp_ref):
    even = lax.axis_index("lat") % 2 == 0
    top, bottom = top_ref[...], bottom_ref[...]
    paired_x, paired_p = has_pair()
    gx_ref[...] = pick(paired_x, pick(even, bottom, top), jnp.zeros_like(top))
    gp_ref[...] = pick(paired_p, pick(even, top, bottom), jnp.zeros_like(top))


def far_rows_kernel(x_ref, u_ref, mask_ref, hx_ref, hp_ref, bits_ref):
    samples, height, across, c = x_ref.shape
    even = lax.axis_index("lat") % 2 == 0
    for k in range(bits_ref.shape[0]):
        bits = mask_ref[k * 128 : (k + 1) * 128].astype(F32)
        bits = jnp.concatenate([bits, jnp.zeros((bits.shape[0], 128 - across), F32)], 1)
        if bits.shape[0] < 128:
            bits = jnp.concatenate([bits, jnp.zeros((128 - bits.shape[0], 128), F32)], 0)
        bits_ref[k] = bits.T[:across]
    zero = jnp.zeros((across, c), BF16)
    for out, down, paired in zip((hx_ref, hp_ref), (even, jnp.logical_not(even)), has_pair()):
        first = jnp.where(down, height - 3, 1)
        edge = jnp.where(down, height - 1, 0)
        for s in range(samples):
            out[2 * s] = pick(paired, x_ref[s, first], zero)
            out[2 * s + 1] = pick(paired, x_ref[s, first + 1], zero)
            out[2 * samples + s] = pick(paired, u_ref[s, edge], zero)
        for k in range(bits_ref.shape[0]):
            bits = bits_ref[k]
            out[3 * samples + k] = pick(paired, bits, jnp.zeros_like(bits)).astype(BF16)


def masks_kernel(bits_ref, m_ref, count_ref):
    samples, height, across, c = m_ref.shape
    count = jnp.zeros((8, c), F32)
    for s in range(samples):
        for r in range(height):
            mask = column_mask(bits_ref, s * height + r, c)
            m_ref[s, r] = mask
            count += fold(mask)
    count_ref[...] = stats_block([count.sum(0, keepdims=True)], c)


def stats_block(rows, c):
    return jnp.concatenate(rows + [jnp.zeros((8 - len(rows), c), F32)], 0)


def gather(refs):
    return jnp.concatenate([r[...] for r in refs], 0)


def middle(value):
    return value.mean(0, keepdims=True)


def add_moments(sums, active, mask):
    masked = active * mask
    sums[0] += fold(masked)
    sums[1] += fold(masked * active)
    return masked


def own_row(inner_ref, outer_ref, s, r, height):
    if 2 <= r < height - 2:
        return inner_ref[s, r - 2]
    return outer_ref[s, r if r < 2 else r - height + 4]


def conv1_inner_kernel(x_ref, m_ref, w_ref, b_ref, a_ref, z_ref, t_ref, part_ref):
    samples, height, across, c = x_ref.shape
    fill_toeplitz(w_ref, t_ref)
    bias = 0.5 * b_ref[...]
    sums = [jnp.zeros((8, c), F32) for _ in range(2)]
    centre = None
    for s in range(samples):
        piece = convolve_rows(lambda r: x_ref[s, r], range(2, height - 2, 2), t_ref, across, False)
        for i in range(height - 4):
            half = piece(i // 2, i % 2) + bias
            active = silu(half)
            if centre is None:
                centre = middle(active)
            active = active - centre
            a_ref[s, i] = active
            z_ref[s, i] = half
            add_moments(sums, active, m_ref[s, i + 2])
    rows = [v.sum(0, keepdims=True) for v in sums]
    part_ref[...] = stats_block([rows[0], rows[1], centre], c)


def conv1_outer_kernel(
    gp_ref, gx_ref, x_ref, m_ref, count_ref, t_ref, b_ref, part_ref, a_ref, z_ref, st_ref
):
    samples, height, across, c = x_ref.shape
    even = lax.axis_index("lat") % 2 == 0
    bias = 0.5 * b_ref[...]
    centre = part_ref[2:3]

    def row(r):
        if r < 0:
            parts = [pick(even, gp_ref[s, 0], gx_ref[s, 0]) for s in range(samples)]
        elif r >= height:
            parts = [pick(even, gx_ref[s, 0], gp_ref[s, 0]) for s in range(samples)]
        else:
            parts = [x_ref[s, r] for s in range(samples)]
        return jnp.concatenate(parts, 0)

    sums = [jnp.zeros((8, c), F32) for _ in range(2)]
    for slot, start in ((0, 0), (2, height - 2)):
        piece = convolve_rows(row, (start,), t_ref, across, False)
        for s in range(samples):
            for j in range(2):
                half = piece(s, j) + bias
                active = silu(half) - centre
                a_ref[s, slot + j] = active
                z_ref[s, slot + j] = half
                add_moments(sums, active, m_ref[s, start + j])
    rows = [part_ref[i : i + 1] + v.sum(0, keepdims=True) for i, v in enumerate(sums)]
    st_ref[...] = stats_block([rows[0], rows[1], centre, count_ref[0:1]], c)


def prepare_kernel(u_ref, m_ref, w2_ref, mu_ref, su_ref, t2_ref, tt2_ref):
    samples, height, across, c = u_ref.shape
    fill_toeplitz(w2_ref, t2_ref)
    fill_toeplitz_transposed(w2_ref, tt2_ref)
    total = jnp.zeros((8, c), F32)
    for s in range(samples):
        for r in range(height):
            value = u_ref[s, r].astype(F32) * m_ref[s, r]
            mu_ref[s, r] = value
            total += fold(value)
    su_ref[...] = stats_block([total.sum(0, keepdims=True)], c)


def conv1_edge_kernel(
    hp_ref, hx_ref, gp_ref, gx_ref, x_ref, st_ref, t_ref, b_ref, a_ref, mh_ref, muh_ref
):
    samples, height, across, c = x_ref.shape
    even = lax.axis_index("lat") % 2 == 0
    bias = 0.5 * b_ref[...]
    centre = st_ref[2:3]

    def row(r):
        parts = []
        for s in range(samples):
            if r < -1:
                parts.append(pick(even, hp_ref[2 * s + r + 3], hx_ref[2 * s + r + 3]))
            elif r == -1:
                parts.append(pick(even, gp_ref[s, 0], gx_ref[s, 0]))
            elif r < height:
                parts.append(x_ref[s, r])
            elif r == height:
                parts.append(pick(even, gx_ref[s, 0], gp_ref[s, 0]))
            else:
                j = r - height - 1
                parts.append(pick(even, hx_ref[2 * s + j], hp_ref[2 * s + j]))
        return jnp.concatenate(parts, 0)

    slabs = slice(3 * samples, hx_ref.shape[0])
    above = pick(even, hp_ref[slabs], hx_ref[slabs])
    below = pick(even, hx_ref[slabs], hp_ref[slabs])
    for slot, start in ((0, -2), (2, height)):
        piece = convolve_rows(row, (start,), t_ref, across, False)
        for s in range(samples):
            for j in range(2):
                a_ref[s, slot + j] = silu(piece(s, j) + bias) - centre
                if start < 0:
                    mask = column_mask(above, s * height + height - 2 + j, c)
                else:
                    mask = column_mask(below, s * height + j, c)
                mh_ref[s, slot + j] = mask
    for s in range(samples):
        up = pick(even, hp_ref[2 * samples + s], hx_ref[2 * samples + s])
        muh_ref[s, 0] = up.astype(F32) * mh_ref[s, 1]
        down = pick(even, hx_ref[2 * samples + s], hp_ref[2 * samples + s])
        muh_ref[s, 1] = down.astype(F32) * mh_ref[s, 2]


def conv2_kernel(
    pieces,
    own_ref, a_ref, ao_ref, ah_ref, m_ref, mh_ref, mu_ref, su_ref, k_ref, b_ref, g_ref, t_ref, *refs,
):
    stats, (n_ref, a2_ref, z2_ref, c1_ref, st2_ref, ext_ref) = gather(refs[:pieces]), refs[pieces:]
    samples, height, across, c = m_ref.shape
    counts = stats[:, 3:4]
    count = counts.sum(0)
    mean, inverse = join(stats, count, 0, counts)
    offset = mean - own_ref[2:3]
    scale = inverse * g_ref[...]
    shift = t_ref[...] - offset * scale
    c1_ref[...] = stats_block([offset, inverse, count, mean], c)
    bias = 0.5 * b_ref[...]
    sums = [jnp.zeros((8, c), F32) for _ in range(3)]
    centre = None
    for s in range(samples):
        ext = ext_ref.at[s % 2]
        for i in range(height + 4):
            r = i - 2
            if 0 <= r < height:
                value, mask = own_row(a_ref, ao_ref, s, r, height), m_ref[s, r]
            else:
                j = i if r < 0 else r - height + 2
                value, mask = ah_ref[s, j], mh_ref[s, j]
            ext[i] = ((value * scale + shift) * mask).astype(BF16)
            if 1 <= i < height + 3:
                n_ref[s, i - 1] = ext[i]

        piece = convolve_rows(
            lambda r: ext[r + 2], range(-1, height + 1, 2), k_ref, across, False
        )
        for i in range(height + 2):
            r = i - 1
            half = piece(i // 2, i % 2) + bias
            active = silu(half)
            if centre is None:
                centre = middle(active)
            active = active - centre
            if 0 <= r < height:
                add_moments(sums, active, m_ref[s, r])
                sums[2] += fold(active * mu_ref[s, r])
            a2_ref[s, i] = active
            z2_ref[s, i] = half
    rows = [v.sum(0, keepdims=True) for v in sums]
    st2_ref[...] = stats_block(
        [rows[0], rows[1], centre, rows[2], su_ref[0:1], own_ref[3:4]], c
    )


def slopes_kernel(z_ref, zo_ref, z2_ref, m_ref, mh_ref, after_ref, s_ref, s2_ref):
    samples, height = m_ref.shape[:2]
    for s in range(samples):
        for r in range(-1, height + 1):
            mask = mh_ref[s, 1 if r < 0 else 2]
            if 0 <= r < height:
                mask = m_ref[s, r]
                s_ref[s, r] = silu_slope(own_row(z_ref, zo_ref, s, r, height)) * mask
            s2_ref[s, r + 1] = silu_slope(z2_ref[s, r + 1]) * mask


def back_terms(scale, inverse, offset, gain_sum, shift_sum, count):
    by_active = -scale * gain_sum * inverse / count
    constant = -scale * (shift_sum - offset * inverse * gain_sum) / count
    return by_active, constant


def back2_kernel(
    pieces,
    own_ref, st1_ref, c1_ref, a2_ref, s2_ref, mu_ref, muh_ref, m_ref, a_ref, ao_ref, k_ref, g_ref, t_ref, *refs,
):
    stats, (d_ref, dn_ref, c2_ref, st3_ref, ext_ref) = gather(refs[:pieces]), refs[pieces:]
    samples, height, across, c = m_ref.shape
    count = c1_ref[2:3]
    mean, inverse = join(stats, count, 0, stats[:, 5:6])
    offset = mean - own_ref[2:3]
    shift_sum = stats[:, 4:5].sum(0)
    away = stats[:, 2:3] - mean
    gain_sum = inverse * (stats[:, 3:4] + away * stats[:, 4:5]).sum(0)
    scale = inverse * g_ref[...]
    by_active, constant = back_terms(scale, inverse, offset, gain_sum, shift_sum, count)
    c2_ref[...] = stats_block([scale, t_ref[...] - offset * scale, gain_sum, shift_sum], c)
    sums = [jnp.zeros((8, c), F32) for _ in range(2)]
    for s in range(samples):
        ext = ext_ref.at[s % 2]
        for i in range(height + 2):
            upstream = mu_ref[s, i - 1] if 0 < i <= height else muh_ref[s, 0 if i == 0 else 1]
            grad = upstream * scale + (a2_ref[s, i] * by_active + constant)
            ext[i] = (grad * s2_ref[s, i]).astype(BF16)
            if 0 < i <= height:
                d_ref[s, i - 1] = ext[i]
        piece = convolve_rows(
            lambda r: ext[r + 1], range(0, height, 2), k_ref, across, True
        )
        for r in range(height):
            part = piece(r // 2, r % 2)
            dn_ref[s, r] = part
            masked = part * m_ref[s, r]
            sums[0] += fold(masked)
            sums[1] += fold(masked * own_row(a_ref, ao_ref, s, r, height))
    rows = [v.sum(0, keepdims=True) for v in sums]
    st3_ref[...] = stats_block([rows[0], rows[1], st1_ref[2:3]], c)


def weight_products(rows, centre, turned, total_ref, first):
    windows = jnp.concatenate(rows, 1)
    product = lax.dot_general(
        windows,
        jnp.concatenate([turned[0], centre, turned[1]], 1),
        (((0,), (0,)), ((), ())),
        preferred_element_type=F32,
    )
    if first:
        total_ref[...] = product
    else:
        total_ref[...] += product


def turn(value, across):
    c = value.shape[-1]
    return [
        pltpu.roll(value, k, 1).astype(BF16).reshape(-1, c) for k in (across - 1, 1)
    ]


def weight2_kernel(n_ref, d_ref, after_ref, w_ref, b_ref, acc_ref):
    samples, height, across, c = d_ref.shape
    bias = jnp.zeros((8, c), F32)
    for s in range(samples):
        grad = d_ref[s]
        wide = grad.astype(F32)
        bias += fold(wide)
        rows = [n_ref[s, a : a + height].reshape(-1, c) for a in range(3)]
        weight_products(rows, grad.reshape(-1, c), turn(wide, across), acc_ref, s == 0)
    b_ref[...] = jnp.broadcast_to(bias.sum(0, keepdims=True), b_ref.shape)
    for a in range(3):
        for b in range(3):
            at = (a * 3 + b) * c
            w_ref[at : at + c] = acc_ref[a * c : (a + 1) * c, b * c : (b + 1) * c].astype(BF16)


def output_kernel(x_ref, a2_ref, m_ref, c2_ref, after_ref, o_hbm, done_ref, o_ref, sems):
    samples, height, across, c = x_ref.shape
    scale, shift = c2_ref[0:1], c2_ref[1:2]
    for s in range(samples):
        for r in range(height):
            normed = (a2_ref[s, r + 1] * scale + shift) * m_ref[s, r]
            o_ref[s, r] = (x_ref[s, r].astype(F32) + normed).astype(BF16)
        pltpu.make_async_copy(o_ref.at[s], o_hbm.at[s], sems.at[s]).start()
    done_ref[...] = jnp.zeros(done_ref.shape, F32)
    for s in range(samples):
        pltpu.make_async_copy(o_ref.at[s], o_hbm.at[s], sems.at[s]).wait()


def small_rows(rows, c):
    high = jnp.concatenate(rows + [jnp.zeros((8 - len(rows), c), F32)], 0)
    first = high.astype(BF16)
    return jnp.concatenate([first, (high - first.astype(F32)).astype(BF16)], 0)


def weight1_kernel(
    group, leads, pieces,
    c1_ref, c2_ref, dn_ref, a_ref, ao_ref, s_ref, x_ref, gx_ref, gp_ref, g_ref, w2_ref, b2_ref, *refs,
):
    stats = gather(refs[:pieces])
    d_ref, send_ref, keep_ref, acc_ref = refs[pieces:]
    samples, height, across, c = x_ref.shape
    even = lax.axis_index("lat") % 2 == 0
    core = lax.axis_index("dp") % 2
    offset, inverse, count, mean = (c1_ref[i : i + 1] for i in range(4))
    shift_sum = stats[:, 0:1].sum(0)
    away = stats[:, 2:3] - mean
    gain_sum = inverse * (stats[:, 1:2] + away * stats[:, 0:1]).sum(0)
    scale = inverse * g_ref[...]
    by_active, constant = back_terms(scale, inverse, offset, gain_sum, shift_sum, count)
    bias = jnp.zeros((8, c), F32)
    for s in range(samples):
        for r in range(height):
            active = own_row(a_ref, ao_ref, s, r, height)
            grad = dn_ref[s, r] * scale + (active * by_active + constant)
            d_ref[s, r] = (grad * s_ref[s, r]).astype(BF16)
        grad = d_ref[s]
        wide = grad.astype(F32)
        bias += fold(wide)
        above = pick(even, gp_ref[s, 0], gx_ref[s, 0])
        below = pick(even, gx_ref[s, 0], gp_ref[s, 0])
        body = x_ref[s].reshape(-1, c)
        rows = [
            jnp.concatenate([above, body[: (height - 1) * across]], 0),
            body,
            jnp.concatenate([body[across:], below], 0),
        ]
        weight_products(rows, grad.reshape(-1, c), turn(wide, across), acc_ref, s == 0)

    share = 1.0 / group
    small = [
        small_rows([bias.sum(0, keepdims=True), gain_sum * share, shift_sum * share], c),
        small_rows([b2_ref[0:1], c2_ref[2:3] * share, c2_ref[3:4] * share], c),
    ]

    def put(target, which):
        size = 9 * c // leads
        for j in range(leads):
            slot = j ^ place(which, leads)
            if which == 1:
                target[slot, :size] = w2_ref[j * size : (j + 1) * size]
            else:
                at = j * size
                while at < (j + 1) * size:
                    tap, low = at // c, at % c
                    step = min(c - low, (j + 1) * size - at)
                    a, b = tap // 3, tap % 3
                    target[slot, at - j * size : at - j * size + step] = acc_ref[
                        a * c + low : a * c + low + step, b * c : (b + 1) * c
                    ].astype(BF16)
                    at += step
            target[slot, size:] = small[which]

    @pl.when(core == 0)
    def _():
        put(keep_ref, 0)
        put(send_ref, 1)

    @pl.when(core != 0)
    def _():
        put(keep_ref, 1)
        put(send_ref, 0)


def edge_rows_kernel(d_ref, after_ref, dx_ref, dp_ref):
    samples, height = d_ref.shape[:2]
    even = lax.axis_index("lat") % 2 == 0
    paired_x, paired_p = has_pair()
    for s in range(samples):
        top, bottom = d_ref[s, 0], d_ref[s, height - 1]
        dx_ref[s] = pick(paired_x, pick(even, bottom, top), jnp.zeros_like(top))
        dp_ref[s] = pick(paired_p, pick(even, top, bottom), jnp.zeros_like(top))


def input_grad_kernel(ep_ref, ex_ref, d_ref, u_ref, w_ref, o_ref, done_ref, k_ref):
    samples, height, across, c = u_ref.shape
    even = lax.axis_index("lat") % 2 == 0
    fill_toeplitz_transposed(w_ref, k_ref)
    for s in range(samples):

        def row(r):
            if r < 0:
                return pick(even, ep_ref[s], ex_ref[s])
            if r >= height:
                return pick(even, ex_ref[s], ep_ref[s])
            return d_ref[s, r]

        piece = convolve_rows(row, range(0, height, 2), k_ref, across, True)
        for r in range(height):
            o_ref[s, r] = (u_ref[s, r].astype(F32) + piece(r // 2, r % 2)).astype(BF16)
    done_ref[...] = jnp.zeros(done_ref.shape, F32)


def join_kernel(leads, *refs):
    out_ref = refs[-1]
    size = refs[0].shape[0] - SMALL
    for k in range(leads):
        out_ref[k * size : (k + 1) * size] = refs[k][:size]
    out_ref[leads * size :] = refs[0][size:]


def write_chunks(leads, which, ref, out_hbm, sum_ref, sems):
    size = out_hbm.shape[0] // leads
    copies = []
    for k in range(leads):
        at = pl.multiple_of((k ^ place(which, leads)) * size, 16)
        rows = slice(k * size, (k + 1) * size)
        sum_ref[rows] = ref[rows].astype(F32)
        copies.append(
            pltpu.make_async_copy(sum_ref.at[rows], out_hbm.at[pl.ds(at, size)], sems.at[k])
        )
        copies[-1].start()
    for copy in copies:
        copy.wait()


def leave_kernel(leads, grad_ref, own_ref, grad_hbm, first_hbm, second_hbm, sum_ref, sems):
    core = lax.axis_index("dp") % 2
    grad = pltpu.make_async_copy(grad_ref, grad_hbm, sems.at[leads])
    grad.start()

    @pl.when(core == 0)
    def _():
        write_chunks(leads, 0, own_ref, first_hbm, sum_ref, sems)

    @pl.when(core != 0)
    def _():
        write_chunks(leads, 1, own_ref, second_hbm, sum_ref, sems)

    grad.wait()


def finish_kernel(leads, own_ref, other_ref, first_in, second_in, first_hbm, second_hbm, *refs):
    small_hbm, (sum_ref, small_ref, sems) = refs[:6], refs[6:]
    core = lax.axis_index("dp") % 2
    small = [r[sum_ref.shape[0] :].astype(F32) for r in (own_ref, other_ref)]
    small = [v[:8] + v[8:] for v in small]
    for which in range(2):
        total = jnp.where(core == which, small[0], small[1])
        for i in range(3):
            small_ref[3 * which + i] = total[i : i + 1]
    copies = [
        pltpu.make_async_copy(small_ref.at[i], small_hbm[i], sems.at[leads + i]) for i in range(6)
    ]
    for copy in copies:
        copy.start()

    @pl.when(core != 0)
    def _():
        write_chunks(leads, 0, other_ref, first_hbm, sum_ref, sems)

    @pl.when(core == 0)
    def _():
        write_chunks(leads, 1, other_ref, second_hbm, sum_ref, sems)

    for copy in copies:
        copy.wait()


def add_kernel(parts, waits, *refs):
    outs = refs[parts + waits :]
    size = outs[0].shape[0] - SMALL
    for k, out in enumerate(outs):
        chunk = [r.at[k] if len(r.shape) == 3 else r for r in refs[:parts]]
        total = functools.reduce(lambda a, b: a + b, [r[...].astype(F32) for r in chunk])
        out[:size] = total[:size].astype(BF16)
        small = total[size : size + 8] + total[size + 8 :]
        high = small.astype(BF16)
        out[size:] = jnp.concatenate([high, (small - high.astype(F32)).astype(BF16)], 0)


def call(
    kernel, outs, scratch, operands, name, flops=0, waits=(), spaces=(VMEM, VMEM), aliases={}
):
    size = sum(o.size * o.dtype.itemsize for o in operands)
    ins, to = (s if isinstance(s, list) else None for s in spaces)
    return pl.pallas_call(
        kernel,
        out_shape=outs,
        in_specs=(ins or [spaces[0]] * len(operands)) + [ANY] * len(waits),
        out_specs=to or jax.tree.map(lambda _: spaces[1], outs),
        scratch_shapes=scratch,
        input_output_aliases=aliases,
        compiler_params=pltpu.CompilerParams(vmem_limit_bytes=16 * 2**20),
        cost_estimate=pl.CostEstimate(flops=flops, bytes_accessed=size, transcendentals=0),
        name=name,
    )(*operands, *waits)


def swap(value, axis, k):
    return lax.ppermute(value, axis, [(i, i ^ k) for i in range(lax.axis_size(axis))])


def cross(value, k, first):
    leads, dps, lats = (lax.axis_size(a) for a in ("lead", "dp", "lat"))
    pairs = []
    for lead in range(leads):
        for dp in range(dps):
            for lat in range(lats):
                by_lead = first if leads != lats else (dp % 2 == 0) == first
                to = (lead ^ k, dp, lat) if by_lead else (lead, dp, lat ^ k)
                pairs.append(tuple((l * dps + d) * lats + t for l, d, t in ((lead, dp, lat), to)))
    return lax.ppermute(value, ("lead", "dp", "lat"), pairs)


def place(which, leads):
    if which == 1 and leads == lax.axis_size("lat"):
        return lax.axis_index("lat")
    return lax.axis_index("lead")


def over_dp_and_lat(value, to):
    dps, lats = lax.axis_size("dp"), lax.axis_size("lat")
    pairs = []
    for dp in range(dps):
        for lat in range(lats):
            to_dp, to_lat = to(dp, lat)
            pairs.append((dp * lats + lat, to_dp * lats + to_lat))
    return lax.ppermute(value, ("dp", "lat"), pairs)


def neighbours(value_x, value_p):
    lats = lax.axis_size("lat")

    def exchange(value, offset):
        def to(dp, lat):
            other = ((lat - offset) ^ 1) + offset if lat >= offset else lats
            return (dp, other) if other < lats else (dp ^ 1, lat)

        return over_dp_and_lat(value, to)

    got_p = exchange(value_p, 1)
    return exchange(value_x, 0), got_p


def spread(stats):
    blocks, k = stats[None], 1
    while k < lax.axis_size("dp"):
        blocks = jnp.concatenate([blocks, swap(blocks, "dp", k)], 0)
        k *= 2
    return [blocks] + [
        over_dp_and_lat(blocks, lambda dp, lat, k=k: (dp ^ 1, lat ^ k))
        for k in range(1, lax.axis_size("lat"))
    ]


def add_chunks(parts, name, outs=1, waits=(), flops=0):
    shape = jax.ShapeDtypeStruct(parts[0].shape[-2:], BF16)
    return call(
        functools.partial(add_kernel, len(parts), len(waits)),
        [shape] * outs,
        [],
        parts,
        name,
        flops,
        waits,
    )


def sum_everywhere(send, keep, edges, block_output, input_grad):
    leads, lats = lax.axis_size("lead"), lax.axis_size("lat")
    chunks = add_chunks([keep, swap(send, "dp", 1)], "add_dp", leads)
    got = [cross(chunks[k], k, True) for k in reversed(range(1, leads))]
    output = block_output(chunks[0])
    (mine,) = add_chunks([chunks[0]] + got, "add_first", waits=(output[1],))
    got = [cross(mine, k, False) for k in range(1, lats)]
    rows = edges(mine)
    (mine,) = add_chunks([mine] + got, "add_second", flops=HIDE)
    k = 2
    while k < lax.axis_size("dp"):
        (mine,) = add_chunks([mine, swap(mine, "dp", k)], "add_far_dp")
        k *= 2
    size, c = mine.shape[0] - SMALL, mine.shape[1]
    got = [cross(mine, k, True) for k in range(1, leads)]
    grad_input = input_grad(rows)
    own = call(
        functools.partial(join_kernel, leads),
        jax.ShapeDtypeStruct((leads * size + SMALL, c), BF16),
        [],
        (mine, *got),
        "join",
        waits=(grad_input[1],),
    )
    whole = jax.ShapeDtypeStruct((leads * size, c), F32)
    row = jax.ShapeDtypeStruct((1, c), F32)
    dma = pltpu.SemaphoreType.DMA
    total = pltpu.VMEM(whole.shape, F32)
    other = swap(own, "dp", 1)
    grad_input, first, second = call(
        functools.partial(leave_kernel, leads),
        [jax.ShapeDtypeStruct(grad_input[0].shape, BF16), whole, whole],
        [total, dma((leads + 1,))],
        (grad_input[0], own),
        "leave",
        spaces=(VMEM, ANY),
    )
    first, second, *rows = call(
        functools.partial(finish_kernel, leads),
        [whole, whole] + [row] * 6,
        [total, pltpu.VMEM((6, 1, c), F32), dma((leads + 6,))],
        (own, other, first, second),
        "finish",
        spaces=([VMEM, VMEM, ANY, ANY], [ANY] * 8),
        aliases={2: 0, 3: 1},
    )
    return (first, *rows[:3]), (second, *rows[3:]), output[0], grad_input


def shards(
    field,
    cotangent,
    land_sea,
    conv1_weight,
    conv1_bias,
    first_norm_scale,
    norm1_shift,
    conv2_weight,
    conv2_bias,
    second_norm_scale,
    norm2_shift,
):
    x, u, mask = field[0], cotangent[0], land_sea[0]
    samples, height, across, c = x.shape
    group = lax.axis_size("dp") * lax.axis_size("lat")
    leads = lax.axis_size("lead")
    slabs = -(-samples * height // 128)
    vec = lambda v: v.reshape(1, c)
    b1, g1, t1 = vec(conv1_bias), vec(first_norm_scale), vec(norm1_shift)
    b2, g2, t2 = vec(conv2_bias), vec(second_norm_scale), vec(norm2_shift)

    array = jax.ShapeDtypeStruct
    shape = lambda rows, dtype=F32: array((samples, rows, across, c), dtype)
    edge = array((samples, across, c), BF16)
    vector = array((8, c), F32)
    weights = array((3, 4 * c, 2 * c), BF16)
    turned = array((3, 2 * c, 4 * c), BF16)
    ext = lambda rows: pltpu.VMEM((2, rows, across, c), BF16)
    acc = pltpu.VMEM((3 * c, 3 * c), F32)
    conv_flops = 2 * 9 * c * c * samples * height * across

    near = call(
        near_rows_kernel,
        (shape(1, BF16), shape(1, BF16)),
        [],
        (x[:, :1], x[:, height - 1 :]),
        "near_rows",
        conv_flops,
    )
    gx, gp = neighbours(*near)
    packed = array((3 * samples + slabs, across, c), BF16)
    far_x, far_p, bits = call(
        far_rows_kernel,
        (packed, packed, array((slabs, across, 128), F32)),
        [],
        (x, u, mask.reshape(samples * height, across)),
        "far_rows",
        conv_flops,
    )
    hx, hp = neighbours(far_x, far_p)
    wide_mask, count = call(masks_kernel, (shape(height), vector), [], (bits,), "masks", conv_flops)
    a1, z1, w1t, part = call(
        conv1_inner_kernel,
        (shape(height - 4), shape(height - 4), weights, vector),
        [],
        (x, wide_mask, conv1_weight, b1),
        "conv1_inner",
        4 * conv_flops,
    )
    a1o, z1o, own1 = call(
        conv1_outer_kernel,
        (shape(4), shape(4), vector),
        [],
        (gp, gx, x, wide_mask, count, w1t, b1, part),
        "conv1_outer",
        16 * conv_flops,
    )
    mu, mu_sum, w2t, w2tt = call(
        prepare_kernel,
        (shape(height), vector, weights, turned),
        [],
        (u, wide_mask, conv2_weight),
        "prepare",
        conv_flops,
    )
    a1h, halo_mask, mu_halo = call(
        conv1_edge_kernel,
        (shape(4), shape(4), shape(2)),
        [],
        (hp, hx, gp, gx, x, own1, w1t, b1),
        "conv1_edges",
        conv_flops // 2,
    )
    st1 = spread(own1)
    n1, a2, z2, c1, own2 = call(
        functools.partial(conv2_kernel, len(st1)),
        (shape(height + 2, BF16), shape(height + 2), shape(height + 2), vector, vector),
        [ext(height + 4)],
        (own1, a1, a1o, a1h, wide_mask, halo_mask, mu, mu_sum, w2t, b2, g1, t1, *st1),
        "conv2",
        conv_flops,
    )
    st2 = spread(own2)
    s1, s2 = call(
        slopes_kernel,
        (shape(height), shape(height + 2)),
        [],
        (z1, z1o, z2, wide_mask, halo_mask),
        "slopes",
        conv_flops,
        waits=(st2[0],),
    )
    d2, dn1, c2, own3 = call(
        functools.partial(back2_kernel, len(st2)),
        (shape(height, BF16), shape(height), vector, vector),
        [ext(height + 2)],
        (own2, own1, c1, a2, s2, mu, mu_halo, wide_mask, a1, a1o, w2tt, g2, t2, *st2),
        "conv2_back",
        conv_flops,
    )
    st3 = spread(own3)
    w2, bias2 = call(
        weight2_kernel,
        (array((9 * c, c), BF16), vector),
        [acc],
        (n1, d2),
        "conv2_weight_grad",
        conv_flops,
        waits=(st3[0],),
    )
    chunks = array((leads, 9 * c // leads + SMALL, c), BF16)
    d1, send, keep = call(
        functools.partial(weight1_kernel, group, leads, len(st3)),
        (shape(height, BF16), chunks, chunks),
        [acc],
        (c1, c2, dn1, a1, a1o, s1, x, gx, gp, g1, w2, bias2, *st3),
        "conv1_weight_grad",
        conv_flops,
    )

    def edges(after):
        rows = call(edge_rows_kernel, (edge, edge), [], (d1,), "edge_rows", waits=(after,))
        return neighbours(*rows)[::-1]

    def input_grad(rows):
        return call(
            input_grad_kernel,
            (shape(height, BF16), vector),
            [pltpu.VMEM(turned.shape, BF16)],
            (*rows, d1, u, conv1_weight),
            "conv1_back",
            conv_flops,
        )

    def block_output(after):
        return call(
            output_kernel,
            (shape(height, BF16), vector),
            [pltpu.VMEM(x.shape, BF16), pltpu.SemaphoreType.DMA((samples,))],
            (x, a2, wide_mask, c2),
            "output",
            conv_flops // 2,
            waits=(after,),
            spaces=(VMEM, [ANY, VMEM]),
        )

    first, second, output, grad_input = sum_everywhere(
        send, keep, edges, block_output, input_grad
    )
    sums = []
    for part in (first, second):
        sums += [part[0].reshape(3, 3, c, c)] + [v.reshape(c) for v in part[1:]]
    return (output[None], grad_input[None], *sums)


def solution(mesh):
    tiles = P("lead", "dp", "lat", None, None)
    in_specs = (tiles, tiles, P("lead", "dp", "lat", None)) + (P(),) * 8
    out_specs = (tiles, tiles) + (P(),) * 8
    return jax.shard_map(shards, mesh=mesh, in_specs=in_specs, out_specs=out_specs, check_vma=False)
```

```python
import functools

import jax
import jax.numpy as jnp
from jax import lax
from jax.experimental import pallas as pl
from jax.experimental.pallas import tpu as pltpu
from jax.sharding import PartitionSpec as P

EPSILON = 1e-05
BF16 = jnp.bfloat16
F32 = jnp.float32
VMEM = pl.BlockSpec(memory_space=pltpu.VMEM)
ANY = pl.BlockSpec(memory_space=pl.ANY)
HIDE = 10**11
SMALL = 16


def fill_toeplitz(taps_ref, out_ref):
    c = taps_ref.shape[-1]
    zero = jnp.zeros((c, c), BF16)
    half = jnp.asarray(0.5, BF16)
    for b in range(3):
        for i in range(4):
            for j in range(2):
                block = taps_ref[i - j, b] * half if 0 <= i - j < 3 else zero
                out_ref[b, i * c : (i + 1) * c, j * c : (j + 1) * c] = block


def fill_toeplitz_transposed(taps_ref, out_ref):
    c = taps_ref.shape[-1]
    zero = jnp.zeros((c, c), BF16)
    for b in range(3):
        for i in range(4):
            for j in range(2):
                block = taps_ref[2 - (i - j), 2 - b] if 0 <= i - j < 3 else zero
                out_ref[b, j * c : (j + 1) * c, i * c : (i + 1) * c] = block


def convolve_rows(row, starts, weights_ref, across, transposed):
    left = jnp.concatenate(
        [jnp.concatenate([row(r - 1 + i) for r in starts], 0) for i in range(4)], 1
    )
    c = left.shape[1] // 4
    dims = (((1,), (1 if transposed else 0,)), ((), ()))
    taps = [
        lax.dot_general(left, weights_ref[b], dims, preferred_element_type=F32)
        for b in range(3)
    ]

    def piece(pair, j):
        part = [t[pair * across : (pair + 1) * across, j * c : (j + 1) * c] for t in taps]
        return pltpu.roll(part[0], 1, 0) + part[1] + pltpu.roll(part[2], across - 1, 0)

    return piece


def silu(half):
    return half + half * jnp.tanh(half)


def silu_slope(half):
    t = jnp.tanh(half)
    return (0.5 + 0.5 * t) * (1.0 + half * (1.0 - t))


def fold(value):
    return value.reshape(-1, 8, value.shape[-1]).sum(0)


def join(stats, count, at, sums):
    centres = stats[:, at + 2 : at + 3]
    mean = (stats[:, at : at + 1] + sums * centres).sum(0) / count
    away = centres - mean
    squares = stats[:, at + 1 : at + 2] + away * (2.0 * stats[:, at : at + 1] + sums * away)
    variance = jnp.maximum(squares.sum(0) / count, 0.0)
    return mean, lax.rsqrt(variance + EPSILON)


def has_pair():
    count, me = lax.axis_size("lat"), lax.axis_index("lat")
    inside = jnp.logical_and(me != 0, me != count - 1)
    return (me == me, inside) if count % 2 == 0 else (me != count - 1, me != 0)


def pick(even, when_even, when_odd):
    return jnp.where(even, when_even, when_odd)


def column_mask(bits, k, c):
    tile = bits[k // 128]
    return jnp.broadcast_to(tile[:, k % 128 : k % 128 + 1].astype(F32), (tile.shape[0], c))


def near_rows_kernel(top_ref, bottom_ref, gx_ref, gp_ref):
    even = lax.axis_index("lat") % 2 == 0
    top, bottom = top_ref[...], bottom_ref[...]
    paired_x, paired_p = has_pair()
    gx_ref[...] = pick(paired_x, pick(even, bottom, top), jnp.zeros_like(top))
    gp_ref[...] = pick(paired_p, pick(even, top, bottom), jnp.zeros_like(top))


def far_rows_kernel(x_ref, mask_ref, hx_ref, hp_ref, bits_ref):
    samples, height, across, c = x_ref.shape
    even = lax.axis_index("lat") % 2 == 0
    for k in range(bits_ref.shape[0]):
        bits = mask_ref[k * 128 : (k + 1) * 128].astype(F32)
        bits = jnp.concatenate([bits, jnp.zeros((bits.shape[0], 128 - across), F32)], 1)
        if bits.shape[0] < 128:
            bits = jnp.concatenate([bits, jnp.zeros((128 - bits.shape[0], 128), F32)], 0)
        bits_ref[k] = bits.T[:across]
    zero = jnp.zeros((across, c), BF16)
    for out, down, paired in zip((hx_ref, hp_ref), (even, jnp.logical_not(even)), has_pair()):
        first = jnp.where(down, height - 3, 1)
        for s in range(samples):
            out[2 * s] = pick(paired, x_ref[s, first], zero)
            out[2 * s + 1] = pick(paired, x_ref[s, first + 1], zero)
        for k in range(bits_ref.shape[0]):
            bits = bits_ref[k]
            out[2 * samples + k] = pick(paired, bits, jnp.zeros_like(bits)).astype(BF16)


def masks_kernel(bits_ref, m_ref, count_ref):
    samples, height, across, c = m_ref.shape
    count = jnp.zeros((8, c), F32)
    for s in range(samples):
        for r in range(height):
            mask = column_mask(bits_ref, s * height + r, c)
            m_ref[s, r] = mask
            count += fold(mask)
    count_ref[...] = stats_block([count.sum(0, keepdims=True)], c)


def stats_block(rows, c):
    return jnp.concatenate(rows + [jnp.zeros((8 - len(rows), c), F32)], 0)


def gather(refs):
    return jnp.concatenate([r[...] for r in refs], 0)


def middle(value):
    return value.mean(0, keepdims=True)


def add_moments(sums, active, mask):
    masked = active * mask
    sums[0] += fold(masked)
    sums[1] += fold(masked * active)
    return masked


def own_row(inner_ref, outer_ref, s, r, height):
    if 2 <= r < height - 2:
        return inner_ref[s, r - 2]
    return outer_ref[s, r if r < 2 else r - height + 4]


def conv1_inner_kernel(x_ref, m_ref, w_ref, b_ref, a_ref, z_ref, t_ref, part_ref):
    samples, height, across, c = x_ref.shape
    fill_toeplitz(w_ref, t_ref)
    bias = 0.5 * b_ref[...]
    sums = [jnp.zeros((8, c), F32) for _ in range(2)]
    centre = None
    for s in range(samples):
        piece = convolve_rows(lambda r: x_ref[s, r], range(2, height - 2, 2), t_ref, across, False)
        for i in range(height - 4):
            half = piece(i // 2, i % 2) + bias
            active = silu(half)
            if centre is None:
                centre = middle(active)
            active = active - centre
            a_ref[s, i] = active
            z_ref[s, i] = half
            add_moments(sums, active, m_ref[s, i + 2])
    rows = [v.sum(0, keepdims=True) for v in sums]
    part_ref[...] = stats_block([rows[0], rows[1], centre], c)


def conv1_outer_kernel(
    gp_ref, gx_ref, x_ref, m_ref, count_ref, t_ref, b_ref, part_ref, a_ref, z_ref, st_ref
):
    samples, height, across, c = x_ref.shape
    even = lax.axis_index("lat") % 2 == 0
    bias = 0.5 * b_ref[...]
    centre = part_ref[2:3]

    def row(r):
        if r < 0:
            parts = [pick(even, gp_ref[s, 0], gx_ref[s, 0]) for s in range(samples)]
        elif r >= height:
            parts = [pick(even, gx_ref[s, 0], gp_ref[s, 0]) for s in range(samples)]
        else:
            parts = [x_ref[s, r] for s in range(samples)]
        return jnp.concatenate(parts, 0)

    sums = [jnp.zeros((8, c), F32) for _ in range(2)]
    for slot, start in ((0, 0), (2, height - 2)):
        piece = convolve_rows(row, (start,), t_ref, across, False)
        for s in range(samples):
            for j in range(2):
                half = piece(s, j) + bias
                active = silu(half) - centre
                a_ref[s, slot + j] = active
                z_ref[s, slot + j] = half
                add_moments(sums, active, m_ref[s, start + j])
    rows = [part_ref[i : i + 1] + v.sum(0, keepdims=True) for i, v in enumerate(sums)]
    st_ref[...] = stats_block([rows[0], rows[1], centre, count_ref[0:1]], c)


def prepare_kernel(u_ref, m_ref, w2_ref, mu_ref, su_ref, t2_ref, tt2_ref):
    samples, height, across, c = u_ref.shape
    fill_toeplitz(w2_ref, t2_ref)
    fill_toeplitz_transposed(w2_ref, tt2_ref)
    total = jnp.zeros((8, c), F32)
    for s in range(samples):
        for r in range(height):
            value = u_ref[s, r].astype(F32) * m_ref[s, r]
            mu_ref[s, r] = value
            total += fold(value)
    su_ref[...] = stats_block([total.sum(0, keepdims=True)], c)


def conv1_edge_kernel(
    hp_ref, hx_ref, gp_ref, gx_ref, x_ref, st_ref, t_ref, b_ref, a_ref, mh_ref
):
    samples, height, across, c = x_ref.shape
    even = lax.axis_index("lat") % 2 == 0
    bias = 0.5 * b_ref[...]
    centre = st_ref[2:3]

    def row(r):
        parts = []
        for s in range(samples):
            if r < -1:
                parts.append(pick(even, hp_ref[2 * s + r + 3], hx_ref[2 * s + r + 3]))
            elif r == -1:
                parts.append(pick(even, gp_ref[s, 0], gx_ref[s, 0]))
            elif r < height:
                parts.append(x_ref[s, r])
            elif r == height:
                parts.append(pick(even, gx_ref[s, 0], gp_ref[s, 0]))
            else:
                j = r - height - 1
                parts.append(pick(even, hx_ref[2 * s + j], hp_ref[2 * s + j]))
        return jnp.concatenate(parts, 0)

    slabs = slice(2 * samples, hx_ref.shape[0])
    above = pick(even, hp_ref[slabs], hx_ref[slabs])
    below = pick(even, hx_ref[slabs], hp_ref[slabs])
    for slot, start in ((0, -2), (2, height)):
        piece = convolve_rows(row, (start,), t_ref, across, False)
        for s in range(samples):
            for j in range(2):
                a_ref[s, slot + j] = silu(piece(s, j) + bias) - centre
                if start < 0:
                    mask = column_mask(above, s * height + height - 2 + j, c)
                else:
                    mask = column_mask(below, s * height + j, c)
                mh_ref[s, slot + j] = mask


def conv2_kernel(
    pieces,
    own_ref, a_ref, ao_ref, ah_ref, m_ref, mh_ref, mu_ref, su_ref, k_ref, b_ref, g_ref, t_ref, *refs,
):
    stats, (n_ref, a2_ref, z2_ref, c1_ref, st2_ref, ext_ref) = gather(refs[:pieces]), refs[pieces:]
    samples, height, across, c = m_ref.shape
    counts = stats[:, 3:4]
    count = counts.sum(0)
    mean, inverse = join(stats, count, 0, counts)
    offset = mean - own_ref[2:3]
    scale = inverse * g_ref[...]
    shift = t_ref[...] - offset * scale
    c1_ref[...] = stats_block([offset, inverse, count, mean], c)
    bias = 0.5 * b_ref[...]
    sums = [jnp.zeros((8, c), F32) for _ in range(3)]
    centre = None
    for s in range(samples):
        ext = ext_ref.at[s % 2]
        for i in range(height + 4):
            r = i - 2
            if 0 <= r < height:
                value, mask = own_row(a_ref, ao_ref, s, r, height), m_ref[s, r]
            else:
                j = i if r < 0 else r - height + 2
                value, mask = ah_ref[s, j], mh_ref[s, j]
            ext[i] = ((value * scale + shift) * mask).astype(BF16)
            if 1 <= i < height + 3:
                n_ref[s, i - 1] = ext[i]

        piece = convolve_rows(
            lambda r: ext[r + 2], range(-1, height + 1, 2), k_ref, across, False
        )
        for i in range(height + 2):
            r = i - 1
            half = piece(i // 2, i % 2) + bias
            active = silu(half)
            if centre is None:
                centre = middle(active)
            active = active - centre
            if 0 <= r < height:
                add_moments(sums, active, m_ref[s, r])
                sums[2] += fold(active * mu_ref[s, r])
            a2_ref[s, i] = active
            z2_ref[s, i] = half
    rows = [v.sum(0, keepdims=True) for v in sums]
    st2_ref[...] = stats_block(
        [rows[0], rows[1], centre, rows[2], su_ref[0:1], own_ref[3:4]], c
    )


def slopes_kernel(z_ref, zo_ref, z2_ref, m_ref, mh_ref, after_ref, s_ref, s2_ref):
    samples, height = m_ref.shape[:2]
    for s in range(samples):
        for r in range(-1, height + 1):
            mask = mh_ref[s, 1 if r < 0 else 2]
            if 0 <= r < height:
                mask = m_ref[s, r]
                s_ref[s, r] = silu_slope(own_row(z_ref, zo_ref, s, r, height)) * mask
            s2_ref[s, r + 1] = silu_slope(z2_ref[s, r + 1]) * mask


def back_terms(scale, inverse, offset, gain_sum, shift_sum, count):
    by_active = -scale * gain_sum * inverse / count
    constant = -scale * (shift_sum - offset * inverse * gain_sum) / count
    return by_active, constant


def back2_kernel(
    pieces,
    own_ref, st1_ref, c1_ref, a2_ref, s2_ref, mu_ref, ux_ref, up_ref, m_ref, a_ref, ao_ref, k_ref, g_ref, t_ref, *refs,
):
    stats, (d_ref, dn_ref, c2_ref, st3_ref, ext_ref) = gather(refs[:pieces]), refs[pieces:]
    samples, height, across, c = m_ref.shape
    even = lax.axis_index("lat") % 2 == 0
    count = c1_ref[2:3]
    mean, inverse = join(stats, count, 0, stats[:, 5:6])
    offset = mean - own_ref[2:3]
    shift_sum = stats[:, 4:5].sum(0)
    away = stats[:, 2:3] - mean
    gain_sum = inverse * (stats[:, 3:4] + away * stats[:, 4:5]).sum(0)
    scale = inverse * g_ref[...]
    by_active, constant = back_terms(scale, inverse, offset, gain_sum, shift_sum, count)
    c2_ref[...] = stats_block([scale, t_ref[...] - offset * scale, gain_sum, shift_sum], c)
    sums = [jnp.zeros((8, c), F32) for _ in range(2)]
    for s in range(samples):
        ext = ext_ref.at[s % 2]
        for i in range(height + 2):
            if 0 < i <= height:
                upstream = mu_ref[s, i - 1]
            else:
                edges = (up_ref[s], ux_ref[s]) if i == 0 else (ux_ref[s], up_ref[s])
                upstream = pick(even, *edges).astype(F32)
            grad = upstream * scale + (a2_ref[s, i] * by_active + constant)
            ext[i] = (grad * s2_ref[s, i]).astype(BF16)
            if 0 < i <= height:
                d_ref[s, i - 1] = ext[i]
        piece = convolve_rows(
            lambda r: ext[r + 1], range(0, height, 2), k_ref, across, True
        )
        for r in range(height):
            part = piece(r // 2, r % 2)
            dn_ref[s, r] = part
            masked = part * m_ref[s, r]
            sums[0] += fold(masked)
            sums[1] += fold(masked * own_row(a_ref, ao_ref, s, r, height))
    rows = [v.sum(0, keepdims=True) for v in sums]
    st3_ref[...] = stats_block([rows[0], rows[1], st1_ref[2:3]], c)


def weight_products(rows, centre, turned, total_ref, first):
    windows = jnp.concatenate(rows, 1)
    product = lax.dot_general(
        windows,
        jnp.concatenate([turned[0], centre, turned[1]], 1),
        (((0,), (0,)), ((), ())),
        preferred_element_type=F32,
    )
    if first:
        total_ref[...] = product
    else:
        total_ref[...] += product


def turn(value, across):
    c = value.shape[-1]
    return [
        pltpu.roll(value, k, 1).astype(BF16).reshape(-1, c) for k in (across - 1, 1)
    ]


def weight2_kernel(n_ref, d_ref, after_ref, w_ref, b_ref, acc_ref):
    samples, height, across, c = d_ref.shape
    bias = jnp.zeros((8, c), F32)
    for s in range(samples):
        grad = d_ref[s]
        wide = grad.astype(F32)
        bias += fold(wide)
        rows = [n_ref[s, a : a + height].reshape(-1, c) for a in range(3)]
        weight_products(rows, grad.reshape(-1, c), turn(wide, across), acc_ref, s == 0)
    b_ref[...] = jnp.broadcast_to(bias.sum(0, keepdims=True), b_ref.shape)
    for a in range(3):
        for b in range(3):
            at = (a * 3 + b) * c
            w_ref[at : at + c] = acc_ref[a * c : (a + 1) * c, b * c : (b + 1) * c].astype(BF16)


def output_kernel(x_ref, a2_ref, m_ref, c2_ref, after_ref, o_hbm, done_ref, o_ref, sems):
    samples, height, across, c = x_ref.shape
    scale, shift = c2_ref[0:1], c2_ref[1:2]
    for s in range(samples):
        for r in range(height):
            normed = (a2_ref[s, r + 1] * scale + shift) * m_ref[s, r]
            o_ref[s, r] = (x_ref[s, r].astype(F32) + normed).astype(BF16)
        pltpu.make_async_copy(o_ref.at[s], o_hbm.at[s], sems.at[s]).start()
    done_ref[...] = jnp.zeros(done_ref.shape, F32)
    for s in range(samples):
        pltpu.make_async_copy(o_ref.at[s], o_hbm.at[s], sems.at[s]).wait()


def small_rows(rows, c):
    high = jnp.concatenate(rows + [jnp.zeros((8 - len(rows), c), F32)], 0)
    first = high.astype(BF16)
    return jnp.concatenate([first, (high - first.astype(F32)).astype(BF16)], 0)


def weight1_kernel(
    group, leads, pieces,
    c1_ref, c2_ref, dn_ref, a_ref, ao_ref, s_ref, x_ref, gx_ref, gp_ref, g_ref, w2_ref, b2_ref, *refs,
):
    stats = gather(refs[:pieces])
    d_ref, send_ref, keep_ref, acc_ref = refs[pieces:]
    samples, height, across, c = x_ref.shape
    even = lax.axis_index("lat") % 2 == 0
    core = lax.axis_index("dp") % 2
    offset, inverse, count, mean = (c1_ref[i : i + 1] for i in range(4))
    shift_sum = stats[:, 0:1].sum(0)
    away = stats[:, 2:3] - mean
    gain_sum = inverse * (stats[:, 1:2] + away * stats[:, 0:1]).sum(0)
    scale = inverse * g_ref[...]
    by_active, constant = back_terms(scale, inverse, offset, gain_sum, shift_sum, count)
    bias = jnp.zeros((8, c), F32)
    for s in range(samples):
        for r in range(height):
            active = own_row(a_ref, ao_ref, s, r, height)
            grad = dn_ref[s, r] * scale + (active * by_active + constant)
            d_ref[s, r] = (grad * s_ref[s, r]).astype(BF16)
        grad = d_ref[s]
        wide = grad.astype(F32)
        bias += fold(wide)
        above = pick(even, gp_ref[s, 0], gx_ref[s, 0])
        below = pick(even, gx_ref[s, 0], gp_ref[s, 0])
        body = x_ref[s].reshape(-1, c)
        rows = [
            jnp.concatenate([above, body[: (height - 1) * across]], 0),
            body,
            jnp.concatenate([body[across:], below], 0),
        ]
        weight_products(rows, grad.reshape(-1, c), turn(wide, across), acc_ref, s == 0)

    share = 1.0 / group
    small = [
        small_rows([bias.sum(0, keepdims=True), gain_sum * share, shift_sum * share], c),
        small_rows([b2_ref[0:1], c2_ref[2:3] * share, c2_ref[3:4] * share], c),
    ]

    def put(target, which):
        size = 9 * c // leads
        for j in range(leads):
            slot = j ^ place(which, leads)
            if which == 1:
                target[slot, :size] = w2_ref[j * size : (j + 1) * size]
            else:
                at = j * size
                while at < (j + 1) * size:
                    tap, low = at // c, at % c
                    step = min(c - low, (j + 1) * size - at)
                    a, b = tap // 3, tap % 3
                    target[slot, at - j * size : at - j * size + step] = acc_ref[
                        a * c + low : a * c + low + step, b * c : (b + 1) * c
                    ].astype(BF16)
                    at += step
            target[slot, size:] = small[which]

    @pl.when(core == 0)
    def _():
        put(keep_ref, 0)
        put(send_ref, 1)

    @pl.when(core != 0)
    def _():
        put(keep_ref, 1)
        put(send_ref, 0)


def edge_rows_kernel(d_ref, *refs):
    dx_ref, dp_ref = refs[-2:]
    samples, height = d_ref.shape[:2]
    even = lax.axis_index("lat") % 2 == 0
    paired_x, paired_p = has_pair()
    for s in range(samples):
        top, bottom = d_ref[s, 0], d_ref[s, height - 1]
        dx_ref[s] = pick(paired_x, pick(even, bottom, top), jnp.zeros_like(top))
        dp_ref[s] = pick(paired_p, pick(even, top, bottom), jnp.zeros_like(top))


def input_grad_kernel(ep_ref, ex_ref, d_ref, u_ref, w_ref, o_ref, done_ref, k_ref):
    samples, height, across, c = u_ref.shape
    even = lax.axis_index("lat") % 2 == 0
    fill_toeplitz_transposed(w_ref, k_ref)
    for s in range(samples):

        def row(r):
            if r < 0:
                return pick(even, ep_ref[s], ex_ref[s])
            if r >= height:
                return pick(even, ex_ref[s], ep_ref[s])
            return d_ref[s, r]

        piece = convolve_rows(row, range(0, height, 2), k_ref, across, True)
        for r in range(height):
            o_ref[s, r] = (u_ref[s, r].astype(F32) + piece(r // 2, r % 2)).astype(BF16)
    done_ref[...] = jnp.zeros(done_ref.shape, F32)


def join_kernel(leads, *refs):
    out_ref = refs[-1]
    size = refs[0].shape[0] - SMALL
    for k in range(leads):
        out_ref[k * size : (k + 1) * size] = refs[k][:size]
    out_ref[leads * size :] = refs[0][size:]


def write_chunks(leads, which, ref, out_hbm, sum_ref, sems):
    size = out_hbm.shape[0] // leads
    copies = []
    for k in range(leads):
        at = pl.multiple_of((k ^ place(which, leads)) * size, 16)
        rows = slice(k * size, (k + 1) * size)
        sum_ref[rows] = ref[rows].astype(F32)
        copies.append(
            pltpu.make_async_copy(sum_ref.at[rows], out_hbm.at[pl.ds(at, size)], sems.at[k])
        )
        copies[-1].start()
    for copy in copies:
        copy.wait()


def leave_kernel(leads, grad_ref, own_ref, grad_hbm, first_hbm, second_hbm, sum_ref, sems):
    core = lax.axis_index("dp") % 2
    grad = pltpu.make_async_copy(grad_ref, grad_hbm, sems.at[leads])
    grad.start()

    @pl.when(core == 0)
    def _():
        write_chunks(leads, 0, own_ref, first_hbm, sum_ref, sems)

    @pl.when(core != 0)
    def _():
        write_chunks(leads, 1, own_ref, second_hbm, sum_ref, sems)

    grad.wait()


def finish_kernel(leads, own_ref, other_ref, first_in, second_in, first_hbm, second_hbm, *refs):
    small_hbm, (sum_ref, small_ref, sems) = refs[:6], refs[6:]
    core = lax.axis_index("dp") % 2
    small = [r[sum_ref.shape[0] :].astype(F32) for r in (own_ref, other_ref)]
    small = [v[:8] + v[8:] for v in small]
    for which in range(2):
        total = jnp.where(core == which, small[0], small[1])
        for i in range(3):
            small_ref[3 * which + i] = total[i : i + 1]
    copies = [
        pltpu.make_async_copy(small_ref.at[i], small_hbm[i], sems.at[leads + i]) for i in range(6)
    ]
    for copy in copies:
        copy.start()

    @pl.when(core != 0)
    def _():
        write_chunks(leads, 0, other_ref, first_hbm, sum_ref, sems)

    @pl.when(core == 0)
    def _():
        write_chunks(leads, 1, other_ref, second_hbm, sum_ref, sems)

    for copy in copies:
        copy.wait()


def add_kernel(parts, waits, *refs):
    outs = refs[parts + waits :]
    size = outs[0].shape[0] - SMALL
    for k, out in enumerate(outs):
        chunk = [r.at[k] if len(r.shape) == 3 else r for r in refs[:parts]]
        total = functools.reduce(lambda a, b: a + b, [r[...].astype(F32) for r in chunk])
        out[:size] = total[:size].astype(BF16)
        small = total[size : size + 8] + total[size + 8 :]
        high = small.astype(BF16)
        out[size:] = jnp.concatenate([high, (small - high.astype(F32)).astype(BF16)], 0)


def call(
    kernel, outs, scratch, operands, name, flops=0, waits=(), spaces=(VMEM, VMEM), aliases={}
):
    size = sum(o.size * o.dtype.itemsize for o in operands)
    ins, to = (s if isinstance(s, list) else None for s in spaces)
    return pl.pallas_call(
        kernel,
        out_shape=outs,
        in_specs=(ins or [spaces[0]] * len(operands)) + [ANY] * len(waits),
        out_specs=to or jax.tree.map(lambda _: spaces[1], outs),
        scratch_shapes=scratch,
        input_output_aliases=aliases,
        compiler_params=pltpu.CompilerParams(vmem_limit_bytes=16 * 2**20),
        cost_estimate=pl.CostEstimate(flops=flops, bytes_accessed=size, transcendentals=0),
        name=name,
    )(*operands, *waits)


def swap(value, axis, k):
    return lax.ppermute(value, axis, [(i, i ^ k) for i in range(lax.axis_size(axis))])


def cross(value, k, first):
    leads, dps, lats = (lax.axis_size(a) for a in ("lead", "dp", "lat"))
    pairs = []
    for lead in range(leads):
        for dp in range(dps):
            for lat in range(lats):
                by_lead = first if leads != lats else (dp % 2 == 0) == first
                to = (lead ^ k, dp, lat) if by_lead else (lead, dp, lat ^ k)
                pairs.append(tuple((l * dps + d) * lats + t for l, d, t in ((lead, dp, lat), to)))
    return lax.ppermute(value, ("lead", "dp", "lat"), pairs)


def place(which, leads):
    if which == 1 and leads == lax.axis_size("lat"):
        return lax.axis_index("lat")
    return lax.axis_index("lead")


def over_dp_and_lat(value, to):
    dps, lats = lax.axis_size("dp"), lax.axis_size("lat")
    pairs = []
    for dp in range(dps):
        for lat in range(lats):
            to_dp, to_lat = to(dp, lat)
            pairs.append((dp * lats + lat, to_dp * lats + to_lat))
    return lax.ppermute(value, ("dp", "lat"), pairs)


def neighbours(value_x, value_p):
    lats = lax.axis_size("lat")

    def exchange(value, offset):
        def to(dp, lat):
            other = ((lat - offset) ^ 1) + offset if lat >= offset else lats
            return (dp, other) if other < lats else (dp ^ 1, lat)

        return over_dp_and_lat(value, to)

    got_p = exchange(value_p, 1)
    return exchange(value_x, 0), got_p


def blocks_kernel(parts, *refs):
    refs[-1][...] = jnp.concatenate([r[...] for r in refs[:parts]], 0)


def spread(stats, flops=0):
    blocks, k = stats[None], 1
    while k < lax.axis_size("dp"):
        both = (blocks, swap(blocks, "dp", k))
        shape = jax.ShapeDtypeStruct((2 * k, *stats.shape), F32)
        blocks = call(functools.partial(blocks_kernel, 2), shape, [], both, "blocks", flops)
        k *= 2
    return [blocks] + [
        over_dp_and_lat(blocks, lambda dp, lat, k=k: (dp ^ 1, lat ^ k))
        for k in range(1, lax.axis_size("lat"))
    ]


def add_chunks(parts, name, outs=1, waits=(), flops=0):
    shape = jax.ShapeDtypeStruct(parts[0].shape[-2:], BF16)
    return call(
        functools.partial(add_kernel, len(parts), len(waits)),
        [shape] * outs,
        [],
        parts,
        name,
        flops,
        waits,
    )


def sum_everywhere(send, keep, edges, block_output, input_grad):
    leads, lats = lax.axis_size("lead"), lax.axis_size("lat")
    chunks = add_chunks([keep, swap(send, "dp", 1)], "add_dp", leads)
    got = [cross(chunks[k], k, True) for k in reversed(range(1, leads))]
    output = block_output(chunks[0])
    (mine,) = add_chunks([chunks[0]] + got, "add_first", waits=(output[1],))
    got = [cross(mine, k, False) for k in range(1, lats)]
    rows = edges(mine)
    (mine,) = add_chunks([mine] + got, "add_second", flops=HIDE)
    k = 2
    while k < lax.axis_size("dp"):
        (mine,) = add_chunks([mine, swap(mine, "dp", k)], "add_far_dp")
        k *= 2
    size, c = mine.shape[0] - SMALL, mine.shape[1]
    got = [cross(mine, k, True) for k in range(1, leads)]
    grad_input = input_grad(rows)
    own = call(
        functools.partial(join_kernel, leads),
        jax.ShapeDtypeStruct((leads * size + SMALL, c), BF16),
        [],
        (mine, *got),
        "join",
        waits=(grad_input[1],),
    )
    whole = jax.ShapeDtypeStruct((leads * size, c), F32)
    row = jax.ShapeDtypeStruct((1, c), F32)
    dma = pltpu.SemaphoreType.DMA
    total = pltpu.VMEM(whole.shape, F32)
    other = swap(own, "dp", 1)
    grad_input, first, second = call(
        functools.partial(leave_kernel, leads),
        [jax.ShapeDtypeStruct(grad_input[0].shape, BF16), whole, whole],
        [total, dma((leads + 1,))],
        (grad_input[0], own),
        "leave",
        spaces=(VMEM, ANY),
    )
    first, second, *rows = call(
        functools.partial(finish_kernel, leads),
        [whole, whole] + [row] * 6,
        [total, pltpu.VMEM((6, 1, c), F32), dma((leads + 6,))],
        (own, other, first, second),
        "finish",
        spaces=([VMEM, VMEM, ANY, ANY], [ANY] * 8),
        aliases={2: 0, 3: 1},
    )
    return (first, *rows[:3]), (second, *rows[3:]), output[0], grad_input


def shards(
    field,
    cotangent,
    land_sea,
    conv1_weight,
    conv1_bias,
    first_norm_scale,
    norm1_shift,
    conv2_weight,
    conv2_bias,
    second_norm_scale,
    norm2_shift,
):
    x, u, mask = field[0], cotangent[0], land_sea[0]
    samples, height, across, c = x.shape
    group = lax.axis_size("dp") * lax.axis_size("lat")
    leads = lax.axis_size("lead")
    slabs = -(-samples * height // 128)
    vec = lambda v: v.reshape(1, c)
    b1, g1, t1 = vec(conv1_bias), vec(first_norm_scale), vec(norm1_shift)
    b2, g2, t2 = vec(conv2_bias), vec(second_norm_scale), vec(norm2_shift)

    array = jax.ShapeDtypeStruct
    shape = lambda rows, dtype=F32: array((samples, rows, across, c), dtype)
    edge = array((samples, across, c), BF16)
    vector = array((8, c), F32)
    weights = array((3, 4 * c, 2 * c), BF16)
    turned = array((3, 2 * c, 4 * c), BF16)
    ext = lambda rows: pltpu.VMEM((2, rows, across, c), BF16)
    acc = pltpu.VMEM((3 * c, 3 * c), F32)
    conv_flops = 2 * 9 * c * c * samples * height * across

    near = call(
        near_rows_kernel,
        (shape(1, BF16), shape(1, BF16)),
        [],
        (x[:, :1], x[:, height - 1 :]),
        "near_rows",
        conv_flops,
    )
    gx, gp = neighbours(*near)
    packed = array((2 * samples + slabs, across, c), BF16)
    far_x, far_p, bits = call(
        far_rows_kernel,
        (packed, packed, array((slabs, across, 128), F32)),
        [],
        (x, mask.reshape(samples * height, across)),
        "far_rows",
        conv_flops,
    )
    hx, hp = neighbours(far_x, far_p)
    wide_mask, count = call(masks_kernel, (shape(height), vector), [], (bits,), "masks", conv_flops)
    a1, z1, w1t, part = call(
        conv1_inner_kernel,
        (shape(height - 4), shape(height - 4), weights, vector),
        [],
        (x, wide_mask, conv1_weight, b1),
        "conv1_inner",
        4 * conv_flops,
    )
    a1o, z1o, own1 = call(
        conv1_outer_kernel,
        (shape(4), shape(4), vector),
        [],
        (gp, gx, x, wide_mask, count, w1t, b1, part),
        "conv1_outer",
        16 * conv_flops,
    )
    mu, mu_sum, w2t, w2tt = call(
        prepare_kernel,
        (shape(height), vector, weights, turned),
        [],
        (u, wide_mask, conv2_weight),
        "prepare",
        conv_flops,
    )
    a1h, halo_mask = call(
        conv1_edge_kernel,
        (shape(4), shape(4)),
        [],
        (hp, hx, gp, gx, x, own1, w1t, b1),
        "conv1_edges",
        conv_flops // 2,
    )
    st1 = spread(own1)
    n1, a2, z2, c1, own2 = call(
        functools.partial(conv2_kernel, len(st1)),
        (shape(height + 2, BF16), shape(height + 2), shape(height + 2), vector, vector),
        [ext(height + 4)],
        (own1, a1, a1o, a1h, wide_mask, halo_mask, mu, mu_sum, w2t, b2, g1, t1, *st1),
        "conv2",
        conv_flops,
    )
    ux, up = neighbours(*call(edge_rows_kernel, (edge, edge), [], (u,), "u_rows", waits=(own2,)))
    st2 = spread(own2, HIDE)
    s1, s2 = call(
        slopes_kernel,
        (shape(height), shape(height + 2)),
        [],
        (z1, z1o, z2, wide_mask, halo_mask),
        "slopes",
        conv_flops,
        waits=(st2[0],),
    )
    d2, dn1, c2, own3 = call(
        functools.partial(back2_kernel, len(st2)),
        (shape(height, BF16), shape(height), vector, vector),
        [ext(height + 2)],
        (own2, own1, c1, a2, s2, mu, ux, up, wide_mask, a1, a1o, w2tt, g2, t2, *st2),
        "conv2_back",
        conv_flops,
    )
    st3 = spread(own3)
    w2, bias2 = call(
        weight2_kernel,
        (array((9 * c, c), BF16), vector),
        [acc],
        (n1, d2),
        "conv2_weight_grad",
        conv_flops,
        waits=(st3[0],),
    )
    chunks = array((leads, 9 * c // leads + SMALL, c), BF16)
    d1, send, keep = call(
        functools.partial(weight1_kernel, group, leads, len(st3)),
        (shape(height, BF16), chunks, chunks),
        [acc],
        (c1, c2, dn1, a1, a1o, s1, x, gx, gp, g1, w2, bias2, *st3),
        "conv1_weight_grad",
        conv_flops,
    )

    def edges(after):
        rows = call(edge_rows_kernel, (edge, edge), [], (d1,), "edge_rows", waits=(after,))
        return neighbours(*rows)[::-1]

    def input_grad(rows):
        return call(
            input_grad_kernel,
            (shape(height, BF16), vector),
            [pltpu.VMEM(turned.shape, BF16)],
            (*rows, d1, u, conv1_weight),
            "conv1_back",
            conv_flops,
        )

    def block_output(after):
        return call(
            output_kernel,
            (shape(height, BF16), vector),
            [pltpu.VMEM(x.shape, BF16), pltpu.SemaphoreType.DMA((samples,))],
            (x, a2, wide_mask, c2),
            "output",
            conv_flops // 2,
            waits=(after,),
            spaces=(VMEM, [ANY, VMEM]),
        )

    first, second, output, grad_input = sum_everywhere(
        send, keep, edges, block_output, input_grad
    )
    sums = []
    for part in (first, second):
        sums += [part[0].reshape(3, 3, c, c)] + [v.reshape(c) for v in part[1:]]
    return (output[None], grad_input[None], *sums)


def solution(mesh):
    tiles = P("lead", "dp", "lat", None, None)
    in_specs = (tiles, tiles, P("lead", "dp", "lat", None)) + (P(),) * 8
    out_specs = (tiles, tiles) + (P(),) * 8
    return jax.shard_map(shards, mesh=mesh, in_specs=in_specs, out_specs=out_specs, check_vma=False)
```

```python
import functools

import jax
import jax.numpy as jnp
from jax import lax
from jax.experimental import pallas as pl
from jax.experimental.pallas import tpu as pltpu
from jax.sharding import PartitionSpec as P

EPSILON = 1e-05
BF16 = jnp.bfloat16
F32 = jnp.float32
VMEM = pl.BlockSpec(memory_space=pltpu.VMEM)
ANY = pl.BlockSpec(memory_space=pl.ANY)
HIDE = 10**11
SMALL = 16


def fill_toeplitz(taps_ref, out_ref):
    c = taps_ref.shape[-1]
    zero = jnp.zeros((c, c), BF16)
    half = jnp.asarray(0.5, BF16)
    for b in range(3):
        for i in range(4):
            for j in range(2):
                block = taps_ref[i - j, b] * half if 0 <= i - j < 3 else zero
                out_ref[b, i * c : (i + 1) * c, j * c : (j + 1) * c] = block


def fill_toeplitz_transposed(taps_ref, out_ref):
    c = taps_ref.shape[-1]
    zero = jnp.zeros((c, c), BF16)
    for b in range(3):
        for i in range(4):
            for j in range(2):
                block = taps_ref[2 - (i - j), 2 - b] if 0 <= i - j < 3 else zero
                out_ref[b, j * c : (j + 1) * c, i * c : (i + 1) * c] = block


def convolve_rows(row, starts, weights_ref, across, transposed):
    left = jnp.concatenate(
        [jnp.concatenate([row(r - 1 + i) for r in starts], 0) for i in range(4)], 1
    )
    c = left.shape[1] // 4
    dims = (((1,), (1 if transposed else 0,)), ((), ()))
    taps = [
        lax.dot_general(left, weights_ref[b], dims, preferred_element_type=F32)
        for b in range(3)
    ]

    def piece(pair, j):
        part = [t[pair * across : (pair + 1) * across, j * c : (j + 1) * c] for t in taps]
        return pltpu.roll(part[0], 1, 0) + part[1] + pltpu.roll(part[2], across - 1, 0)

    return piece


def silu(half):
    return half + half * jnp.tanh(half)


def silu_slope(half):
    t = jnp.tanh(half)
    return (0.5 + 0.5 * t) * (1.0 + half * (1.0 - t))


def fold(value):
    return value.reshape(-1, 8, value.shape[-1]).sum(0)


def join(stats, count, at, sums):
    centres = stats[:, at + 2 : at + 3]
    mean = (stats[:, at : at + 1] + sums * centres).sum(0) / count
    away = centres - mean
    squares = stats[:, at + 1 : at + 2] + away * (2.0 * stats[:, at : at + 1] + sums * away)
    variance = jnp.maximum(squares.sum(0) / count, 0.0)
    return mean, lax.rsqrt(variance + EPSILON)


def has_pair():
    count, me = lax.axis_size("lat"), lax.axis_index("lat")
    inside = jnp.logical_and(me != 0, me != count - 1)
    return (me == me, inside) if count % 2 == 0 else (me != count - 1, me != 0)


def pick(even, when_even, when_odd):
    return jnp.where(even, when_even, when_odd)


def column_mask(bits, k, c):
    tile = bits[k // 128]
    return jnp.broadcast_to(tile[:, k % 128 : k % 128 + 1].astype(F32), (tile.shape[0], c))


def near_rows_kernel(top_ref, bottom_ref, gx_ref, gp_ref):
    even = lax.axis_index("lat") % 2 == 0
    top, bottom = top_ref[...], bottom_ref[...]
    paired_x, paired_p = has_pair()
    gx_ref[...] = pick(paired_x, pick(even, bottom, top), jnp.zeros_like(top))
    gp_ref[...] = pick(paired_p, pick(even, top, bottom), jnp.zeros_like(top))


def far_rows_kernel(x_ref, bits_ref, *refs):
    samples, height, across, c = x_ref.shape
    even = lax.axis_index("lat") % 2 == 0
    hx_ref, hp_ref = refs[-2:]
    zero = jnp.zeros((across, c), BF16)
    for out, down, paired in zip((hx_ref, hp_ref), (even, jnp.logical_not(even)), has_pair()):
        first = jnp.where(down, height - 3, 1)
        for s in range(samples):
            out[2 * s] = pick(paired, x_ref[s, first], zero)
            out[2 * s + 1] = pick(paired, x_ref[s, first + 1], zero)
        for k in range(bits_ref.shape[0]):
            bits = bits_ref[k]
            out[2 * samples + k] = pick(paired, bits, jnp.zeros_like(bits)).astype(BF16)


def masks_kernel(mask_ref, x_ref, w_ref, b_ref, m_ref, count_ref, bits_ref):
    samples, height, across, c = m_ref.shape
    for k in range(bits_ref.shape[0]):
        bits = mask_ref[k * 128 : (k + 1) * 128].astype(F32)
        bits = jnp.concatenate([bits, jnp.zeros((bits.shape[0], 128 - across), F32)], 1)
        if bits.shape[0] < 128:
            bits = jnp.concatenate([bits, jnp.zeros((128 - bits.shape[0], 128), F32)], 0)
        bits_ref[k] = bits.T[:across]
    count = jnp.zeros((8, c), F32)
    for s in range(samples):
        for r in range(height):
            mask = column_mask(bits_ref, s * height + r, c)
            m_ref[s, r] = mask
            count += fold(mask)
    count_ref[...] = stats_block([count.sum(0, keepdims=True)], c)


def stats_block(rows, c):
    return jnp.concatenate(rows + [jnp.zeros((8 - len(rows), c), F32)], 0)


def gather(refs):
    return jnp.concatenate([r[...] for r in refs], 0)


def middle(value):
    return value.mean(0, keepdims=True)


def add_moments(sums, active, mask):
    masked = active * mask
    sums[0] += fold(masked)
    sums[1] += fold(masked * active)
    return masked


def own_row(inner_ref, outer_ref, s, r, height):
    if 2 <= r < height - 2:
        return inner_ref[s, r - 2]
    return outer_ref[s, r if r < 2 else r - height + 4]


def conv1_inner_kernel(x_ref, m_ref, w_ref, b_ref, a_ref, z_ref, t_ref, part_ref):
    samples, height, across, c = x_ref.shape
    fill_toeplitz(w_ref, t_ref)
    bias = 0.5 * b_ref[...]
    sums = [jnp.zeros((8, c), F32) for _ in range(2)]
    centre = None
    for s in range(samples):
        piece = convolve_rows(lambda r: x_ref[s, r], range(2, height - 2, 2), t_ref, across, False)
        for i in range(height - 4):
            half = piece(i // 2, i % 2) + bias
            active = silu(half)
            if centre is None:
                centre = middle(active)
            active = active - centre
            a_ref[s, i] = active
            z_ref[s, i] = half
            add_moments(sums, active, m_ref[s, i + 2])
    rows = [v.sum(0, keepdims=True) for v in sums]
    part_ref[...] = stats_block([rows[0], rows[1], centre], c)


def conv1_outer_kernel(
    gp_ref, gx_ref, x_ref, m_ref, count_ref, t_ref, b_ref, part_ref, a_ref, z_ref, st_ref
):
    samples, height, across, c = x_ref.shape
    even = lax.axis_index("lat") % 2 == 0
    bias = 0.5 * b_ref[...]
    centre = part_ref[2:3]

    def row(r):
        if r < 0:
            parts = [pick(even, gp_ref[s, 0], gx_ref[s, 0]) for s in range(samples)]
        elif r >= height:
            parts = [pick(even, gx_ref[s, 0], gp_ref[s, 0]) for s in range(samples)]
        else:
            parts = [x_ref[s, r] for s in range(samples)]
        return jnp.concatenate(parts, 0)

    sums = [jnp.zeros((8, c), F32) for _ in range(2)]
    for slot, start in ((0, 0), (2, height - 2)):
        piece = convolve_rows(row, (start,), t_ref, across, False)
        for s in range(samples):
            for j in range(2):
                half = piece(s, j) + bias
                active = silu(half) - centre
                a_ref[s, slot + j] = active
                z_ref[s, slot + j] = half
                add_moments(sums, active, m_ref[s, start + j])
    rows = [part_ref[i : i + 1] + v.sum(0, keepdims=True) for i, v in enumerate(sums)]
    st_ref[...] = stats_block([rows[0], rows[1], centre, count_ref[0:1]], c)


def prepare_kernel(u_ref, m_ref, w2_ref, mu_ref, su_ref, t2_ref, tt2_ref):
    samples, height, across, c = u_ref.shape
    fill_toeplitz(w2_ref, t2_ref)
    fill_toeplitz_transposed(w2_ref, tt2_ref)
    total = jnp.zeros((8, c), F32)
    for s in range(samples):
        for r in range(height):
            value = u_ref[s, r].astype(F32) * m_ref[s, r]
            mu_ref[s, r] = value
            total += fold(value)
    su_ref[...] = stats_block([total.sum(0, keepdims=True)], c)


def conv1_edge_kernel(
    hp_ref, hx_ref, gp_ref, gx_ref, x_ref, st_ref, t_ref, b_ref, a_ref, mh_ref
):
    samples, height, across, c = x_ref.shape
    even = lax.axis_index("lat") % 2 == 0
    bias = 0.5 * b_ref[...]
    centre = st_ref[2:3]

    def row(r):
        parts = []
        for s in range(samples):
            if r < -1:
                parts.append(pick(even, hp_ref[2 * s + r + 3], hx_ref[2 * s + r + 3]))
            elif r == -1:
                parts.append(pick(even, gp_ref[s, 0], gx_ref[s, 0]))
            elif r < height:
                parts.append(x_ref[s, r])
            elif r == height:
                parts.append(pick(even, gx_ref[s, 0], gp_ref[s, 0]))
            else:
                j = r - height - 1
                parts.append(pick(even, hx_ref[2 * s + j], hp_ref[2 * s + j]))
        return jnp.concatenate(parts, 0)

    slabs = slice(2 * samples, hx_ref.shape[0])
    above = pick(even, hp_ref[slabs], hx_ref[slabs])
    below = pick(even, hx_ref[slabs], hp_ref[slabs])
    for slot, start in ((0, -2), (2, height)):
        piece = convolve_rows(row, (start,), t_ref, across, False)
        for s in range(samples):
            for j in range(2):
                a_ref[s, slot + j] = silu(piece(s, j) + bias) - centre
                if start < 0:
                    mask = column_mask(above, s * height + height - 2 + j, c)
                else:
                    mask = column_mask(below, s * height + j, c)
                mh_ref[s, slot + j] = mask


def conv2_kernel(
    pieces,
    own_ref, a_ref, ao_ref, ah_ref, m_ref, mh_ref, mu_ref, su_ref, k_ref, b_ref, g_ref, t_ref, *refs,
):
    stats, (n_ref, a2_ref, z2_ref, c1_ref, st2_ref, ext_ref) = gather(refs[:pieces]), refs[pieces:]
    samples, height, across, c = m_ref.shape
    counts = stats[:, 3:4]
    count = counts.sum(0)
    mean, inverse = join(stats, count, 0, counts)
    offset = mean - own_ref[2:3]
    scale = inverse * g_ref[...]
    shift = t_ref[...] - offset * scale
    c1_ref[...] = stats_block([offset, inverse, count, mean], c)
    bias = 0.5 * b_ref[...]
    sums = [jnp.zeros((8, c), F32) for _ in range(3)]
    centre = None
    for s in range(samples):
        ext = ext_ref.at[s % 2]
        for i in range(height + 4):
            r = i - 2
            if 0 <= r < height:
                value, mask = own_row(a_ref, ao_ref, s, r, height), m_ref[s, r]
            else:
                j = i if r < 0 else r - height + 2
                value, mask = ah_ref[s, j], mh_ref[s, j]
            ext[i] = ((value * scale + shift) * mask).astype(BF16)
            if 1 <= i < height + 3:
                n_ref[s, i - 1] = ext[i]

        piece = convolve_rows(
            lambda r: ext[r + 2], range(-1, height + 1, 2), k_ref, across, False
        )
        for i in range(height + 2):
            r = i - 1
            half = piece(i // 2, i % 2) + bias
            active = silu(half)
            if centre is None:
                centre = middle(active)
            active = active - centre
            if 0 <= r < height:
                add_moments(sums, active, m_ref[s, r])
                sums[2] += fold(active * mu_ref[s, r])
            a2_ref[s, i] = active
            z2_ref[s, i] = half
    rows = [v.sum(0, keepdims=True) for v in sums]
    st2_ref[...] = stats_block(
        [rows[0], rows[1], centre, rows[2], su_ref[0:1], own_ref[3:4]], c
    )


def slopes_kernel(z_ref, zo_ref, z2_ref, m_ref, mh_ref, after_ref, s_ref, s2_ref):
    samples, height = m_ref.shape[:2]
    for s in range(samples):
        for r in range(-1, height + 1):
            mask = mh_ref[s, 1 if r < 0 else 2]
            if 0 <= r < height:
                mask = m_ref[s, r]
                s_ref[s, r] = silu_slope(own_row(z_ref, zo_ref, s, r, height)) * mask
            s2_ref[s, r + 1] = silu_slope(z2_ref[s, r + 1]) * mask


def back_terms(scale, inverse, offset, gain_sum, shift_sum, count):
    by_active = -scale * gain_sum * inverse / count
    constant = -scale * (shift_sum - offset * inverse * gain_sum) / count
    return by_active, constant


def back2_kernel(
    pieces,
    own_ref, st1_ref, c1_ref, a2_ref, s2_ref, mu_ref, ux_ref, up_ref, m_ref, a_ref, ao_ref, k_ref, g_ref, t_ref, *refs,
):
    stats, (d_ref, dn_ref, c2_ref, st3_ref, ext_ref) = gather(refs[:pieces]), refs[pieces:]
    samples, height, across, c = m_ref.shape
    even = lax.axis_index("lat") % 2 == 0
    count = c1_ref[2:3]
    mean, inverse = join(stats, count, 0, stats[:, 5:6])
    offset = mean - own_ref[2:3]
    shift_sum = stats[:, 4:5].sum(0)
    away = stats[:, 2:3] - mean
    gain_sum = inverse * (stats[:, 3:4] + away * stats[:, 4:5]).sum(0)
    scale = inverse * g_ref[...]
    by_active, constant = back_terms(scale, inverse, offset, gain_sum, shift_sum, count)
    c2_ref[...] = stats_block([scale, t_ref[...] - offset * scale, gain_sum, shift_sum], c)
    sums = [jnp.zeros((8, c), F32) for _ in range(2)]
    for s in range(samples):
        ext = ext_ref.at[s % 2]
        for i in range(height + 2):
            if 0 < i <= height:
                upstream = mu_ref[s, i - 1]
            else:
                edges = (up_ref[s], ux_ref[s]) if i == 0 else (ux_ref[s], up_ref[s])
                upstream = pick(even, *edges).astype(F32)
            grad = upstream * scale + (a2_ref[s, i] * by_active + constant)
            ext[i] = (grad * s2_ref[s, i]).astype(BF16)
            if 0 < i <= height:
                d_ref[s, i - 1] = ext[i]
        piece = convolve_rows(
            lambda r: ext[r + 1], range(0, height, 2), k_ref, across, True
        )
        for r in range(height):
            part = piece(r // 2, r % 2)
            dn_ref[s, r] = part
            masked = part * m_ref[s, r]
            sums[0] += fold(masked)
            sums[1] += fold(masked * own_row(a_ref, ao_ref, s, r, height))
    rows = [v.sum(0, keepdims=True) for v in sums]
    st3_ref[...] = stats_block([rows[0], rows[1], st1_ref[2:3]], c)


def weight_products(rows, centre, turned, total_ref, first):
    windows = jnp.concatenate(rows, 1)
    product = lax.dot_general(
        windows,
        jnp.concatenate([turned[0], centre, turned[1]], 1),
        (((0,), (0,)), ((), ())),
        preferred_element_type=F32,
    )
    if first:
        total_ref[...] = product
    else:
        total_ref[...] += product


def turn(value, across):
    c = value.shape[-1]
    return [
        pltpu.roll(value, k, 1).astype(BF16).reshape(-1, c) for k in (across - 1, 1)
    ]


def weight2_kernel(n_ref, d_ref, after_ref, w_ref, b_ref, acc_ref):
    samples, height, across, c = d_ref.shape
    bias = jnp.zeros((8, c), F32)
    for s in range(samples):
        grad = d_ref[s]
        wide = grad.astype(F32)
        bias += fold(wide)
        rows = [n_ref[s, a : a + height].reshape(-1, c) for a in range(3)]
        weight_products(rows, grad.reshape(-1, c), turn(wide, across), acc_ref, s == 0)
    b_ref[...] = jnp.broadcast_to(bias.sum(0, keepdims=True), b_ref.shape)
    for a in range(3):
        for b in range(3):
            at = (a * 3 + b) * c
            w_ref[at : at + c] = acc_ref[a * c : (a + 1) * c, b * c : (b + 1) * c].astype(BF16)


def output_kernel(x_ref, a2_ref, m_ref, c2_ref, after_ref, o_hbm, done_ref, o_ref, sems):
    samples, height, across, c = x_ref.shape
    scale, shift = c2_ref[0:1], c2_ref[1:2]
    for s in range(samples):
        for r in range(height):
            normed = (a2_ref[s, r + 1] * scale + shift) * m_ref[s, r]
            o_ref[s, r] = (x_ref[s, r].astype(F32) + normed).astype(BF16)
        pltpu.make_async_copy(o_ref.at[s], o_hbm.at[s], sems.at[s]).start()
    done_ref[...] = jnp.zeros(done_ref.shape, F32)
    for s in range(samples):
        pltpu.make_async_copy(o_ref.at[s], o_hbm.at[s], sems.at[s]).wait()


def small_rows(rows, c):
    high = jnp.concatenate(rows + [jnp.zeros((8 - len(rows), c), F32)], 0)
    first = high.astype(BF16)
    return jnp.concatenate([first, (high - first.astype(F32)).astype(BF16)], 0)


def weight1_kernel(
    group, leads, pieces,
    c1_ref, c2_ref, dn_ref, a_ref, ao_ref, s_ref, x_ref, gx_ref, gp_ref, g_ref, w2_ref, b2_ref, *refs,
):
    stats = gather(refs[:pieces])
    d_ref, send_ref, keep_ref, acc_ref = refs[pieces:]
    samples, height, across, c = x_ref.shape
    even = lax.axis_index("lat") % 2 == 0
    core = lax.axis_index("dp") % 2
    offset, inverse, count, mean = (c1_ref[i : i + 1] for i in range(4))
    shift_sum = stats[:, 0:1].sum(0)
    away = stats[:, 2:3] - mean
    gain_sum = inverse * (stats[:, 1:2] + away * stats[:, 0:1]).sum(0)
    scale = inverse * g_ref[...]
    by_active, constant = back_terms(scale, inverse, offset, gain_sum, shift_sum, count)
    bias = jnp.zeros((8, c), F32)
    for s in range(samples):
        for r in range(height):
            active = own_row(a_ref, ao_ref, s, r, height)
            grad = dn_ref[s, r] * scale + (active * by_active + constant)
            d_ref[s, r] = (grad * s_ref[s, r]).astype(BF16)
        grad = d_ref[s]
        wide = grad.astype(F32)
        bias += fold(wide)
        above = pick(even, gp_ref[s, 0], gx_ref[s, 0])
        below = pick(even, gx_ref[s, 0], gp_ref[s, 0])
        body = x_ref[s].reshape(-1, c)
        rows = [
            jnp.concatenate([above, body[: (height - 1) * across]], 0),
            body,
            jnp.concatenate([body[across:], below], 0),
        ]
        weight_products(rows, grad.reshape(-1, c), turn(wide, across), acc_ref, s == 0)

    share = 1.0 / group
    small = [
        small_rows([bias.sum(0, keepdims=True), gain_sum * share, shift_sum * share], c),
        small_rows([b2_ref[0:1], c2_ref[2:3] * share, c2_ref[3:4] * share], c),
    ]

    def put(target, which):
        size = 9 * c // leads
        for j in range(leads):
            slot = j ^ place(which, leads)
            if which == 1:
                target[slot, :size] = w2_ref[j * size : (j + 1) * size]
            else:
                at = j * size
                while at < (j + 1) * size:
                    tap, low = at // c, at % c
                    step = min(c - low, (j + 1) * size - at)
                    a, b = tap // 3, tap % 3
                    target[slot, at - j * size : at - j * size + step] = acc_ref[
                        a * c + low : a * c + low + step, b * c : (b + 1) * c
                    ].astype(BF16)
                    at += step
            target[slot, size:] = small[which]

    @pl.when(core == 0)
    def _():
        put(keep_ref, 0)
        put(send_ref, 1)

    @pl.when(core != 0)
    def _():
        put(keep_ref, 1)
        put(send_ref, 0)


def edge_rows_kernel(d_ref, *refs):
    dx_ref, dp_ref = refs[-2:]
    samples, height = d_ref.shape[:2]
    even = lax.axis_index("lat") % 2 == 0
    paired_x, paired_p = has_pair()
    for s in range(samples):
        top, bottom = d_ref[s, 0], d_ref[s, height - 1]
        dx_ref[s] = pick(paired_x, pick(even, bottom, top), jnp.zeros_like(top))
        dp_ref[s] = pick(paired_p, pick(even, top, bottom), jnp.zeros_like(top))


def input_grad_kernel(ep_ref, ex_ref, d_ref, u_ref, w_ref, o_ref, done_ref, k_ref):
    samples, height, across, c = u_ref.shape
    even = lax.axis_index("lat") % 2 == 0
    fill_toeplitz_transposed(w_ref, k_ref)
    for s in range(samples):

        def row(r):
            if r < 0:
                return pick(even, ep_ref[s], ex_ref[s])
            if r >= height:
                return pick(even, ex_ref[s], ep_ref[s])
            return d_ref[s, r]

        piece = convolve_rows(row, range(0, height, 2), k_ref, across, True)
        for r in range(height):
            o_ref[s, r] = (u_ref[s, r].astype(F32) + piece(r // 2, r % 2)).astype(BF16)
    done_ref[...] = jnp.zeros(done_ref.shape, F32)


def join_kernel(leads, *refs):
    out_ref = refs[-1]
    size = refs[0].shape[0] - SMALL
    for k in range(leads):
        out_ref[k * size : (k + 1) * size] = refs[k][:size]
    out_ref[leads * size :] = refs[0][size:]


def write_chunks(leads, which, ref, out_hbm, sum_ref, sems):
    size = out_hbm.shape[0] // leads
    copies = []
    for k in range(leads):
        at = pl.multiple_of((k ^ place(which, leads)) * size, 16)
        rows = slice(k * size, (k + 1) * size)
        sum_ref[rows] = ref[rows].astype(F32)
        copies.append(
            pltpu.make_async_copy(sum_ref.at[rows], out_hbm.at[pl.ds(at, size)], sems.at[k])
        )
        copies[-1].start()
    for copy in copies:
        copy.wait()


def leave_kernel(leads, grad_ref, own_ref, grad_hbm, first_hbm, second_hbm, sum_ref, sems):
    core = lax.axis_index("dp") % 2
    grad = pltpu.make_async_copy(grad_ref, grad_hbm, sems.at[leads])
    grad.start()

    @pl.when(core == 0)
    def _():
        write_chunks(leads, 0, own_ref, first_hbm, sum_ref, sems)

    @pl.when(core != 0)
    def _():
        write_chunks(leads, 1, own_ref, second_hbm, sum_ref, sems)

    grad.wait()


def finish_kernel(leads, own_ref, other_ref, first_in, second_in, first_hbm, second_hbm, *refs):
    small_hbm, (sum_ref, small_ref, sems) = refs[:6], refs[6:]
    core = lax.axis_index("dp") % 2
    small = [r[sum_ref.shape[0] :].astype(F32) for r in (own_ref, other_ref)]
    small = [v[:8] + v[8:] for v in small]
    for which in range(2):
        total = jnp.where(core == which, small[0], small[1])
        for i in range(3):
            small_ref[3 * which + i] = total[i : i + 1]
    copies = [
        pltpu.make_async_copy(small_ref.at[i], small_hbm[i], sems.at[leads + i]) for i in range(6)
    ]
    for copy in copies:
        copy.start()

    @pl.when(core != 0)
    def _():
        write_chunks(leads, 0, other_ref, first_hbm, sum_ref, sems)

    @pl.when(core == 0)
    def _():
        write_chunks(leads, 1, other_ref, second_hbm, sum_ref, sems)

    for copy in copies:
        copy.wait()


def add_kernel(parts, waits, *refs):
    outs = refs[parts + waits :]
    size = outs[0].shape[0] - SMALL
    for k, out in enumerate(outs):
        chunk = [r.at[k] if len(r.shape) == 3 else r for r in refs[:parts]]
        total = functools.reduce(lambda a, b: a + b, [r[...].astype(F32) for r in chunk])
        out[:size] = total[:size].astype(BF16)
        small = total[size : size + 8] + total[size + 8 :]
        high = small.astype(BF16)
        out[size:] = jnp.concatenate([high, (small - high.astype(F32)).astype(BF16)], 0)


def call(
    kernel, outs, scratch, operands, name, flops=0, waits=(), spaces=(VMEM, VMEM), aliases={}
):
    size = sum(o.size * o.dtype.itemsize for o in operands)
    ins, to = (s if isinstance(s, list) else None for s in spaces)
    return pl.pallas_call(
        kernel,
        out_shape=outs,
        in_specs=(ins or [spaces[0]] * len(operands)) + [ANY] * len(waits),
        out_specs=to or jax.tree.map(lambda _: spaces[1], outs),
        scratch_shapes=scratch,
        input_output_aliases=aliases,
        compiler_params=pltpu.CompilerParams(vmem_limit_bytes=16 * 2**20),
        cost_estimate=pl.CostEstimate(flops=flops, bytes_accessed=size, transcendentals=0),
        name=name,
    )(*operands, *waits)


def swap(value, axis, k):
    return lax.ppermute(value, axis, [(i, i ^ k) for i in range(lax.axis_size(axis))])


def cross(value, k, first):
    leads, dps, lats = (lax.axis_size(a) for a in ("lead", "dp", "lat"))
    pairs = []
    for lead in range(leads):
        for dp in range(dps):
            for lat in range(lats):
                by_lead = first if leads != lats else (dp % 2 == 0) == first
                to = (lead ^ k, dp, lat) if by_lead else (lead, dp, lat ^ k)
                pairs.append(tuple((l * dps + d) * lats + t for l, d, t in ((lead, dp, lat), to)))
    return lax.ppermute(value, ("lead", "dp", "lat"), pairs)


def place(which, leads):
    if which == 1 and leads == lax.axis_size("lat"):
        return lax.axis_index("lat")
    return lax.axis_index("lead")


def over_dp_and_lat(value, to):
    dps, lats = lax.axis_size("dp"), lax.axis_size("lat")
    pairs = []
    for dp in range(dps):
        for lat in range(lats):
            to_dp, to_lat = to(dp, lat)
            pairs.append((dp * lats + lat, to_dp * lats + to_lat))
    return lax.ppermute(value, ("dp", "lat"), pairs)


def neighbours(value_x, value_p):
    lats = lax.axis_size("lat")

    def exchange(value, offset):
        def to(dp, lat):
            other = ((lat - offset) ^ 1) + offset if lat >= offset else lats
            return (dp, other) if other < lats else (dp ^ 1, lat)

        return over_dp_and_lat(value, to)

    got_p = exchange(value_p, 1)
    return exchange(value_x, 0), got_p


def blocks_kernel(parts, *refs):
    refs[-1][...] = jnp.concatenate([r[...] for r in refs[:parts]], 0)


def spread(stats, flops=0):
    blocks, k = stats[None], 1
    while k < lax.axis_size("dp"):
        both = (blocks, swap(blocks, "dp", k))
        shape = jax.ShapeDtypeStruct((2 * k, *stats.shape), F32)
        blocks = call(functools.partial(blocks_kernel, 2), shape, [], both, "blocks", flops)
        k *= 2
    return [blocks] + [
        over_dp_and_lat(blocks, lambda dp, lat, k=k: (dp ^ 1, lat ^ k))
        for k in range(1, lax.axis_size("lat"))
    ]


def add_chunks(parts, name, outs=1, waits=(), flops=0):
    shape = jax.ShapeDtypeStruct(parts[0].shape[-2:], BF16)
    return call(
        functools.partial(add_kernel, len(parts), len(waits)),
        [shape] * outs,
        [],
        parts,
        name,
        flops,
        waits,
    )


def sum_everywhere(send, keep, edges, block_output, input_grad):
    leads, lats = lax.axis_size("lead"), lax.axis_size("lat")
    chunks = add_chunks([keep, swap(send, "dp", 1)], "add_dp", leads)
    got = [cross(chunks[k], k, True) for k in reversed(range(1, leads))]
    output = block_output(chunks[0])
    (mine,) = add_chunks([chunks[0]] + got, "add_first", waits=(output[1],))
    got = [cross(mine, k, False) for k in range(1, lats)]
    rows = edges(mine)
    (mine,) = add_chunks([mine] + got, "add_second", flops=HIDE)
    k = 2
    while k < lax.axis_size("dp"):
        (mine,) = add_chunks([mine, swap(mine, "dp", k)], "add_far_dp")
        k *= 2
    size, c = mine.shape[0] - SMALL, mine.shape[1]
    got = [cross(mine, k, True) for k in range(1, leads)]
    grad_input = input_grad(rows)
    own = call(
        functools.partial(join_kernel, leads),
        jax.ShapeDtypeStruct((leads * size + SMALL, c), BF16),
        [],
        (mine, *got),
        "join",
        waits=(grad_input[1],),
    )
    whole = jax.ShapeDtypeStruct((leads * size, c), F32)
    row = jax.ShapeDtypeStruct((1, c), F32)
    dma = pltpu.SemaphoreType.DMA
    total = pltpu.VMEM(whole.shape, F32)
    other = swap(own, "dp", 1)
    grad_input, first, second = call(
        functools.partial(leave_kernel, leads),
        [jax.ShapeDtypeStruct(grad_input[0].shape, BF16), whole, whole],
        [total, dma((leads + 1,))],
        (grad_input[0], own),
        "leave",
        spaces=(VMEM, ANY),
    )
    first, second, *rows = call(
        functools.partial(finish_kernel, leads),
        [whole, whole] + [row] * 6,
        [total, pltpu.VMEM((6, 1, c), F32), dma((leads + 6,))],
        (own, other, first, second),
        "finish",
        spaces=([VMEM, VMEM, ANY, ANY], [ANY] * 8),
        aliases={2: 0, 3: 1},
    )
    return (first, *rows[:3]), (second, *rows[3:]), output[0], grad_input


def shards(
    field,
    cotangent,
    land_sea,
    conv1_weight,
    conv1_bias,
    first_norm_scale,
    norm1_shift,
    conv2_weight,
    conv2_bias,
    second_norm_scale,
    norm2_shift,
):
    x, u, mask = field[0], cotangent[0], land_sea[0]
    samples, height, across, c = x.shape
    group = lax.axis_size("dp") * lax.axis_size("lat")
    leads = lax.axis_size("lead")
    slabs = -(-samples * height // 128)
    vec = lambda v: v.reshape(1, c)
    b1, g1, t1 = vec(conv1_bias), vec(first_norm_scale), vec(norm1_shift)
    b2, g2, t2 = vec(conv2_bias), vec(second_norm_scale), vec(norm2_shift)

    array = jax.ShapeDtypeStruct
    shape = lambda rows, dtype=F32: array((samples, rows, across, c), dtype)
    edge = array((samples, across, c), BF16)
    vector = array((8, c), F32)
    weights = array((3, 4 * c, 2 * c), BF16)
    turned = array((3, 2 * c, 4 * c), BF16)
    ext = lambda rows: pltpu.VMEM((2, rows, across, c), BF16)
    acc = pltpu.VMEM((3 * c, 3 * c), F32)
    conv_flops = 2 * 9 * c * c * samples * height * across

    near = call(
        near_rows_kernel,
        (shape(1, BF16), shape(1, BF16)),
        [],
        (x[:, :1], x[:, height - 1 :]),
        "near_rows",
        conv_flops,
    )
    gx, gp = neighbours(*near)
    packed = array((2 * samples + slabs, across, c), BF16)
    wide_mask, count, bits = call(
        masks_kernel,
        (shape(height), vector, array((slabs, across, 128), F32)),
        [],
        (mask.reshape(samples * height, across), x, conv1_weight, b1),
        "masks",
        conv_flops,
    )
    a1, z1, w1t, part = call(
        conv1_inner_kernel,
        (shape(height - 4), shape(height - 4), weights, vector),
        [],
        (x, wide_mask, conv1_weight, b1),
        "conv1_inner",
        4 * conv_flops,
    )
    hx, hp = neighbours(
        *call(far_rows_kernel, (packed, packed), [], (x, bits), "far_rows", conv_flops, (part,))
    )
    a1o, z1o, own1 = call(
        conv1_outer_kernel,
        (shape(4), shape(4), vector),
        [],
        (gp, gx, x, wide_mask, count, w1t, b1, part),
        "conv1_outer",
        16 * conv_flops,
    )
    mu, mu_sum, w2t, w2tt = call(
        prepare_kernel,
        (shape(height), vector, weights, turned),
        [],
        (u, wide_mask, conv2_weight),
        "prepare",
        conv_flops,
    )
    a1h, halo_mask = call(
        conv1_edge_kernel,
        (shape(4), shape(4)),
        [],
        (hp, hx, gp, gx, x, own1, w1t, b1),
        "conv1_edges",
        conv_flops // 2,
    )
    st1 = spread(own1)
    n1, a2, z2, c1, own2 = call(
        functools.partial(conv2_kernel, len(st1)),
        (shape(height + 2, BF16), shape(height + 2), shape(height + 2), vector, vector),
        [ext(height + 4)],
        (own1, a1, a1o, a1h, wide_mask, halo_mask, mu, mu_sum, w2t, b2, g1, t1, *st1),
        "conv2",
        conv_flops,
    )
    ux, up = neighbours(*call(edge_rows_kernel, (edge, edge), [], (u,), "u_rows", waits=(own2,)))
    st2 = spread(own2, HIDE)
    s1, s2 = call(
        slopes_kernel,
        (shape(height), shape(height + 2)),
        [],
        (z1, z1o, z2, wide_mask, halo_mask),
        "slopes",
        conv_flops,
        waits=(st2[0],),
    )
    d2, dn1, c2, own3 = call(
        functools.partial(back2_kernel, len(st2)),
        (shape(height, BF16), shape(height), vector, vector),
        [ext(height + 2)],
        (own2, own1, c1, a2, s2, mu, ux, up, wide_mask, a1, a1o, w2tt, g2, t2, *st2),
        "conv2_back",
        conv_flops,
    )
    st3 = spread(own3)
    w2, bias2 = call(
        weight2_kernel,
        (array((9 * c, c), BF16), vector),
        [acc],
        (n1, d2),
        "conv2_weight_grad",
        conv_flops,
        waits=(st3[0],),
    )
    chunks = array((leads, 9 * c // leads + SMALL, c), BF16)
    d1, send, keep = call(
        functools.partial(weight1_kernel, group, leads, len(st3)),
        (shape(height, BF16), chunks, chunks),
        [acc],
        (c1, c2, dn1, a1, a1o, s1, x, gx, gp, g1, w2, bias2, *st3),
        "conv1_weight_grad",
        conv_flops,
    )

    def edges(after):
        rows = call(edge_rows_kernel, (edge, edge), [], (d1,), "edge_rows", waits=(after,))
        return neighbours(*rows)[::-1]

    def input_grad(rows):
        return call(
            input_grad_kernel,
            (shape(height, BF16), vector),
            [pltpu.VMEM(turned.shape, BF16)],
            (*rows, d1, u, conv1_weight),
            "conv1_back",
            conv_flops,
        )

    def block_output(after):
        return call(
            output_kernel,
            (shape(height, BF16), vector),
            [pltpu.VMEM(x.shape, BF16), pltpu.SemaphoreType.DMA((samples,))],
            (x, a2, wide_mask, c2),
            "output",
            conv_flops // 2,
            waits=(after,),
            spaces=(VMEM, [ANY, VMEM]),
        )

    first, second, output, grad_input = sum_everywhere(
        send, keep, edges, block_output, input_grad
    )
    sums = []
    for part in (first, second):
        sums += [part[0].reshape(3, 3, c, c)] + [v.reshape(c) for v in part[1:]]
    return (output[None], grad_input[None], *sums)


def solution(mesh):
    tiles = P("lead", "dp", "lat", None, None)
    in_specs = (tiles, tiles, P("lead", "dp", "lat", None)) + (P(),) * 8
    out_specs = (tiles, tiles) + (P(),) * 8
    return jax.shard_map(shards, mesh=mesh, in_specs=in_specs, out_specs=out_specs, check_vma=False)
```

```python
import functools

import jax
import jax.numpy as jnp
from jax import lax
from jax.experimental import pallas as pl
from jax.experimental.pallas import tpu as pltpu
from jax.sharding import PartitionSpec as P

EPSILON = 1e-05
BF16 = jnp.bfloat16
F32 = jnp.float32
VMEM = pl.BlockSpec(memory_space=pltpu.VMEM)
ANY = pl.BlockSpec(memory_space=pl.ANY)
HIDE = 10**11
SMALL = 16


def fill_toeplitz(taps_ref, out_ref):
    c = taps_ref.shape[-1]
    zero = jnp.zeros((c, c), BF16)
    half = jnp.asarray(0.5, BF16)
    for b in range(3):
        for i in range(4):
            for j in range(2):
                block = taps_ref[i - j, b] * half if 0 <= i - j < 3 else zero
                out_ref[b, i * c : (i + 1) * c, j * c : (j + 1) * c] = block


def fill_toeplitz_transposed(taps_ref, out_ref):
    c = taps_ref.shape[-1]
    zero = jnp.zeros((c, c), BF16)
    for b in range(3):
        for i in range(4):
            for j in range(2):
                block = taps_ref[2 - (i - j), 2 - b] if 0 <= i - j < 3 else zero
                out_ref[b, j * c : (j + 1) * c, i * c : (i + 1) * c] = block


def convolve_rows(row, starts, weights_ref, across, transposed):
    left = jnp.concatenate(
        [jnp.concatenate([row(r - 1 + i) for r in starts], 0) for i in range(4)], 1
    )
    c = left.shape[1] // 4
    dims = (((1,), (1 if transposed else 0,)), ((), ()))
    taps = [
        lax.dot_general(left, weights_ref[b], dims, preferred_element_type=F32)
        for b in range(3)
    ]

    def piece(pair, j):
        part = [t[pair * across : (pair + 1) * across, j * c : (j + 1) * c] for t in taps]
        return pltpu.roll(part[0], 1, 0) + part[1] + pltpu.roll(part[2], across - 1, 0)

    return piece


def silu(half):
    return half + half * jnp.tanh(half)


def silu_slope(half):
    t = jnp.tanh(half)
    return (0.5 + 0.5 * t) * (1.0 + half * (1.0 - t))


def fold(value):
    return value.reshape(-1, 8, value.shape[-1]).sum(0)


def join(stats, count, at, sums):
    centres = stats[:, at + 2 : at + 3]
    mean = (stats[:, at : at + 1] + sums * centres).sum(0) / count
    away = centres - mean
    squares = stats[:, at + 1 : at + 2] + away * (2.0 * stats[:, at : at + 1] + sums * away)
    variance = jnp.maximum(squares.sum(0) / count, 0.0)
    return mean, lax.rsqrt(variance + EPSILON)


def has_pair():
    count, me = lax.axis_size("lat"), lax.axis_index("lat")
    inside = jnp.logical_and(me != 0, me != count - 1)
    return (me == me, inside) if count % 2 == 0 else (me != count - 1, me != 0)


def pick(even, when_even, when_odd):
    return jnp.where(even, when_even, when_odd)


def column_mask(bits, k, c):
    tile = bits[k // 128]
    return jnp.broadcast_to(tile[:, k % 128 : k % 128 + 1].astype(F32), (tile.shape[0], c))


def near_rows_kernel(top_ref, bottom_ref, gx_ref, gp_ref):
    even = lax.axis_index("lat") % 2 == 0
    top, bottom = top_ref[...], bottom_ref[...]
    paired_x, paired_p = has_pair()
    gx_ref[...] = pick(paired_x, pick(even, bottom, top), jnp.zeros_like(top))
    gp_ref[...] = pick(paired_p, pick(even, top, bottom), jnp.zeros_like(top))


def far_rows_kernel(x_ref, bits_ref, *refs):
    samples, height, across, c = x_ref.shape
    even = lax.axis_index("lat") % 2 == 0
    hx_ref, hp_ref = refs[-2:]
    zero = jnp.zeros((across, c), BF16)
    for out, down, paired in zip((hx_ref, hp_ref), (even, jnp.logical_not(even)), has_pair()):
        first = jnp.where(down, height - 3, 1)
        for s in range(samples):
            out[2 * s] = pick(paired, x_ref[s, first], zero)
            out[2 * s + 1] = pick(paired, x_ref[s, first + 1], zero)
        for k in range(bits_ref.shape[0]):
            bits = bits_ref[k]
            out[2 * samples + k] = pick(paired, bits, jnp.zeros_like(bits)).astype(BF16)


def masks_kernel(mask_ref, x_ref, w_ref, b_ref, m_ref, count_ref, bits_ref):
    samples, height, across, c = m_ref.shape
    for k in range(bits_ref.shape[0]):
        bits = mask_ref[k * 128 : (k + 1) * 128].astype(F32)
        bits = jnp.concatenate([bits, jnp.zeros((bits.shape[0], 128 - across), F32)], 1)
        if bits.shape[0] < 128:
            bits = jnp.concatenate([bits, jnp.zeros((128 - bits.shape[0], 128), F32)], 0)
        bits_ref[k] = bits.T[:across]
    count = jnp.zeros((8, c), F32)
    for s in range(samples):
        for r in range(height):
            mask = column_mask(bits_ref, s * height + r, c)
            m_ref[s, r] = mask
            count += fold(mask)
    count_ref[...] = stats_block([count.sum(0, keepdims=True)], c)


def stats_block(rows, c):
    return jnp.concatenate(rows + [jnp.zeros((8 - len(rows), c), F32)], 0)


def gather(refs):
    return jnp.concatenate([r[...] for r in refs], 0)


def middle(value):
    return value.mean(0, keepdims=True)


def add_moments(sums, active, mask):
    masked = active * mask
    sums[0] += fold(masked)
    sums[1] += fold(masked * active)
    return masked


def own_row(inner_ref, outer_ref, s, r, height):
    if 2 <= r < height - 2:
        return inner_ref[s, r - 2]
    return outer_ref[s, r if r < 2 else r - height + 4]


def conv1_inner_kernel(x_ref, m_ref, w_ref, b_ref, a_ref, z_ref, t_ref, part_ref):
    samples, height, across, c = x_ref.shape
    fill_toeplitz(w_ref, t_ref)
    bias = 0.5 * b_ref[...]
    sums = [jnp.zeros((8, c), F32) for _ in range(2)]
    centre = None
    for s in range(samples):
        piece = convolve_rows(lambda r: x_ref[s, r], range(2, height - 2, 2), t_ref, across, False)
        for i in range(height - 4):
            half = piece(i // 2, i % 2) + bias
            active = silu(half)
            if centre is None:
                centre = middle(active)
            active = active - centre
            a_ref[s, i] = active
            z_ref[s, i] = half
            add_moments(sums, active, m_ref[s, i + 2])
    rows = [v.sum(0, keepdims=True) for v in sums]
    part_ref[...] = stats_block([rows[0], rows[1], centre], c)


def conv1_outer_kernel(
    gp_ref, gx_ref, x_ref, m_ref, count_ref, t_ref, b_ref, part_ref, a_ref, z_ref, st_ref
):
    samples, height, across, c = x_ref.shape
    even = lax.axis_index("lat") % 2 == 0
    bias = 0.5 * b_ref[...]
    centre = part_ref[2:3]

    def row(r):
        if r < 0:
            parts = [pick(even, gp_ref[s, 0], gx_ref[s, 0]) for s in range(samples)]
        elif r >= height:
            parts = [pick(even, gx_ref[s, 0], gp_ref[s, 0]) for s in range(samples)]
        else:
            parts = [x_ref[s, r] for s in range(samples)]
        return jnp.concatenate(parts, 0)

    sums = [jnp.zeros((8, c), F32) for _ in range(2)]
    for slot, start in ((0, 0), (2, height - 2)):
        piece = convolve_rows(row, (start,), t_ref, across, False)
        for s in range(samples):
            for j in range(2):
                half = piece(s, j) + bias
                active = silu(half) - centre
                a_ref[s, slot + j] = active
                z_ref[s, slot + j] = half
                add_moments(sums, active, m_ref[s, start + j])
    rows = [part_ref[i : i + 1] + v.sum(0, keepdims=True) for i, v in enumerate(sums)]
    st_ref[...] = stats_block([rows[0], rows[1], centre, count_ref[0:1]], c)


def prepare_kernel(u_ref, m_ref, w2_ref, mu_ref, su_ref, t2_ref, tt2_ref):
    samples, height, across, c = u_ref.shape
    fill_toeplitz(w2_ref, t2_ref)
    fill_toeplitz_transposed(w2_ref, tt2_ref)
    total = jnp.zeros((8, c), F32)
    for s in range(samples):
        for r in range(height):
            value = u_ref[s, r].astype(F32) * m_ref[s, r]
            mu_ref[s, r] = value
            total += fold(value)
    su_ref[...] = stats_block([total.sum(0, keepdims=True)], c)


def conv1_edge_kernel(
    hp_ref, hx_ref, gp_ref, gx_ref, x_ref, st_ref, t_ref, b_ref, a_ref, mh_ref
):
    samples, height, across, c = x_ref.shape
    even = lax.axis_index("lat") % 2 == 0
    bias = 0.5 * b_ref[...]
    centre = st_ref[2:3]

    def row(r):
        parts = []
        for s in range(samples):
            if r < -1:
                parts.append(pick(even, hp_ref[2 * s + r + 3], hx_ref[2 * s + r + 3]))
            elif r == -1:
                parts.append(pick(even, gp_ref[s, 0], gx_ref[s, 0]))
            elif r < height:
                parts.append(x_ref[s, r])
            elif r == height:
                parts.append(pick(even, gx_ref[s, 0], gp_ref[s, 0]))
            else:
                j = r - height - 1
                parts.append(pick(even, hx_ref[2 * s + j], hp_ref[2 * s + j]))
        return jnp.concatenate(parts, 0)

    slabs = slice(2 * samples, hx_ref.shape[0])
    above = pick(even, hp_ref[slabs], hx_ref[slabs])
    below = pick(even, hx_ref[slabs], hp_ref[slabs])
    for slot, start in ((0, -2), (2, height)):
        piece = convolve_rows(row, (start,), t_ref, across, False)
        for s in range(samples):
            for j in range(2):
                a_ref[s, slot + j] = silu(piece(s, j) + bias) - centre
                if start < 0:
                    mask = column_mask(above, s * height + height - 2 + j, c)
                else:
                    mask = column_mask(below, s * height + j, c)
                mh_ref[s, slot + j] = mask


def conv2_kernel(
    pieces,
    own_ref, a_ref, ao_ref, ah_ref, m_ref, mh_ref, mu_ref, su_ref, k_ref, b_ref, g_ref, t_ref, *refs,
):
    stats, (n_ref, a2_ref, z2_ref, c1_ref, st2_ref, ext_ref) = gather(refs[:pieces]), refs[pieces:]
    samples, height, across, c = m_ref.shape
    counts = stats[:, 3:4]
    count = counts.sum(0)
    mean, inverse = join(stats, count, 0, counts)
    offset = mean - own_ref[2:3]
    scale = inverse * g_ref[...]
    shift = t_ref[...] - offset * scale
    c1_ref[...] = stats_block([offset, inverse, count, mean], c)
    bias = 0.5 * b_ref[...]
    sums = [jnp.zeros((8, c), F32) for _ in range(3)]
    centre = None
    for s in range(samples):
        ext = ext_ref.at[s % 2]
        for i in range(height + 4):
            r = i - 2
            if 0 <= r < height:
                value, mask = own_row(a_ref, ao_ref, s, r, height), m_ref[s, r]
            else:
                j = i if r < 0 else r - height + 2
                value, mask = ah_ref[s, j], mh_ref[s, j]
            ext[i] = ((value * scale + shift) * mask).astype(BF16)
            if 1 <= i < height + 3:
                n_ref[s, i - 1] = ext[i]

        piece = convolve_rows(
            lambda r: ext[r + 2], range(-1, height + 1, 2), k_ref, across, False
        )
        for i in range(height + 2):
            r = i - 1
            half = piece(i // 2, i % 2) + bias
            active = silu(half)
            if centre is None:
                centre = middle(active)
            active = active - centre
            if 0 <= r < height:
                add_moments(sums, active, m_ref[s, r])
                sums[2] += fold(active * mu_ref[s, r])
            a2_ref[s, i] = active
            z2_ref[s, i] = half
    rows = [v.sum(0, keepdims=True) for v in sums]
    st2_ref[...] = stats_block(
        [rows[0], rows[1], centre, rows[2], su_ref[0:1], own_ref[3:4]], c
    )


def slopes_kernel(z_ref, zo_ref, z2_ref, m_ref, mh_ref, after_ref, s_ref, s2_ref):
    samples, height = m_ref.shape[:2]
    for s in range(samples):
        for r in range(-1, height + 1):
            mask = mh_ref[s, 1 if r < 0 else 2]
            if 0 <= r < height:
                mask = m_ref[s, r]
                s_ref[s, r] = silu_slope(own_row(z_ref, zo_ref, s, r, height)) * mask
            s2_ref[s, r + 1] = silu_slope(z2_ref[s, r + 1]) * mask


def back_terms(scale, inverse, offset, gain_sum, shift_sum, count):
    by_active = -scale * gain_sum * inverse / count
    constant = -scale * (shift_sum - offset * inverse * gain_sum) / count
    return by_active, constant


def back2_kernel(
    pieces,
    own_ref, st1_ref, c1_ref, a2_ref, s2_ref, mu_ref, ux_ref, up_ref, m_ref, a_ref, ao_ref, k_ref, g_ref, t_ref, *refs,
):
    stats, (d_ref, dn_ref, c2_ref, st3_ref, ext_ref) = gather(refs[:pieces]), refs[pieces:]
    samples, height, across, c = m_ref.shape
    even = lax.axis_index("lat") % 2 == 0
    count = c1_ref[2:3]
    mean, inverse = join(stats, count, 0, stats[:, 5:6])
    offset = mean - own_ref[2:3]
    shift_sum = stats[:, 4:5].sum(0)
    away = stats[:, 2:3] - mean
    gain_sum = inverse * (stats[:, 3:4] + away * stats[:, 4:5]).sum(0)
    scale = inverse * g_ref[...]
    by_active, constant = back_terms(scale, inverse, offset, gain_sum, shift_sum, count)
    c2_ref[...] = stats_block([scale, t_ref[...] - offset * scale, gain_sum, shift_sum], c)
    sums = [jnp.zeros((8, c), F32) for _ in range(2)]
    for s in range(samples):
        ext = ext_ref.at[s % 2]
        for i in range(height + 2):
            if 0 < i <= height:
                upstream = mu_ref[s, i - 1]
            else:
                edges = (up_ref[s], ux_ref[s]) if i == 0 else (ux_ref[s], up_ref[s])
                upstream = pick(even, *edges).astype(F32)
            grad = upstream * scale + (a2_ref[s, i] * by_active + constant)
            ext[i] = (grad * s2_ref[s, i]).astype(BF16)
            if 0 < i <= height:
                d_ref[s, i - 1] = ext[i]
        piece = convolve_rows(
            lambda r: ext[r + 1], range(0, height, 2), k_ref, across, True
        )
        for r in range(height):
            part = piece(r // 2, r % 2)
            dn_ref[s, r] = part
            masked = part * m_ref[s, r]
            sums[0] += fold(masked)
            sums[1] += fold(masked * own_row(a_ref, ao_ref, s, r, height))
    rows = [v.sum(0, keepdims=True) for v in sums]
    st3_ref[...] = stats_block([rows[0], rows[1], st1_ref[2:3]], c)


def weight_products(rows, centre, turned, total_ref, first):
    windows = jnp.concatenate(rows, 1)
    product = lax.dot_general(
        windows,
        jnp.concatenate([turned[0], centre, turned[1]], 1),
        (((0,), (0,)), ((), ())),
        preferred_element_type=F32,
    )
    if first:
        total_ref[...] = product
    else:
        total_ref[...] += product


def turn(value, across):
    c = value.shape[-1]
    return [
        pltpu.roll(value, k, 1).astype(BF16).reshape(-1, c) for k in (across - 1, 1)
    ]


def weight2_kernel(n_ref, d_ref, after_ref, w_ref, b_ref, acc_ref):
    samples, height, across, c = d_ref.shape
    bias = jnp.zeros((8, c), F32)
    for s in range(samples):
        grad = d_ref[s]
        wide = grad.astype(F32)
        bias += fold(wide)
        rows = [n_ref[s, a : a + height].reshape(-1, c) for a in range(3)]
        weight_products(rows, grad.reshape(-1, c), turn(wide, across), acc_ref, s == 0)
    b_ref[...] = jnp.broadcast_to(bias.sum(0, keepdims=True), b_ref.shape)
    for a in range(3):
        for b in range(3):
            at = (a * 3 + b) * c
            w_ref[at : at + c] = acc_ref[a * c : (a + 1) * c, b * c : (b + 1) * c].astype(BF16)


def output_kernel(x_ref, a2_ref, m_ref, c2_ref, after_ref, o_hbm, done_ref, o_ref, sems):
    samples, height, across, c = x_ref.shape
    scale, shift = c2_ref[0:1], c2_ref[1:2]
    for s in range(samples):
        for r in range(height):
            normed = (a2_ref[s, r + 1] * scale + shift) * m_ref[s, r]
            o_ref[s, r] = (x_ref[s, r].astype(F32) + normed).astype(BF16)
        pltpu.make_async_copy(o_ref.at[s], o_hbm.at[s], sems.at[s]).start()
    done_ref[...] = jnp.zeros(done_ref.shape, F32)
    for s in range(samples):
        pltpu.make_async_copy(o_ref.at[s], o_hbm.at[s], sems.at[s]).wait()


def small_rows(rows, c):
    high = jnp.concatenate(rows + [jnp.zeros((8 - len(rows), c), F32)], 0)
    first = high.astype(BF16)
    return jnp.concatenate([first, (high - first.astype(F32)).astype(BF16)], 0)


def weight1_kernel(
    group, leads, pieces,
    c1_ref, c2_ref, dn_ref, a_ref, ao_ref, s_ref, x_ref, gx_ref, gp_ref, g_ref, w2_ref, b2_ref, *refs,
):
    stats = gather(refs[:pieces])
    d_ref, send_ref, keep_ref, acc_ref = refs[pieces:]
    samples, height, across, c = x_ref.shape
    even = lax.axis_index("lat") % 2 == 0
    core = lax.axis_index("dp") % 2
    offset, inverse, count, mean = (c1_ref[i : i + 1] for i in range(4))
    shift_sum = stats[:, 0:1].sum(0)
    away = stats[:, 2:3] - mean
    gain_sum = inverse * (stats[:, 1:2] + away * stats[:, 0:1]).sum(0)
    scale = inverse * g_ref[...]
    by_active, constant = back_terms(scale, inverse, offset, gain_sum, shift_sum, count)
    bias = jnp.zeros((8, c), F32)
    for s in range(samples):
        for r in range(height):
            active = own_row(a_ref, ao_ref, s, r, height)
            grad = dn_ref[s, r] * scale + (active * by_active + constant)
            d_ref[s, r] = (grad * s_ref[s, r]).astype(BF16)
        grad = d_ref[s]
        wide = grad.astype(F32)
        bias += fold(wide)
        above = pick(even, gp_ref[s, 0], gx_ref[s, 0])
        below = pick(even, gx_ref[s, 0], gp_ref[s, 0])
        body = x_ref[s].reshape(-1, c)
        rows = [
            jnp.concatenate([above, body[: (height - 1) * across]], 0),
            body,
            jnp.concatenate([body[across:], below], 0),
        ]
        weight_products(rows, grad.reshape(-1, c), turn(wide, across), acc_ref, s == 0)

    share = 1.0 / group
    small = [
        small_rows([bias.sum(0, keepdims=True), gain_sum * share, shift_sum * share], c),
        small_rows([b2_ref[0:1], c2_ref[2:3] * share, c2_ref[3:4] * share], c),
    ]

    def put(target, which):
        size = 9 * c // leads
        for j in range(leads):
            slot = j ^ place(which, leads)
            if which == 1:
                target[slot, :size] = w2_ref[j * size : (j + 1) * size]
            else:
                at = j * size
                while at < (j + 1) * size:
                    tap, low = at // c, at % c
                    step = min(c - low, (j + 1) * size - at)
                    a, b = tap // 3, tap % 3
                    target[slot, at - j * size : at - j * size + step] = acc_ref[
                        a * c + low : a * c + low + step, b * c : (b + 1) * c
                    ].astype(BF16)
                    at += step
            target[slot, size:] = small[which]

    @pl.when(core == 0)
    def _():
        put(keep_ref, 0)
        put(send_ref, 1)

    @pl.when(core != 0)
    def _():
        put(keep_ref, 1)
        put(send_ref, 0)


def edge_rows_kernel(d_ref, *refs):
    dx_ref, dp_ref = refs[-2:]
    samples, height = d_ref.shape[:2]
    even = lax.axis_index("lat") % 2 == 0
    paired_x, paired_p = has_pair()
    for s in range(samples):
        top, bottom = d_ref[s, 0], d_ref[s, height - 1]
        dx_ref[s] = pick(paired_x, pick(even, bottom, top), jnp.zeros_like(top))
        dp_ref[s] = pick(paired_p, pick(even, top, bottom), jnp.zeros_like(top))


def input_grad_kernel(ep_ref, ex_ref, d_ref, u_ref, w_ref, o_ref, done_ref, k_ref):
    samples, height, across, c = u_ref.shape
    even = lax.axis_index("lat") % 2 == 0
    fill_toeplitz_transposed(w_ref, k_ref)
    for s in range(samples):

        def row(r):
            if r < 0:
                return pick(even, ep_ref[s], ex_ref[s])
            if r >= height:
                return pick(even, ex_ref[s], ep_ref[s])
            return d_ref[s, r]

        piece = convolve_rows(row, range(0, height, 2), k_ref, across, True)
        for r in range(height):
            o_ref[s, r] = (u_ref[s, r].astype(F32) + piece(r // 2, r % 2)).astype(BF16)
    done_ref[...] = jnp.zeros(done_ref.shape, F32)


def join_kernel(leads, *refs):
    out_ref = refs[-1]
    size = refs[0].shape[0] - SMALL
    for k in range(leads):
        out_ref[k * size : (k + 1) * size] = refs[k][:size]
    out_ref[leads * size :] = refs[0][size:]


def write_chunks(leads, which, ref, out_hbm, sum_ref, sems):
    size = out_hbm.shape[0] // leads
    copies = []
    for k in range(leads):
        at = pl.multiple_of((k ^ place(which, leads)) * size, 16)
        rows = slice(k * size, (k + 1) * size)
        sum_ref[rows] = ref[rows].astype(F32)
        copies.append(
            pltpu.make_async_copy(sum_ref.at[rows], out_hbm.at[pl.ds(at, size)], sems.at[k])
        )
        copies[-1].start()
    for copy in copies:
        copy.wait()


def leave_kernel(leads, grad_ref, own_ref, grad_hbm, first_hbm, second_hbm, sum_ref, sems):
    core = lax.axis_index("dp") % 2
    grad = pltpu.make_async_copy(grad_ref, grad_hbm, sems.at[leads])
    grad.start()

    @pl.when(core == 0)
    def _():
        write_chunks(leads, 0, own_ref, first_hbm, sum_ref, sems)

    @pl.when(core != 0)
    def _():
        write_chunks(leads, 1, own_ref, second_hbm, sum_ref, sems)

    grad.wait()


def finish_kernel(leads, own_ref, other_ref, first_in, second_in, first_hbm, second_hbm, *refs):
    small_hbm, (sum_ref, small_ref, sems) = refs[:6], refs[6:]
    core = lax.axis_index("dp") % 2
    small = [r[sum_ref.shape[0] :].astype(F32) for r in (own_ref, other_ref)]
    small = [v[:8] + v[8:] for v in small]
    for which in range(2):
        total = jnp.where(core == which, small[0], small[1])
        for i in range(3):
            small_ref[3 * which + i] = total[i : i + 1]
    copies = [
        pltpu.make_async_copy(small_ref.at[i], small_hbm[i], sems.at[leads + i]) for i in range(6)
    ]
    for copy in copies:
        copy.start()

    @pl.when(core != 0)
    def _():
        write_chunks(leads, 0, other_ref, first_hbm, sum_ref, sems)

    @pl.when(core == 0)
    def _():
        write_chunks(leads, 1, other_ref, second_hbm, sum_ref, sems)

    for copy in copies:
        copy.wait()


def add_kernel(parts, waits, *refs):
    outs = refs[parts + waits :]
    size = outs[0].shape[0] - SMALL
    for k, out in enumerate(outs):
        chunk = [r.at[k] if len(r.shape) == 3 else r for r in refs[:parts]]
        total = functools.reduce(lambda a, b: a + b, [r[...].astype(F32) for r in chunk])
        out[:size] = total[:size].astype(BF16)
        small = total[size : size + 8] + total[size + 8 :]
        high = small.astype(BF16)
        out[size:] = jnp.concatenate([high, (small - high.astype(F32)).astype(BF16)], 0)


def call(
    kernel, outs, scratch, operands, name, flops=0, waits=(), spaces=(VMEM, VMEM), aliases={}
):
    size = sum(o.size * o.dtype.itemsize for o in operands)
    ins, to = (s if isinstance(s, list) else None for s in spaces)
    return pl.pallas_call(
        kernel,
        out_shape=outs,
        in_specs=(ins or [spaces[0]] * len(operands)) + [ANY] * len(waits),
        out_specs=to or jax.tree.map(lambda _: spaces[1], outs),
        scratch_shapes=scratch,
        input_output_aliases=aliases,
        compiler_params=pltpu.CompilerParams(vmem_limit_bytes=16 * 2**20),
        cost_estimate=pl.CostEstimate(flops=flops, bytes_accessed=size, transcendentals=0),
        name=name,
    )(*operands, *waits)


def swap(value, axis, k):
    return lax.ppermute(value, axis, [(i, i ^ k) for i in range(lax.axis_size(axis))])


def cross(value, k, first):
    leads, dps, lats = (lax.axis_size(a) for a in ("lead", "dp", "lat"))
    pairs = []
    for lead in range(leads):
        for dp in range(dps):
            for lat in range(lats):
                by_lead = first if leads != lats else (dp % 2 == 0) == first
                to = (lead ^ k, dp, lat) if by_lead else (lead, dp, lat ^ k)
                pairs.append(tuple((l * dps + d) * lats + t for l, d, t in ((lead, dp, lat), to)))
    return lax.ppermute(value, ("lead", "dp", "lat"), pairs)


def place(which, leads):
    if which == 1 and leads == lax.axis_size("lat"):
        return lax.axis_index("lat")
    return lax.axis_index("lead")


def over_dp_and_lat(value, to):
    dps, lats = lax.axis_size("dp"), lax.axis_size("lat")
    pairs = []
    for dp in range(dps):
        for lat in range(lats):
            to_dp, to_lat = to(dp, lat)
            pairs.append((dp * lats + lat, to_dp * lats + to_lat))
    return lax.ppermute(value, ("dp", "lat"), pairs)


def neighbours(value_x, value_p):
    lats = lax.axis_size("lat")

    def exchange(value, offset):
        def to(dp, lat):
            other = ((lat - offset) ^ 1) + offset if lat >= offset else lats
            return (dp, other) if other < lats else (dp ^ 1, lat)

        return over_dp_and_lat(value, to)

    got_p = exchange(value_p, 1)
    return exchange(value_x, 0), got_p


def blocks_kernel(parts, *refs):
    refs[-1][...] = jnp.concatenate([r[...] for r in refs[:parts]], 0)


def spread(stats, flops=0):
    blocks, k = stats[None], 1
    while k < lax.axis_size("dp"):
        both = (blocks, swap(blocks, "dp", k))
        shape = jax.ShapeDtypeStruct((2 * k, *stats.shape), F32)
        blocks = call(functools.partial(blocks_kernel, 2), shape, [], both, "blocks", flops)
        k *= 2
    return [blocks] + [
        over_dp_and_lat(blocks, lambda dp, lat, k=k: (dp ^ 1, lat ^ k))
        for k in range(1, lax.axis_size("lat"))
    ]


def add_chunks(parts, name, outs=1, waits=(), flops=0):
    shape = jax.ShapeDtypeStruct(parts[0].shape[-2:], BF16)
    return call(
        functools.partial(add_kernel, len(parts), len(waits)),
        [shape] * outs,
        [],
        parts,
        name,
        flops,
        waits,
    )


def sum_everywhere(send, keep, edges, block_output, input_grad):
    leads, lats = lax.axis_size("lead"), lax.axis_size("lat")
    chunks = add_chunks([keep, swap(send, "dp", 1)], "add_dp", leads)
    got = [cross(chunks[k], k, True) for k in reversed(range(1, leads))]
    output = block_output(chunks[0])
    rows = edges(chunks[0])
    (mine,) = add_chunks([chunks[0]] + got, "add_first", waits=(output[1],), flops=HIDE)
    got = [cross(mine, k, False) for k in range(1, lats)]
    grad_input = input_grad(rows)
    (mine,) = add_chunks([mine] + got, "add_second", waits=(grad_input[1],))
    k = 2
    while k < lax.axis_size("dp"):
        (mine,) = add_chunks([mine, swap(mine, "dp", k)], "add_far_dp")
        k *= 2
    size, c = mine.shape[0] - SMALL, mine.shape[1]
    got = [cross(mine, k, True) for k in range(1, leads)]
    own = call(
        functools.partial(join_kernel, leads),
        jax.ShapeDtypeStruct((leads * size + SMALL, c), BF16),
        [],
        (mine, *got),
        "join",
    )
    whole = jax.ShapeDtypeStruct((leads * size, c), F32)
    row = jax.ShapeDtypeStruct((1, c), F32)
    dma = pltpu.SemaphoreType.DMA
    total = pltpu.VMEM(whole.shape, F32)
    other = swap(own, "dp", 1)
    grad_input, first, second = call(
        functools.partial(leave_kernel, leads),
        [jax.ShapeDtypeStruct(grad_input[0].shape, BF16), whole, whole],
        [total, dma((leads + 1,))],
        (grad_input[0], own),
        "leave",
        spaces=(VMEM, ANY),
    )
    first, second, *rows = call(
        functools.partial(finish_kernel, leads),
        [whole, whole] + [row] * 6,
        [total, pltpu.VMEM((6, 1, c), F32), dma((leads + 6,))],
        (own, other, first, second),
        "finish",
        spaces=([VMEM, VMEM, ANY, ANY], [ANY] * 8),
        aliases={2: 0, 3: 1},
    )
    return (first, *rows[:3]), (second, *rows[3:]), output[0], grad_input


def shards(
    field,
    cotangent,
    land_sea,
    conv1_weight,
    conv1_bias,
    first_norm_scale,
    norm1_shift,
    conv2_weight,
    conv2_bias,
    second_norm_scale,
    norm2_shift,
):
    x, u, mask = field[0], cotangent[0], land_sea[0]
    samples, height, across, c = x.shape
    group = lax.axis_size("dp") * lax.axis_size("lat")
    leads = lax.axis_size("lead")
    slabs = -(-samples * height // 128)
    vec = lambda v: v.reshape(1, c)
    b1, g1, t1 = vec(conv1_bias), vec(first_norm_scale), vec(norm1_shift)
    b2, g2, t2 = vec(conv2_bias), vec(second_norm_scale), vec(norm2_shift)

    array = jax.ShapeDtypeStruct
    shape = lambda rows, dtype=F32: array((samples, rows, across, c), dtype)
    edge = array((samples, across, c), BF16)
    vector = array((8, c), F32)
    weights = array((3, 4 * c, 2 * c), BF16)
    turned = array((3, 2 * c, 4 * c), BF16)
    ext = lambda rows: pltpu.VMEM((2, rows, across, c), BF16)
    acc = pltpu.VMEM((3 * c, 3 * c), F32)
    conv_flops = 2 * 9 * c * c * samples * height * across

    near = call(
        near_rows_kernel,
        (shape(1, BF16), shape(1, BF16)),
        [],
        (x[:, :1], x[:, height - 1 :]),
        "near_rows",
        conv_flops,
    )
    gx, gp = neighbours(*near)
    packed = array((2 * samples + slabs, across, c), BF16)
    wide_mask, count, bits = call(
        masks_kernel,
        (shape(height), vector, array((slabs, across, 128), F32)),
        [],
        (mask.reshape(samples * height, across), x, conv1_weight, b1),
        "masks",
        conv_flops,
    )
    a1, z1, w1t, part = call(
        conv1_inner_kernel,
        (shape(height - 4), shape(height - 4), weights, vector),
        [],
        (x, wide_mask, conv1_weight, b1),
        "conv1_inner",
        4 * conv_flops,
    )
    hx, hp = neighbours(
        *call(far_rows_kernel, (packed, packed), [], (x, bits), "far_rows", conv_flops, (part,))
    )
    a1o, z1o, own1 = call(
        conv1_outer_kernel,
        (shape(4), shape(4), vector),
        [],
        (gp, gx, x, wide_mask, count, w1t, b1, part),
        "conv1_outer",
        16 * conv_flops,
    )
    mu, mu_sum, w2t, w2tt = call(
        prepare_kernel,
        (shape(height), vector, weights, turned),
        [],
        (u, wide_mask, conv2_weight),
        "prepare",
        conv_flops,
    )
    a1h, halo_mask = call(
        conv1_edge_kernel,
        (shape(4), shape(4)),
        [],
        (hp, hx, gp, gx, x, own1, w1t, b1),
        "conv1_edges",
        conv_flops // 2,
    )
    st1 = spread(own1)
    n1, a2, z2, c1, own2 = call(
        functools.partial(conv2_kernel, len(st1)),
        (shape(height + 2, BF16), shape(height + 2), shape(height + 2), vector, vector),
        [ext(height + 4)],
        (own1, a1, a1o, a1h, wide_mask, halo_mask, mu, mu_sum, w2t, b2, g1, t1, *st1),
        "conv2",
        conv_flops,
    )
    ux, up = neighbours(*call(edge_rows_kernel, (edge, edge), [], (u,), "u_rows", waits=(own2,)))
    st2 = spread(own2, HIDE)
    s1, s2 = call(
        slopes_kernel,
        (shape(height), shape(height + 2)),
        [],
        (z1, z1o, z2, wide_mask, halo_mask),
        "slopes",
        conv_flops,
        waits=(st2[0],),
    )
    d2, dn1, c2, own3 = call(
        functools.partial(back2_kernel, len(st2)),
        (shape(height, BF16), shape(height), vector, vector),
        [ext(height + 2)],
        (own2, own1, c1, a2, s2, mu, ux, up, wide_mask, a1, a1o, w2tt, g2, t2, *st2),
        "conv2_back",
        conv_flops,
    )
    st3 = spread(own3)
    w2, bias2 = call(
        weight2_kernel,
        (array((9 * c, c), BF16), vector),
        [acc],
        (n1, d2),
        "conv2_weight_grad",
        conv_flops,
        waits=(st3[0],),
    )
    chunks = array((leads, 9 * c // leads + SMALL, c), BF16)
    d1, send, keep = call(
        functools.partial(weight1_kernel, group, leads, len(st3)),
        (shape(height, BF16), chunks, chunks),
        [acc],
        (c1, c2, dn1, a1, a1o, s1, x, gx, gp, g1, w2, bias2, *st3),
        "conv1_weight_grad",
        conv_flops,
    )

    def edges(after):
        rows = call(edge_rows_kernel, (edge, edge), [], (d1,), "edge_rows", waits=(after,))
        return neighbours(*rows)[::-1]

    def input_grad(rows):
        return call(
            input_grad_kernel,
            (shape(height, BF16), vector),
            [pltpu.VMEM(turned.shape, BF16)],
            (*rows, d1, u, conv1_weight),
            "conv1_back",
            conv_flops,
        )

    def block_output(after):
        return call(
            output_kernel,
            (shape(height, BF16), vector),
            [pltpu.VMEM(x.shape, BF16), pltpu.SemaphoreType.DMA((samples,))],
            (x, a2, wide_mask, c2),
            "output",
            conv_flops // 2,
            waits=(after,),
            spaces=(VMEM, [ANY, VMEM]),
        )

    first, second, output, grad_input = sum_everywhere(
        send, keep, edges, block_output, input_grad
    )
    sums = []
    for part in (first, second):
        sums += [part[0].reshape(3, 3, c, c)] + [v.reshape(c) for v in part[1:]]
    return (output[None], grad_input[None], *sums)


def solution(mesh):
    tiles = P("lead", "dp", "lat", None, None)
    in_specs = (tiles, tiles, P("lead", "dp", "lat", None)) + (P(),) * 8
    out_specs = (tiles, tiles) + (P(),) * 8
    return jax.shard_map(shards, mesh=mesh, in_specs=in_specs, out_specs=out_specs, check_vma=False)
```

```python
import functools

import jax
import jax.numpy as jnp
from jax import lax
from jax.experimental import pallas as pl
from jax.experimental.pallas import tpu as pltpu
from jax.sharding import PartitionSpec as P

EPSILON = 1e-05
BF16 = jnp.bfloat16
F32 = jnp.float32
VMEM = pl.BlockSpec(memory_space=pltpu.VMEM)
ANY = pl.BlockSpec(memory_space=pl.ANY)
HIDE = 10**11
SMALL = 16


def fill_toeplitz(taps_ref, out_ref):
    c = taps_ref.shape[-1]
    zero = jnp.zeros((c, c), BF16)
    half = jnp.asarray(0.5, BF16)
    for b in range(3):
        for i in range(4):
            for j in range(2):
                block = taps_ref[i - j, b] * half if 0 <= i - j < 3 else zero
                out_ref[b, i * c : (i + 1) * c, j * c : (j + 1) * c] = block


def fill_toeplitz_transposed(taps_ref, out_ref):
    c = taps_ref.shape[-1]
    zero = jnp.zeros((c, c), BF16)
    for b in range(3):
        for i in range(4):
            for j in range(2):
                block = taps_ref[2 - (i - j), 2 - b] if 0 <= i - j < 3 else zero
                out_ref[b, j * c : (j + 1) * c, i * c : (i + 1) * c] = block


def convolve_rows(row, starts, weights_ref, across, transposed):
    left = jnp.concatenate(
        [jnp.concatenate([row(r - 1 + i) for r in starts], 0) for i in range(4)], 1
    )
    c = left.shape[1] // 4
    dims = (((1,), (1 if transposed else 0,)), ((), ()))
    taps = [
        lax.dot_general(left, weights_ref[b], dims, preferred_element_type=F32)
        for b in range(3)
    ]

    def piece(pair, j):
        part = [t[pair * across : (pair + 1) * across, j * c : (j + 1) * c] for t in taps]
        return pltpu.roll(part[0], 1, 0) + part[1] + pltpu.roll(part[2], across - 1, 0)

    return piece


def silu(half):
    return half + half * jnp.tanh(half)


def silu_slope(half):
    t = jnp.tanh(half)
    return (0.5 + 0.5 * t) * (1.0 + half * (1.0 - t))


def fold(value):
    return value.reshape(-1, 8, value.shape[-1]).sum(0)


def join(stats, count, at, sums):
    centres = stats[:, at + 2 : at + 3]
    mean = (stats[:, at : at + 1] + sums * centres).sum(0) / count
    away = centres - mean
    squares = stats[:, at + 1 : at + 2] + away * (2.0 * stats[:, at : at + 1] + sums * away)
    variance = jnp.maximum(squares.sum(0) / count, 0.0)
    return mean, lax.rsqrt(variance + EPSILON)


def has_pair():
    count, me = lax.axis_size("lat"), lax.axis_index("lat")
    inside = jnp.logical_and(me != 0, me != count - 1)
    return (me == me, inside) if count % 2 == 0 else (me != count - 1, me != 0)


def pick(even, when_even, when_odd):
    return jnp.where(even, when_even, when_odd)


def column_mask(bits, k, c):
    tile = bits[k // 128]
    return jnp.broadcast_to(tile[:, k % 128 : k % 128 + 1].astype(F32), (tile.shape[0], c))


def near_rows_kernel(top_ref, bottom_ref, gx_ref, gp_ref):
    even = lax.axis_index("lat") % 2 == 0
    top, bottom = top_ref[...], bottom_ref[...]
    paired_x, paired_p = has_pair()
    gx_ref[...] = pick(paired_x, pick(even, bottom, top), jnp.zeros_like(top))
    gp_ref[...] = pick(paired_p, pick(even, top, bottom), jnp.zeros_like(top))


def far_rows_kernel(x_ref, bits_ref, *refs):
    samples, height, across, c = x_ref.shape
    even = lax.axis_index("lat") % 2 == 0
    hx_ref, hp_ref = refs[-2:]
    zero = jnp.zeros((across, c), BF16)
    for out, down, paired in zip((hx_ref, hp_ref), (even, jnp.logical_not(even)), has_pair()):
        first = jnp.where(down, height - 3, 1)
        for s in range(samples):
            out[2 * s] = pick(paired, x_ref[s, first], zero)
            out[2 * s + 1] = pick(paired, x_ref[s, first + 1], zero)
        for k in range(bits_ref.shape[0]):
            bits = bits_ref[k]
            out[2 * samples + k] = pick(paired, bits, jnp.zeros_like(bits)).astype(BF16)


def masks_kernel(mask_ref, x_ref, w_ref, b_ref, m_ref, count_ref, bits_ref):
    samples, height, across, c = m_ref.shape
    for k in range(bits_ref.shape[0]):
        bits = mask_ref[k * 128 : (k + 1) * 128].astype(F32)
        bits = jnp.concatenate([bits, jnp.zeros((bits.shape[0], 128 - across), F32)], 1)
        if bits.shape[0] < 128:
            bits = jnp.concatenate([bits, jnp.zeros((128 - bits.shape[0], 128), F32)], 0)
        bits_ref[k] = bits.T[:across]
    count = jnp.zeros((8, c), F32)
    for s in range(samples):
        for r in range(height):
            mask = column_mask(bits_ref, s * height + r, c)
            m_ref[s, r] = mask
            count += fold(mask)
    count_ref[...] = stats_block([count.sum(0, keepdims=True)], c)


def stats_block(rows, c):
    return jnp.concatenate(rows + [jnp.zeros((8 - len(rows), c), F32)], 0)


def gather(refs):
    return jnp.concatenate([r[...] for r in refs], 0)


def middle(value):
    return value.mean(0, keepdims=True)


def add_moments(sums, active, mask):
    masked = active * mask
    sums[0] += fold(masked)
    sums[1] += fold(masked * active)
    return masked


def own_row(inner_ref, outer_ref, s, r, height):
    if 2 <= r < height - 2:
        return inner_ref[s, r - 2]
    return outer_ref[s, r if r < 2 else r - height + 4]


def conv1_inner_kernel(x_ref, m_ref, w_ref, b_ref, a_ref, z_ref, t_ref, part_ref):
    samples, height, across, c = x_ref.shape
    fill_toeplitz(w_ref, t_ref)
    bias = 0.5 * b_ref[...]
    sums = [jnp.zeros((8, c), F32) for _ in range(2)]
    centre = None
    for s in range(samples):
        piece = convolve_rows(lambda r: x_ref[s, r], range(2, height - 2, 2), t_ref, across, False)
        for i in range(height - 4):
            half = piece(i // 2, i % 2) + bias
            active = silu(half)
            if centre is None:
                centre = middle(active)
            active = active - centre
            a_ref[s, i] = active
            z_ref[s, i] = half
            add_moments(sums, active, m_ref[s, i + 2])
    rows = [v.sum(0, keepdims=True) for v in sums]
    part_ref[...] = stats_block([rows[0], rows[1], centre], c)


def conv1_outer_kernel(
    gp_ref, gx_ref, x_ref, m_ref, count_ref, t_ref, b_ref, part_ref, a_ref, z_ref, st_ref
):
    samples, height, across, c = x_ref.shape
    even = lax.axis_index("lat") % 2 == 0
    bias = 0.5 * b_ref[...]
    centre = part_ref[2:3]

    def row(r):
        if r < 0:
            parts = [pick(even, gp_ref[s, 0], gx_ref[s, 0]) for s in range(samples)]
        elif r >= height:
            parts = [pick(even, gx_ref[s, 0], gp_ref[s, 0]) for s in range(samples)]
        else:
            parts = [x_ref[s, r] for s in range(samples)]
        return jnp.concatenate(parts, 0)

    sums = [jnp.zeros((8, c), F32) for _ in range(2)]
    for slot, start in ((0, 0), (2, height - 2)):
        piece = convolve_rows(row, (start,), t_ref, across, False)
        for s in range(samples):
            for j in range(2):
                half = piece(s, j) + bias
                active = silu(half) - centre
                a_ref[s, slot + j] = active
                z_ref[s, slot + j] = half
                add_moments(sums, active, m_ref[s, start + j])
    rows = [part_ref[i : i + 1] + v.sum(0, keepdims=True) for i, v in enumerate(sums)]
    st_ref[...] = stats_block([rows[0], rows[1], centre, count_ref[0:1]], c)


def prepare_kernel(u_ref, m_ref, w2_ref, mu_ref, su_ref, t2_ref, tt2_ref):
    samples, height, across, c = u_ref.shape
    fill_toeplitz(w2_ref, t2_ref)
    fill_toeplitz_transposed(w2_ref, tt2_ref)
    total = jnp.zeros((8, c), F32)
    for s in range(samples):
        for r in range(height):
            value = u_ref[s, r].astype(F32) * m_ref[s, r]
            mu_ref[s, r] = value
            total += fold(value)
    su_ref[...] = stats_block([total.sum(0, keepdims=True)], c)


def conv1_edge_kernel(
    hp_ref, hx_ref, gp_ref, gx_ref, x_ref, st_ref, t_ref, b_ref, a_ref, mh_ref
):
    samples, height, across, c = x_ref.shape
    even = lax.axis_index("lat") % 2 == 0
    bias = 0.5 * b_ref[...]
    centre = st_ref[2:3]

    def row(r):
        parts = []
        for s in range(samples):
            if r < -1:
                parts.append(pick(even, hp_ref[2 * s + r + 3], hx_ref[2 * s + r + 3]))
            elif r == -1:
                parts.append(pick(even, gp_ref[s, 0], gx_ref[s, 0]))
            elif r < height:
                parts.append(x_ref[s, r])
            elif r == height:
                parts.append(pick(even, gx_ref[s, 0], gp_ref[s, 0]))
            else:
                j = r - height - 1
                parts.append(pick(even, hx_ref[2 * s + j], hp_ref[2 * s + j]))
        return jnp.concatenate(parts, 0)

    slabs = slice(2 * samples, hx_ref.shape[0])
    above = pick(even, hp_ref[slabs], hx_ref[slabs])
    below = pick(even, hx_ref[slabs], hp_ref[slabs])
    for slot, start in ((0, -2), (2, height)):
        piece = convolve_rows(row, (start,), t_ref, across, False)
        for s in range(samples):
            for j in range(2):
                a_ref[s, slot + j] = silu(piece(s, j) + bias) - centre
                if start < 0:
                    mask = column_mask(above, s * height + height - 2 + j, c)
                else:
                    mask = column_mask(below, s * height + j, c)
                mh_ref[s, slot + j] = mask


def conv2_kernel(
    pieces,
    own_ref, a_ref, ao_ref, ah_ref, m_ref, mh_ref, mu_ref, su_ref, k_ref, b_ref, g_ref, t_ref, *refs,
):
    stats, (n_ref, a2_ref, z2_ref, c1_ref, st2_ref) = gather(refs[:pieces]), refs[pieces:]
    samples, height, across, c = m_ref.shape
    counts = stats[:, 3:4]
    count = counts.sum(0)
    mean, inverse = join(stats, count, 0, counts)
    offset = mean - own_ref[2:3]
    scale = inverse * g_ref[...]
    shift = t_ref[...] - offset * scale
    c1_ref[...] = stats_block([offset, inverse, count, mean], c)
    bias = 0.5 * b_ref[...]
    sums = [jnp.zeros((8, c), F32) for _ in range(3)]
    centre = None
    for s in range(samples):
        for i in range(height + 4):
            r = i - 2
            if 0 <= r < height:
                value, mask = own_row(a_ref, ao_ref, s, r, height), m_ref[s, r]
            else:
                j = i if r < 0 else r - height + 2
                value, mask = ah_ref[s, j], mh_ref[s, j]
            n_ref[s, i] = ((value * scale + shift) * mask).astype(BF16)

        piece = convolve_rows(
            lambda r: n_ref[s, r + 2], range(-1, height + 1, 2), k_ref, across, False
        )
        for i in range(height + 2):
            r = i - 1
            half = piece(i // 2, i % 2) + bias
            active = silu(half)
            if centre is None:
                centre = middle(active)
            active = active - centre
            if 0 <= r < height:
                add_moments(sums, active, m_ref[s, r])
                sums[2] += fold(active * mu_ref[s, r])
            a2_ref[s, i] = active
            z2_ref[s, i] = half
    rows = [v.sum(0, keepdims=True) for v in sums]
    st2_ref[...] = stats_block(
        [rows[0], rows[1], centre, rows[2], su_ref[0:1], own_ref[3:4]], c
    )


def slopes_kernel(z_ref, zo_ref, z2_ref, m_ref, mh_ref, after_ref, s_ref, s2_ref):
    samples, height = m_ref.shape[:2]
    for s in range(samples):
        for r in range(-1, height + 1):
            mask = mh_ref[s, 1 if r < 0 else 2]
            if 0 <= r < height:
                mask = m_ref[s, r]
                s_ref[s, r] = silu_slope(own_row(z_ref, zo_ref, s, r, height)) * mask
            s2_ref[s, r + 1] = silu_slope(z2_ref[s, r + 1]) * mask


def back_terms(scale, inverse, offset, gain_sum, shift_sum, count):
    by_active = -scale * gain_sum * inverse / count
    constant = -scale * (shift_sum - offset * inverse * gain_sum) / count
    return by_active, constant


def back2_kernel(
    pieces,
    own_ref, st1_ref, c1_ref, a2_ref, s2_ref, mu_ref, ux_ref, up_ref, m_ref, a_ref, ao_ref, k_ref, g_ref, t_ref, *refs,
):
    stats, (d_ref, dn_ref, c2_ref, st3_ref) = gather(refs[:pieces]), refs[pieces:]
    samples, height, across, c = m_ref.shape
    even = lax.axis_index("lat") % 2 == 0
    count = c1_ref[2:3]
    mean, inverse = join(stats, count, 0, stats[:, 5:6])
    offset = mean - own_ref[2:3]
    shift_sum = stats[:, 4:5].sum(0)
    away = stats[:, 2:3] - mean
    gain_sum = inverse * (stats[:, 3:4] + away * stats[:, 4:5]).sum(0)
    scale = inverse * g_ref[...]
    by_active, constant = back_terms(scale, inverse, offset, gain_sum, shift_sum, count)
    c2_ref[...] = stats_block([scale, t_ref[...] - offset * scale, gain_sum, shift_sum], c)
    sums = [jnp.zeros((8, c), F32) for _ in range(2)]
    for s in range(samples):
        for i in range(height + 2):
            if 0 < i <= height:
                upstream = mu_ref[s, i - 1]
            else:
                edges = (up_ref[s], ux_ref[s]) if i == 0 else (ux_ref[s], up_ref[s])
                upstream = pick(even, *edges).astype(F32)
            grad = upstream * scale + (a2_ref[s, i] * by_active + constant)
            d_ref[s, i] = (grad * s2_ref[s, i]).astype(BF16)
        piece = convolve_rows(
            lambda r: d_ref[s, r + 1], range(0, height, 2), k_ref, across, True
        )
        for r in range(height):
            part = piece(r // 2, r % 2)
            dn_ref[s, r] = part
            masked = part * m_ref[s, r]
            sums[0] += fold(masked)
            sums[1] += fold(masked * own_row(a_ref, ao_ref, s, r, height))
    rows = [v.sum(0, keepdims=True) for v in sums]
    st3_ref[...] = stats_block([rows[0], rows[1], st1_ref[2:3]], c)


def weight_products(rows, centre, turned, total_ref, first):
    windows = jnp.concatenate(rows, 1)
    product = lax.dot_general(
        windows,
        jnp.concatenate([turned[0], centre, turned[1]], 1),
        (((0,), (0,)), ((), ())),
        preferred_element_type=F32,
    )
    if first:
        total_ref[...] = product
    else:
        total_ref[...] += product


def turn(value, across):
    c = value.shape[-1]
    return [
        pltpu.roll(value, k, 1).astype(BF16).reshape(-1, c) for k in (across - 1, 1)
    ]


def weight2_kernel(n_ref, d_ref, after_ref, w_ref, b_ref, acc_ref):
    samples, rows, across, c = d_ref.shape
    height = rows - 2
    bias = jnp.zeros((8, c), F32)
    for s in range(samples):
        grad = d_ref[s, 1 : 1 + height]
        wide = grad.astype(F32)
        bias += fold(wide)
        rows = [n_ref[s, a + 1 : a + 1 + height].reshape(-1, c) for a in range(3)]
        weight_products(rows, grad.reshape(-1, c), turn(wide, across), acc_ref, s == 0)
    b_ref[...] = jnp.broadcast_to(bias.sum(0, keepdims=True), b_ref.shape)
    for a in range(3):
        for b in range(3):
            at = (a * 3 + b) * c
            w_ref[at : at + c] = acc_ref[a * c : (a + 1) * c, b * c : (b + 1) * c].astype(BF16)


def output_kernel(x_ref, a2_ref, m_ref, c2_ref, after_ref, o_hbm, done_ref, o_ref, sems):
    samples, height, across, c = x_ref.shape
    scale, shift = c2_ref[0:1], c2_ref[1:2]
    for s in range(samples):
        for r in range(height):
            normed = (a2_ref[s, r + 1] * scale + shift) * m_ref[s, r]
            o_ref[s, r] = (x_ref[s, r].astype(F32) + normed).astype(BF16)
        pltpu.make_async_copy(o_ref.at[s], o_hbm.at[s], sems.at[s]).start()
    done_ref[...] = jnp.zeros(done_ref.shape, F32)
    for s in range(samples):
        pltpu.make_async_copy(o_ref.at[s], o_hbm.at[s], sems.at[s]).wait()


def small_rows(rows, c):
    high = jnp.concatenate(rows + [jnp.zeros((8 - len(rows), c), F32)], 0)
    first = high.astype(BF16)
    return jnp.concatenate([first, (high - first.astype(F32)).astype(BF16)], 0)


def weight1_kernel(
    group, leads, pieces,
    c1_ref, c2_ref, dn_ref, a_ref, ao_ref, s_ref, x_ref, gx_ref, gp_ref, g_ref, w2_ref, b2_ref, *refs,
):
    stats = gather(refs[:pieces])
    d_ref, send_ref, keep_ref, acc_ref = refs[pieces:]
    samples, height, across, c = x_ref.shape
    even = lax.axis_index("lat") % 2 == 0
    core = lax.axis_index("dp") % 2
    offset, inverse, count, mean = (c1_ref[i : i + 1] for i in range(4))
    shift_sum = stats[:, 0:1].sum(0)
    away = stats[:, 2:3] - mean
    gain_sum = inverse * (stats[:, 1:2] + away * stats[:, 0:1]).sum(0)
    scale = inverse * g_ref[...]
    by_active, constant = back_terms(scale, inverse, offset, gain_sum, shift_sum, count)
    bias = jnp.zeros((8, c), F32)
    for s in range(samples):
        for r in range(height):
            active = own_row(a_ref, ao_ref, s, r, height)
            grad = dn_ref[s, r] * scale + (active * by_active + constant)
            d_ref[s, r] = (grad * s_ref[s, r]).astype(BF16)
        grad = d_ref[s]
        wide = grad.astype(F32)
        bias += fold(wide)
        above = pick(even, gp_ref[s, 0], gx_ref[s, 0])
        below = pick(even, gx_ref[s, 0], gp_ref[s, 0])
        body = x_ref[s].reshape(-1, c)
        rows = [
            jnp.concatenate([above, body[: (height - 1) * across]], 0),
            body,
            jnp.concatenate([body[across:], below], 0),
        ]
        weight_products(rows, grad.reshape(-1, c), turn(wide, across), acc_ref, s == 0)

    share = 1.0 / group
    small = [
        small_rows([bias.sum(0, keepdims=True), gain_sum * share, shift_sum * share], c),
        small_rows([b2_ref[0:1], c2_ref[2:3] * share, c2_ref[3:4] * share], c),
    ]

    def put(target, which):
        size = 9 * c // leads
        for j in range(leads):
            slot = j ^ place(which, leads)
            if which == 1:
                target[slot, :size] = w2_ref[j * size : (j + 1) * size]
            else:
                at = j * size
                while at < (j + 1) * size:
                    tap, low = at // c, at % c
                    step = min(c - low, (j + 1) * size - at)
                    a, b = tap // 3, tap % 3
                    target[slot, at - j * size : at - j * size + step] = acc_ref[
                        a * c + low : a * c + low + step, b * c : (b + 1) * c
                    ].astype(BF16)
                    at += step
            target[slot, size:] = small[which]

    @pl.when(core == 0)
    def _():
        put(keep_ref, 0)
        put(send_ref, 1)

    @pl.when(core != 0)
    def _():
        put(keep_ref, 1)
        put(send_ref, 0)


def edge_rows_kernel(d_ref, *refs):
    dx_ref, dp_ref = refs[-2:]
    samples, height = d_ref.shape[:2]
    even = lax.axis_index("lat") % 2 == 0
    paired_x, paired_p = has_pair()
    for s in range(samples):
        top, bottom = d_ref[s, 0], d_ref[s, height - 1]
        dx_ref[s] = pick(paired_x, pick(even, bottom, top), jnp.zeros_like(top))
        dp_ref[s] = pick(paired_p, pick(even, top, bottom), jnp.zeros_like(top))


def input_grad_kernel(ep_ref, ex_ref, d_ref, u_ref, w_ref, o_ref, done_ref, k_ref):
    samples, height, across, c = u_ref.shape
    even = lax.axis_index("lat") % 2 == 0
    fill_toeplitz_transposed(w_ref, k_ref)
    for s in range(samples):

        def row(r):
            if r < 0:
                return pick(even, ep_ref[s], ex_ref[s])
            if r >= height:
                return pick(even, ex_ref[s], ep_ref[s])
            return d_ref[s, r]

        piece = convolve_rows(row, range(0, height, 2), k_ref, across, True)
        for r in range(height):
            o_ref[s, r] = (u_ref[s, r].astype(F32) + piece(r // 2, r % 2)).astype(BF16)
    done_ref[...] = jnp.zeros(done_ref.shape, F32)


def join_kernel(leads, *refs):
    out_ref = refs[-1]
    size = refs[0].shape[0] - SMALL
    for k in range(leads):
        out_ref[k * size : (k + 1) * size] = refs[k][:size]
    out_ref[leads * size :] = refs[0][size:]


def write_chunks(leads, which, ref, out_hbm, sum_ref, sems):
    size = out_hbm.shape[0] // leads
    copies = []
    for k in range(leads):
        at = pl.multiple_of((k ^ place(which, leads)) * size, 16)
        rows = slice(k * size, (k + 1) * size)
        sum_ref[rows] = ref[rows].astype(F32)
        copies.append(
            pltpu.make_async_copy(sum_ref.at[rows], out_hbm.at[pl.ds(at, size)], sems.at[k])
        )
        copies[-1].start()
    for copy in copies:
        copy.wait()


def leave_kernel(leads, grad_ref, own_ref, grad_hbm, first_hbm, second_hbm, sum_ref, sems):
    core = lax.axis_index("dp") % 2
    grad = pltpu.make_async_copy(grad_ref, grad_hbm, sems.at[leads])
    grad.start()

    @pl.when(core == 0)
    def _():
        write_chunks(leads, 0, own_ref, first_hbm, sum_ref, sems)

    @pl.when(core != 0)
    def _():
        write_chunks(leads, 1, own_ref, second_hbm, sum_ref, sems)

    grad.wait()


def finish_kernel(leads, own_ref, other_ref, first_in, second_in, first_hbm, second_hbm, *refs):
    small_hbm, (sum_ref, small_ref, sems) = refs[:6], refs[6:]
    core = lax.axis_index("dp") % 2
    small = [r[sum_ref.shape[0] :].astype(F32) for r in (own_ref, other_ref)]
    small = [v[:8] + v[8:] for v in small]
    for which in range(2):
        total = jnp.where(core == which, small[0], small[1])
        for i in range(3):
            small_ref[3 * which + i] = total[i : i + 1]
    copies = [
        pltpu.make_async_copy(small_ref.at[i], small_hbm[i], sems.at[leads + i]) for i in range(6)
    ]
    for copy in copies:
        copy.start()

    @pl.when(core != 0)
    def _():
        write_chunks(leads, 0, other_ref, first_hbm, sum_ref, sems)

    @pl.when(core == 0)
    def _():
        write_chunks(leads, 1, other_ref, second_hbm, sum_ref, sems)

    for copy in copies:
        copy.wait()


def add_kernel(parts, waits, *refs):
    outs = refs[parts + waits :]
    size = outs[0].shape[0] - SMALL
    for k, out in enumerate(outs):
        chunk = [r.at[k] if len(r.shape) == 3 else r for r in refs[:parts]]
        total = functools.reduce(lambda a, b: a + b, [r[...].astype(F32) for r in chunk])
        out[:size] = total[:size].astype(BF16)
        small = total[size : size + 8] + total[size + 8 :]
        high = small.astype(BF16)
        out[size:] = jnp.concatenate([high, (small - high.astype(F32)).astype(BF16)], 0)


def call(
    kernel, outs, scratch, operands, name, flops=0, waits=(), spaces=(VMEM, VMEM), aliases={}
):
    size = sum(o.size * o.dtype.itemsize for o in operands)
    ins, to = (s if isinstance(s, list) else None for s in spaces)
    return pl.pallas_call(
        kernel,
        out_shape=outs,
        in_specs=(ins or [spaces[0]] * len(operands)) + [ANY] * len(waits),
        out_specs=to or jax.tree.map(lambda _: spaces[1], outs),
        scratch_shapes=scratch,
        input_output_aliases=aliases,
        compiler_params=pltpu.CompilerParams(vmem_limit_bytes=16 * 2**20),
        cost_estimate=pl.CostEstimate(flops=flops, bytes_accessed=size, transcendentals=0),
        name=name,
    )(*operands, *waits)


def swap(value, axis, k):
    return lax.ppermute(value, axis, [(i, i ^ k) for i in range(lax.axis_size(axis))])


def cross(value, k, first):
    leads, dps, lats = (lax.axis_size(a) for a in ("lead", "dp", "lat"))
    pairs = []
    for lead in range(leads):
        for dp in range(dps):
            for lat in range(lats):
                by_lead = first if leads != lats else (dp % 2 == 0) == first
                to = (lead ^ k, dp, lat) if by_lead else (lead, dp, lat ^ k)
                pairs.append(tuple((l * dps + d) * lats + t for l, d, t in ((lead, dp, lat), to)))
    return lax.ppermute(value, ("lead", "dp", "lat"), pairs)


def place(which, leads):
    if which == 1 and leads == lax.axis_size("lat"):
        return lax.axis_index("lat")
    return lax.axis_index("lead")


def over_dp_and_lat(value, to):
    dps, lats = lax.axis_size("dp"), lax.axis_size("lat")
    pairs = []
    for dp in range(dps):
        for lat in range(lats):
            to_dp, to_lat = to(dp, lat)
            pairs.append((dp * lats + lat, to_dp * lats + to_lat))
    return lax.ppermute(value, ("dp", "lat"), pairs)


def neighbours(value_x, value_p):
    lats = lax.axis_size("lat")

    def exchange(value, offset):
        def to(dp, lat):
            other = ((lat - offset) ^ 1) + offset if lat >= offset else lats
            return (dp, other) if other < lats else (dp ^ 1, lat)

        return over_dp_and_lat(value, to)

    got_p = exchange(value_p, 1)
    return exchange(value_x, 0), got_p


def blocks_kernel(parts, *refs):
    refs[-1][...] = jnp.concatenate([r[...] for r in refs[:parts]], 0)


def spread(stats, flops=0):
    blocks, k = stats[None], 1
    while k < lax.axis_size("dp"):
        both = (blocks, swap(blocks, "dp", k))
        shape = jax.ShapeDtypeStruct((2 * k, *stats.shape), F32)
        blocks = call(functools.partial(blocks_kernel, 2), shape, [], both, "blocks", flops)
        k *= 2
    return [blocks] + [
        over_dp_and_lat(blocks, lambda dp, lat, k=k: (dp ^ 1, lat ^ k))
        for k in [1, *reversed(range(2, lax.axis_size("lat")))]
    ]


def add_chunks(parts, name, outs=1, waits=(), flops=0):
    shape = jax.ShapeDtypeStruct(parts[0].shape[-2:], BF16)
    return call(
        functools.partial(add_kernel, len(parts), len(waits)),
        [shape] * outs,
        [],
        parts,
        name,
        flops,
        waits,
    )


def sum_everywhere(send, keep, edges, block_output, input_grad):
    leads, lats = lax.axis_size("lead"), lax.axis_size("lat")
    chunks = add_chunks([keep, swap(send, "dp", 1)], "add_dp", leads)
    got = [cross(chunks[k], k, True) for k in reversed(range(1, leads))]
    output = block_output(chunks[0])
    rows = edges(chunks[0])
    (mine,) = add_chunks([chunks[0]] + got, "add_first", waits=(output[1],), flops=HIDE)
    got = [cross(mine, k, False) for k in range(1, lats)]
    grad_input = input_grad(rows)
    (mine,) = add_chunks([mine] + got, "add_second", waits=(grad_input[1],))
    k = 2
    while k < lax.axis_size("dp"):
        (mine,) = add_chunks([mine, swap(mine, "dp", k)], "add_far_dp")
        k *= 2
    size, c = mine.shape[0] - SMALL, mine.shape[1]
    got = [cross(mine, k, True) for k in range(1, leads)]
    own = call(
        functools.partial(join_kernel, leads),
        jax.ShapeDtypeStruct((leads * size + SMALL, c), BF16),
        [],
        (mine, *got),
        "join",
    )
    whole = jax.ShapeDtypeStruct((leads * size, c), F32)
    row = jax.ShapeDtypeStruct((1, c), F32)
    dma = pltpu.SemaphoreType.DMA
    total = pltpu.VMEM(whole.shape, F32)
    other = swap(own, "dp", 1)
    grad_input, first, second = call(
        functools.partial(leave_kernel, leads),
        [jax.ShapeDtypeStruct(grad_input[0].shape, BF16), whole, whole],
        [total, dma((leads + 1,))],
        (grad_input[0], own),
        "leave",
        spaces=(VMEM, ANY),
    )
    first, second, *rows = call(
        functools.partial(finish_kernel, leads),
        [whole, whole] + [row] * 6,
        [total, pltpu.VMEM((6, 1, c), F32), dma((leads + 6,))],
        (own, other, first, second),
        "finish",
        spaces=([VMEM, VMEM, ANY, ANY], [ANY] * 8),
        aliases={2: 0, 3: 1},
    )
    return (first, *rows[:3]), (second, *rows[3:]), output[0], grad_input


def shards(
    field,
    cotangent,
    land_sea,
    conv1_weight,
    conv1_bias,
    first_norm_scale,
    norm1_shift,
    conv2_weight,
    conv2_bias,
    second_norm_scale,
    norm2_shift,
):
    x, u, mask = field[0], cotangent[0], land_sea[0]
    samples, height, across, c = x.shape
    group = lax.axis_size("dp") * lax.axis_size("lat")
    leads = lax.axis_size("lead")
    slabs = -(-samples * height // 128)
    vec = lambda v: v.reshape(1, c)
    b1, g1, t1 = vec(conv1_bias), vec(first_norm_scale), vec(norm1_shift)
    b2, g2, t2 = vec(conv2_bias), vec(second_norm_scale), vec(norm2_shift)

    array = jax.ShapeDtypeStruct
    shape = lambda rows, dtype=F32: array((samples, rows, across, c), dtype)
    edge = array((samples, across, c), BF16)
    vector = array((8, c), F32)
    weights = array((3, 4 * c, 2 * c), BF16)
    turned = array((3, 2 * c, 4 * c), BF16)
    acc = pltpu.VMEM((3 * c, 3 * c), F32)
    conv_flops = 2 * 9 * c * c * samples * height * across

    near = call(
        near_rows_kernel,
        (shape(1, BF16), shape(1, BF16)),
        [],
        (x[:, :1], x[:, height - 1 :]),
        "near_rows",
        conv_flops,
    )
    gx, gp = neighbours(*near)
    packed = array((2 * samples + slabs, across, c), BF16)
    wide_mask, count, bits = call(
        masks_kernel,
        (shape(height), vector, array((slabs, across, 128), F32)),
        [],
        (mask.reshape(samples * height, across), x, conv1_weight, b1),
        "masks",
        conv_flops,
    )
    a1, z1, w1t, part = call(
        conv1_inner_kernel,
        (shape(height - 4), shape(height - 4), weights, vector),
        [],
        (x, wide_mask, conv1_weight, b1),
        "conv1_inner",
        4 * conv_flops,
    )
    hx, hp = neighbours(
        *call(far_rows_kernel, (packed, packed), [], (x, bits), "far_rows", conv_flops, (part,))
    )
    a1o, z1o, own1 = call(
        conv1_outer_kernel,
        (shape(4), shape(4), vector),
        [],
        (gp, gx, x, wide_mask, count, w1t, b1, part),
        "conv1_outer",
        16 * conv_flops,
    )
    mu, mu_sum, w2t, w2tt = call(
        prepare_kernel,
        (shape(height), vector, weights, turned),
        [],
        (u, wide_mask, conv2_weight),
        "prepare",
        conv_flops,
    )
    a1h, halo_mask = call(
        conv1_edge_kernel,
        (shape(4), shape(4)),
        [],
        (hp, hx, gp, gx, x, own1, w1t, b1),
        "conv1_edges",
        conv_flops // 2,
    )
    st1 = spread(own1)
    n1, a2, z2, c1, own2 = call(
        functools.partial(conv2_kernel, len(st1)),
        (shape(height + 4, BF16), shape(height + 2), shape(height + 2), vector, vector),
        [],
        (own1, a1, a1o, a1h, wide_mask, halo_mask, mu, mu_sum, w2t, b2, g1, t1, *st1),
        "conv2",
        conv_flops,
    )
    ux, up = neighbours(*call(edge_rows_kernel, (edge, edge), [], (u,), "u_rows", waits=(own2,)))
    st2 = spread(own2, HIDE)
    s1, s2 = call(
        slopes_kernel,
        (shape(height), shape(height + 2)),
        [],
        (z1, z1o, z2, wide_mask, halo_mask),
        "slopes",
        conv_flops,
        waits=(st2[0],),
    )
    d2, dn1, c2, own3 = call(
        functools.partial(back2_kernel, len(st2)),
        (shape(height + 2, BF16), shape(height), vector, vector),
        [],
        (own2, own1, c1, a2, s2, mu, ux, up, wide_mask, a1, a1o, w2tt, g2, t2, *st2),
        "conv2_back",
        conv_flops,
    )
    st3 = spread(own3)
    w2, bias2 = call(
        weight2_kernel,
        (array((9 * c, c), BF16), vector),
        [acc],
        (n1, d2),
        "conv2_weight_grad",
        conv_flops,
        waits=(st3[0],),
    )
    chunks = array((leads, 9 * c // leads + SMALL, c), BF16)
    d1, send, keep = call(
        functools.partial(weight1_kernel, group, leads, len(st3)),
        (shape(height, BF16), chunks, chunks),
        [acc],
        (c1, c2, dn1, a1, a1o, s1, x, gx, gp, g1, w2, bias2, *st3),
        "conv1_weight_grad",
        conv_flops,
    )

    def edges(after):
        rows = call(edge_rows_kernel, (edge, edge), [], (d1,), "edge_rows", waits=(after,))
        return neighbours(*rows)[::-1]

    def input_grad(rows):
        return call(
            input_grad_kernel,
            (shape(height, BF16), vector),
            [pltpu.VMEM(turned.shape, BF16)],
            (*rows, d1, u, conv1_weight),
            "conv1_back",
            conv_flops,
        )

    def block_output(after):
        return call(
            output_kernel,
            (shape(height, BF16), vector),
            [pltpu.VMEM(x.shape, BF16), pltpu.SemaphoreType.DMA((samples,))],
            (x, a2, wide_mask, c2),
            "output",
            conv_flops // 2,
            waits=(after,),
            spaces=(VMEM, [ANY, VMEM]),
        )

    first, second, output, grad_input = sum_everywhere(
        send, keep, edges, block_output, input_grad
    )
    sums = []
    for part in (first, second):
        sums += [part[0].reshape(3, 3, c, c)] + [v.reshape(c) for v in part[1:]]
    return (output[None], grad_input[None], *sums)


def solution(mesh):
    tiles = P("lead", "dp", "lat", None, None)
    in_specs = (tiles, tiles, P("lead", "dp", "lat", None)) + (P(),) * 8
    out_specs = (tiles, tiles) + (P(),) * 8
    return jax.shard_map(shards, mesh=mesh, in_specs=in_specs, out_specs=out_specs, check_vma=False)
```

```python
import functools

import jax
import jax.numpy as jnp
from jax import lax
from jax.experimental import pallas as pl
from jax.experimental.pallas import tpu as pltpu
from jax.sharding import PartitionSpec as P

EPSILON = 1e-05
BF16 = jnp.bfloat16
F32 = jnp.float32
VMEM = pl.BlockSpec(memory_space=pltpu.VMEM)
ANY = pl.BlockSpec(memory_space=pl.ANY)
HIDE = 10**11
SMALL = 16


def fill_toeplitz(taps_ref, out_ref):
    c = taps_ref.shape[-1]
    zero = jnp.zeros((c, c), BF16)
    half = jnp.asarray(0.5, BF16)
    for b in range(3):
        for i in range(4):
            for j in range(2):
                block = taps_ref[i - j, b] * half if 0 <= i - j < 3 else zero
                out_ref[b, i * c : (i + 1) * c, j * c : (j + 1) * c] = block


def fill_toeplitz_transposed(taps_ref, out_ref):
    c = taps_ref.shape[-1]
    zero = jnp.zeros((c, c), BF16)
    for b in range(3):
        for i in range(4):
            for j in range(2):
                block = taps_ref[2 - (i - j), 2 - b] if 0 <= i - j < 3 else zero
                out_ref[b, j * c : (j + 1) * c, i * c : (i + 1) * c] = block


def convolve_rows(row, starts, weights_ref, across, transposed):
    left = jnp.concatenate(
        [jnp.concatenate([row(r - 1 + i) for r in starts], 0) for i in range(4)], 1
    )
    c = left.shape[1] // 4
    dims = (((1,), (1 if transposed else 0,)), ((), ()))
    taps = [
        lax.dot_general(left, weights_ref[b], dims, preferred_element_type=F32)
        for b in range(3)
    ]

    def piece(pair, j):
        part = [t[pair * across : (pair + 1) * across, j * c : (j + 1) * c] for t in taps]
        return pltpu.roll(part[0], 1, 0) + part[1] + pltpu.roll(part[2], across - 1, 0)

    return piece


def silu(half):
    return half + half * jnp.tanh(half)


def silu_slope(half):
    t = jnp.tanh(half)
    return (0.5 + 0.5 * t) * (1.0 + half * (1.0 - t))


def fold(value):
    return value.reshape(-1, 8, value.shape[-1]).sum(0)


def join(stats, count, at, sums):
    centres = stats[:, at + 2 : at + 3]
    mean = (stats[:, at : at + 1] + sums * centres).sum(0) / count
    away = centres - mean
    squares = stats[:, at + 1 : at + 2] + away * (2.0 * stats[:, at : at + 1] + sums * away)
    variance = jnp.maximum(squares.sum(0) / count, 0.0)
    return mean, lax.rsqrt(variance + EPSILON)


def has_pair():
    count, me = lax.axis_size("lat"), lax.axis_index("lat")
    inside = jnp.logical_and(me != 0, me != count - 1)
    return (me == me, inside) if count % 2 == 0 else (me != count - 1, me != 0)


def pick(even, when_even, when_odd):
    return jnp.where(even, when_even, when_odd)


def column_mask(bits, k, c):
    tile = bits[k // 128]
    return jnp.broadcast_to(tile[:, k % 128 : k % 128 + 1].astype(F32), (tile.shape[0], c))


def near_rows_kernel(top_ref, bottom_ref, gx_ref, gp_ref):
    even = lax.axis_index("lat") % 2 == 0
    top, bottom = top_ref[...], bottom_ref[...]
    paired_x, paired_p = has_pair()
    gx_ref[...] = pick(paired_x, pick(even, bottom, top), jnp.zeros_like(top))
    gp_ref[...] = pick(paired_p, pick(even, top, bottom), jnp.zeros_like(top))


def far_rows_kernel(x_ref, bits_ref, *refs):
    samples, height, across, c = x_ref.shape
    even = lax.axis_index("lat") % 2 == 0
    hx_ref, hp_ref = refs[-2:]
    zero = jnp.zeros((across, c), BF16)
    for out, down, paired in zip((hx_ref, hp_ref), (even, jnp.logical_not(even)), has_pair()):
        first = jnp.where(down, height - 3, 1)
        for s in range(samples):
            out[2 * s] = pick(paired, x_ref[s, first], zero)
            out[2 * s + 1] = pick(paired, x_ref[s, first + 1], zero)
        for k in range(bits_ref.shape[0]):
            bits = bits_ref[k]
            out[2 * samples + k] = pick(paired, bits, jnp.zeros_like(bits)).astype(BF16)


def masks_kernel(mask_ref, x_ref, w_ref, b_ref, m_ref, count_ref, bits_ref):
    samples, height, across, c = m_ref.shape
    for k in range(bits_ref.shape[0]):
        bits = mask_ref[k * 128 : (k + 1) * 128].astype(F32)
        bits = jnp.concatenate([bits, jnp.zeros((bits.shape[0], 128 - across), F32)], 1)
        if bits.shape[0] < 128:
            bits = jnp.concatenate([bits, jnp.zeros((128 - bits.shape[0], 128), F32)], 0)
        bits_ref[k] = bits.T[:across]
    count = jnp.zeros((8, c), F32)
    for s in range(samples):
        for r in range(height):
            mask = column_mask(bits_ref, s * height + r, c)
            m_ref[s, r] = mask
            count += fold(mask)
    count_ref[...] = stats_block([count.sum(0, keepdims=True)], c)


def stats_block(rows, c):
    return jnp.concatenate(rows + [jnp.zeros((8 - len(rows), c), F32)], 0)


def gather(refs):
    return jnp.concatenate([r[...] for r in refs], 0)


def middle(value):
    return value.mean(0, keepdims=True)


def add_moments(sums, active, mask):
    masked = active * mask
    sums[0] += fold(masked)
    sums[1] += fold(masked * active)
    return masked


def own_row(inner_ref, outer_ref, s, r, height):
    if 2 <= r < height - 2:
        return inner_ref[s, r - 2]
    return outer_ref[s, r if r < 2 else r - height + 4]


def conv1_inner_kernel(x_ref, m_ref, w_ref, b_ref, a_ref, z_ref, t_ref, part_ref):
    samples, height, across, c = x_ref.shape
    fill_toeplitz(w_ref, t_ref)
    bias = 0.5 * b_ref[...]
    sums = [jnp.zeros((8, c), F32) for _ in range(2)]
    centre = None
    for s in range(samples):
        piece = convolve_rows(lambda r: x_ref[s, r], range(2, height - 2, 2), t_ref, across, False)
        for i in range(height - 4):
            half = piece(i // 2, i % 2) + bias
            active = silu(half)
            if centre is None:
                centre = middle(active)
            active = active - centre
            a_ref[s, i] = active
            z_ref[s, i] = half
            add_moments(sums, active, m_ref[s, i + 2])
    rows = [v.sum(0, keepdims=True) for v in sums]
    part_ref[...] = stats_block([rows[0], rows[1], centre], c)


def conv1_outer_kernel(
    gp_ref, gx_ref, x_ref, m_ref, count_ref, t_ref, b_ref, part_ref, a_ref, z_ref, st_ref
):
    samples, height, across, c = x_ref.shape
    even = lax.axis_index("lat") % 2 == 0
    bias = 0.5 * b_ref[...]
    centre = part_ref[2:3]

    def row(r):
        if r < 0:
            parts = [pick(even, gp_ref[s, 0], gx_ref[s, 0]) for s in range(samples)]
        elif r >= height:
            parts = [pick(even, gx_ref[s, 0], gp_ref[s, 0]) for s in range(samples)]
        else:
            parts = [x_ref[s, r] for s in range(samples)]
        return jnp.concatenate(parts, 0)

    sums = [jnp.zeros((8, c), F32) for _ in range(2)]
    for slot, start in ((0, 0), (2, height - 2)):
        piece = convolve_rows(row, (start,), t_ref, across, False)
        for s in range(samples):
            for j in range(2):
                half = piece(s, j) + bias
                active = silu(half) - centre
                a_ref[s, slot + j] = active
                z_ref[s, slot + j] = half
                add_moments(sums, active, m_ref[s, start + j])
    rows = [part_ref[i : i + 1] + v.sum(0, keepdims=True) for i, v in enumerate(sums)]
    st_ref[...] = stats_block([rows[0], rows[1], centre, count_ref[0:1]], c)


def prepare_kernel(u_ref, m_ref, w2_ref, mu_ref, su_ref, t2_ref, tt2_ref):
    samples, height, across, c = u_ref.shape
    fill_toeplitz(w2_ref, t2_ref)
    fill_toeplitz_transposed(w2_ref, tt2_ref)
    total = jnp.zeros((8, c), F32)
    for s in range(samples):
        for r in range(height):
            value = u_ref[s, r].astype(F32) * m_ref[s, r]
            mu_ref[s, r] = value
            total += fold(value)
    su_ref[...] = stats_block([total.sum(0, keepdims=True)], c)


def conv1_edge_kernel(
    hp_ref, hx_ref, gp_ref, gx_ref, x_ref, st_ref, t_ref, b_ref, a_ref, mh_ref
):
    samples, height, across, c = x_ref.shape
    even = lax.axis_index("lat") % 2 == 0
    bias = 0.5 * b_ref[...]
    centre = st_ref[2:3]

    def row(r):
        parts = []
        for s in range(samples):
            if r < -1:
                parts.append(pick(even, hp_ref[2 * s + r + 3], hx_ref[2 * s + r + 3]))
            elif r == -1:
                parts.append(pick(even, gp_ref[s, 0], gx_ref[s, 0]))
            elif r < height:
                parts.append(x_ref[s, r])
            elif r == height:
                parts.append(pick(even, gx_ref[s, 0], gp_ref[s, 0]))
            else:
                j = r - height - 1
                parts.append(pick(even, hx_ref[2 * s + j], hp_ref[2 * s + j]))
        return jnp.concatenate(parts, 0)

    slabs = slice(2 * samples, hx_ref.shape[0])
    above = pick(even, hp_ref[slabs], hx_ref[slabs])
    below = pick(even, hx_ref[slabs], hp_ref[slabs])
    for slot, start in ((0, -2), (2, height)):
        piece = convolve_rows(row, (start,), t_ref, across, False)
        for s in range(samples):
            for j in range(2):
                a_ref[s, slot + j] = silu(piece(s, j) + bias) - centre
                if start < 0:
                    mask = column_mask(above, s * height + height - 2 + j, c)
                else:
                    mask = column_mask(below, s * height + j, c)
                mh_ref[s, slot + j] = mask


def conv2_kernel(
    pieces,
    own_ref, a_ref, ao_ref, ah_ref, m_ref, mh_ref, mu_ref, su_ref, k_ref, b_ref, g_ref, t_ref, *refs,
):
    stats, (n_ref, a2_ref, z2_ref, c1_ref, st2_ref) = gather(refs[:pieces]), refs[pieces:]
    samples, height, across, c = m_ref.shape
    counts = stats[:, 3:4]
    count = counts.sum(0)
    mean, inverse = join(stats, count, 0, counts)
    offset = mean - own_ref[2:3]
    scale = inverse * g_ref[...]
    shift = t_ref[...] - offset * scale
    c1_ref[...] = stats_block([offset, inverse, count, mean], c)
    bias = 0.5 * b_ref[...]
    sums = [jnp.zeros((8, c), F32) for _ in range(3)]
    centre = None
    for s in range(samples):
        for i in range(height + 4):
            r = i - 2
            if 0 <= r < height:
                value, mask = own_row(a_ref, ao_ref, s, r, height), m_ref[s, r]
            else:
                j = i if r < 0 else r - height + 2
                value, mask = ah_ref[s, j], mh_ref[s, j]
            n_ref[s, i] = ((value * scale + shift) * mask).astype(BF16)

        piece = convolve_rows(
            lambda r: n_ref[s, r + 2], range(-1, height + 1, 2), k_ref, across, False
        )
        for i in range(height + 2):
            r = i - 1
            half = piece(i // 2, i % 2) + bias
            active = silu(half)
            if centre is None:
                centre = middle(active)
            active = active - centre
            if 0 <= r < height:
                add_moments(sums, active, m_ref[s, r])
                sums[2] += fold(active * mu_ref[s, r])
            a2_ref[s, i] = active
            z2_ref[s, i] = half
    rows = [v.sum(0, keepdims=True) for v in sums]
    st2_ref[...] = stats_block(
        [rows[0], rows[1], centre, rows[2], su_ref[0:1], own_ref[3:4]], c
    )


def slopes_kernel(z_ref, zo_ref, z2_ref, m_ref, mh_ref, after_ref, s_ref, s2_ref):
    samples, height = m_ref.shape[:2]
    for s in range(samples):
        for r in range(-1, height + 1):
            mask = mh_ref[s, 1 if r < 0 else 2]
            if 0 <= r < height:
                mask = m_ref[s, r]
                s_ref[s, r] = silu_slope(own_row(z_ref, zo_ref, s, r, height)) * mask
            s2_ref[s, r + 1] = silu_slope(z2_ref[s, r + 1]) * mask


def back_terms(scale, inverse, offset, gain_sum, shift_sum, count):
    by_active = -scale * gain_sum * inverse / count
    constant = -scale * (shift_sum - offset * inverse * gain_sum) / count
    return by_active, constant


def back2_kernel(
    pieces,
    own_ref, st1_ref, c1_ref, a2_ref, s2_ref, mu_ref, ux_ref, up_ref, m_ref, a_ref, ao_ref, k_ref, g_ref, t_ref, *refs,
):
    stats, (d_ref, dn_ref, c2_ref, st3_ref) = gather(refs[:pieces]), refs[pieces:]
    samples, height, across, c = m_ref.shape
    even = lax.axis_index("lat") % 2 == 0
    count = c1_ref[2:3]
    mean, inverse = join(stats, count, 0, stats[:, 5:6])
    offset = mean - own_ref[2:3]
    shift_sum = stats[:, 4:5].sum(0)
    away = stats[:, 2:3] - mean
    gain_sum = inverse * (stats[:, 3:4] + away * stats[:, 4:5]).sum(0)
    scale = inverse * g_ref[...]
    by_active, constant = back_terms(scale, inverse, offset, gain_sum, shift_sum, count)
    c2_ref[...] = stats_block([scale, t_ref[...] - offset * scale, gain_sum, shift_sum], c)
    sums = [jnp.zeros((8, c), F32) for _ in range(2)]
    for s in range(samples):
        for i in range(height + 2):
            if 0 < i <= height:
                upstream = mu_ref[s, i - 1]
            else:
                edges = (up_ref[s], ux_ref[s]) if i == 0 else (ux_ref[s], up_ref[s])
                upstream = pick(even, *edges).astype(F32)
            grad = upstream * scale + (a2_ref[s, i] * by_active + constant)
            d_ref[s, i] = (grad * s2_ref[s, i]).astype(BF16)
        piece = convolve_rows(
            lambda r: d_ref[s, r + 1], range(0, height, 2), k_ref, across, True
        )
        for r in range(height):
            part = piece(r // 2, r % 2)
            dn_ref[s, r] = part
            masked = part * m_ref[s, r]
            sums[0] += fold(masked)
            sums[1] += fold(masked * own_row(a_ref, ao_ref, s, r, height))
    rows = [v.sum(0, keepdims=True) for v in sums]
    st3_ref[...] = stats_block([rows[0], rows[1], st1_ref[2:3]], c)


def weight_products(rows, centre, turned, total_ref, first):
    windows = jnp.concatenate(rows, 1)
    product = lax.dot_general(
        windows,
        jnp.concatenate([turned[0], centre, turned[1]], 1),
        (((0,), (0,)), ((), ())),
        preferred_element_type=F32,
    )
    if first:
        total_ref[...] = product
    else:
        total_ref[...] += product


def turn(value, across):
    c = value.shape[-1]
    return [
        pltpu.roll(value, k, 1).astype(BF16).reshape(-1, c) for k in (across - 1, 1)
    ]


def weight2_kernel(n_ref, d_ref, after_ref, w_ref, b_ref, acc_ref):
    samples, rows, across, c = d_ref.shape
    height = rows - 2
    bias = jnp.zeros((8, c), F32)
    for s in range(samples):
        grad = d_ref[s, 1 : 1 + height]
        wide = grad.astype(F32)
        bias += fold(wide)
        rows = [n_ref[s, a + 1 : a + 1 + height].reshape(-1, c) for a in range(3)]
        weight_products(rows, grad.reshape(-1, c), turn(wide, across), acc_ref, s == 0)
    b_ref[...] = jnp.broadcast_to(bias.sum(0, keepdims=True), b_ref.shape)
    for a in range(3):
        for b in range(3):
            at = (a * 3 + b) * c
            w_ref[at : at + c] = acc_ref[a * c : (a + 1) * c, b * c : (b + 1) * c].astype(BF16)


def output_kernel(x_ref, a2_ref, m_ref, c2_ref, after_ref, o_hbm, done_ref, o_ref, sems):
    samples, height, across, c = x_ref.shape
    scale, shift = c2_ref[0:1], c2_ref[1:2]
    for s in range(samples):
        for r in range(height):
            normed = (a2_ref[s, r + 1] * scale + shift) * m_ref[s, r]
            o_ref[s, r] = (x_ref[s, r].astype(F32) + normed).astype(BF16)
        pltpu.make_async_copy(o_ref.at[s], o_hbm.at[s], sems.at[s]).start()
    done_ref[...] = jnp.zeros(done_ref.shape, F32)
    for s in range(samples):
        pltpu.make_async_copy(o_ref.at[s], o_hbm.at[s], sems.at[s]).wait()


def small_rows(rows, c):
    high = jnp.concatenate(rows + [jnp.zeros((8 - len(rows), c), F32)], 0)
    first = high.astype(BF16)
    return jnp.concatenate([first, (high - first.astype(F32)).astype(BF16)], 0)


def weight1_kernel(
    group, leads, pieces,
    c1_ref, c2_ref, dn_ref, a_ref, ao_ref, s_ref, x_ref, gx_ref, gp_ref, g_ref, w2_ref, b2_ref, *refs,
):
    stats = gather(refs[:pieces])
    d_ref, send_ref, keep_ref, acc_ref = refs[pieces:]
    samples, height, across, c = x_ref.shape
    even = lax.axis_index("lat") % 2 == 0
    core = lax.axis_index("dp") % 2
    offset, inverse, count, mean = (c1_ref[i : i + 1] for i in range(4))
    shift_sum = stats[:, 0:1].sum(0)
    away = stats[:, 2:3] - mean
    gain_sum = inverse * (stats[:, 1:2] + away * stats[:, 0:1]).sum(0)
    scale = inverse * g_ref[...]
    by_active, constant = back_terms(scale, inverse, offset, gain_sum, shift_sum, count)
    bias = jnp.zeros((8, c), F32)
    for s in range(samples):
        for r in range(height):
            active = own_row(a_ref, ao_ref, s, r, height)
            grad = dn_ref[s, r] * scale + (active * by_active + constant)
            d_ref[s, r] = (grad * s_ref[s, r]).astype(BF16)
        grad = d_ref[s]
        wide = grad.astype(F32)
        bias += fold(wide)
        above = pick(even, gp_ref[s, 0], gx_ref[s, 0])
        below = pick(even, gx_ref[s, 0], gp_ref[s, 0])
        body = x_ref[s].reshape(-1, c)
        rows = [
            jnp.concatenate([above, body[: (height - 1) * across]], 0),
            body,
            jnp.concatenate([body[across:], below], 0),
        ]
        weight_products(rows, grad.reshape(-1, c), turn(wide, across), acc_ref, s == 0)

    share = 1.0 / group
    small = [
        small_rows([bias.sum(0, keepdims=True), gain_sum * share, shift_sum * share], c),
        small_rows([b2_ref[0:1], c2_ref[2:3] * share, c2_ref[3:4] * share], c),
    ]

    def put(target, which):
        size = 9 * c // leads
        for j in range(leads):
            slot = j ^ place(which, leads)
            if which == 1:
                target[slot, :size] = w2_ref[j * size : (j + 1) * size]
            else:
                at = j * size
                while at < (j + 1) * size:
                    tap, low = at // c, at % c
                    step = min(c - low, (j + 1) * size - at)
                    a, b = tap // 3, tap % 3
                    target[slot, at - j * size : at - j * size + step] = acc_ref[
                        a * c + low : a * c + low + step, b * c : (b + 1) * c
                    ].astype(BF16)
                    at += step
            target[slot, size:] = small[which]

    @pl.when(core == 0)
    def _():
        put(keep_ref, 0)
        put(send_ref, 1)

    @pl.when(core != 0)
    def _():
        put(keep_ref, 1)
        put(send_ref, 0)


def edge_rows_kernel(d_ref, *refs):
    dx_ref, dp_ref = refs[-2:]
    samples, height = d_ref.shape[:2]
    even = lax.axis_index("lat") % 2 == 0
    paired_x, paired_p = has_pair()
    for s in range(samples):
        top, bottom = d_ref[s, 0], d_ref[s, height - 1]
        dx_ref[s] = pick(paired_x, pick(even, bottom, top), jnp.zeros_like(top))
        dp_ref[s] = pick(paired_p, pick(even, top, bottom), jnp.zeros_like(top))


def input_grad_kernel(ep_ref, ex_ref, d_ref, u_ref, w_ref, o_ref, done_ref, k_ref):
    samples, height, across, c = u_ref.shape
    even = lax.axis_index("lat") % 2 == 0
    fill_toeplitz_transposed(w_ref, k_ref)
    for s in range(samples):

        def row(r):
            if r < 0:
                return pick(even, ep_ref[s], ex_ref[s])
            if r >= height:
                return pick(even, ex_ref[s], ep_ref[s])
            return d_ref[s, r]

        piece = convolve_rows(row, range(0, height, 2), k_ref, across, True)
        for r in range(height):
            o_ref[s, r] = (u_ref[s, r].astype(F32) + piece(r // 2, r % 2)).astype(BF16)
    done_ref[...] = jnp.zeros(done_ref.shape, F32)


def join_kernel(leads, *refs):
    out_ref = refs[-1]
    size = refs[0].shape[0] - SMALL
    for k in range(leads):
        out_ref[k * size : (k + 1) * size] = refs[k][:size]
    out_ref[leads * size :] = refs[0][size:]


def write_chunks(leads, which, ref, out_hbm, sum_ref, sems):
    size = out_hbm.shape[0] // leads
    copies = []
    for k in range(leads):
        at = pl.multiple_of((k ^ place(which, leads)) * size, 16)
        rows = slice(k * size, (k + 1) * size)
        sum_ref[rows] = ref[rows].astype(F32)
        copies.append(
            pltpu.make_async_copy(sum_ref.at[rows], out_hbm.at[pl.ds(at, size)], sems.at[k])
        )
        copies[-1].start()
    for copy in copies:
        copy.wait()


def leave_kernel(leads, grad_ref, own_ref, grad_hbm, first_hbm, second_hbm, sum_ref, sems):
    core = lax.axis_index("dp") % 2
    grad = pltpu.make_async_copy(grad_ref, grad_hbm, sems.at[leads])
    grad.start()

    @pl.when(core == 0)
    def _():
        write_chunks(leads, 0, own_ref, first_hbm, sum_ref, sems)

    @pl.when(core != 0)
    def _():
        write_chunks(leads, 1, own_ref, second_hbm, sum_ref, sems)

    grad.wait()


def finish_kernel(leads, own_ref, other_ref, first_in, second_in, first_hbm, second_hbm, *refs):
    small_hbm, (sum_ref, small_ref, sems) = refs[:6], refs[6:]
    core = lax.axis_index("dp") % 2
    small = [r[sum_ref.shape[0] :].astype(F32) for r in (own_ref, other_ref)]
    small = [v[:8] + v[8:] for v in small]
    for which in range(2):
        total = jnp.where(core == which, small[0], small[1])
        for i in range(3):
            small_ref[3 * which + i] = total[i : i + 1]
    copies = [
        pltpu.make_async_copy(small_ref.at[i], small_hbm[i], sems.at[leads + i]) for i in range(6)
    ]
    for copy in copies:
        copy.start()

    @pl.when(core != 0)
    def _():
        write_chunks(leads, 0, other_ref, first_hbm, sum_ref, sems)

    @pl.when(core == 0)
    def _():
        write_chunks(leads, 1, other_ref, second_hbm, sum_ref, sems)

    for copy in copies:
        copy.wait()


def add_kernel(parts, waits, *refs):
    outs = refs[parts + waits :]
    size = outs[0].shape[0] - SMALL
    for k, out in enumerate(outs):
        chunk = [r.at[k] if len(r.shape) == 3 else r for r in refs[:parts]]
        total = functools.reduce(lambda a, b: a + b, [r[...].astype(F32) for r in chunk])
        out[:size] = total[:size].astype(BF16)
        small = total[size : size + 8] + total[size + 8 :]
        high = small.astype(BF16)
        out[size:] = jnp.concatenate([high, (small - high.astype(F32)).astype(BF16)], 0)


def call(
    kernel, outs, scratch, operands, name, flops=0, waits=(), spaces=(VMEM, VMEM), aliases={}
):
    size = sum(o.size * o.dtype.itemsize for o in operands)
    ins, to = (s if isinstance(s, list) else None for s in spaces)
    return pl.pallas_call(
        kernel,
        out_shape=outs,
        in_specs=(ins or [spaces[0]] * len(operands)) + [ANY] * len(waits),
        out_specs=to or jax.tree.map(lambda _: spaces[1], outs),
        scratch_shapes=scratch,
        input_output_aliases=aliases,
        compiler_params=pltpu.CompilerParams(vmem_limit_bytes=16 * 2**20),
        cost_estimate=pl.CostEstimate(flops=flops, bytes_accessed=size, transcendentals=0),
        name=name,
    )(*operands, *waits)


def swap(value, axis, k):
    return lax.ppermute(value, axis, [(i, i ^ k) for i in range(lax.axis_size(axis))])


def cross(value, k, first):
    leads, dps, lats = (lax.axis_size(a) for a in ("lead", "dp", "lat"))
    pairs = []
    for lead in range(leads):
        for dp in range(dps):
            for lat in range(lats):
                by_lead = first if leads != lats else (dp % 2 == 0) == first
                to = (lead ^ k, dp, lat) if by_lead else (lead, dp, lat ^ k)
                pairs.append(tuple((l * dps + d) * lats + t for l, d, t in ((lead, dp, lat), to)))
    return lax.ppermute(value, ("lead", "dp", "lat"), pairs)


def place(which, leads):
    if which == 1 and leads == lax.axis_size("lat"):
        return lax.axis_index("lat")
    return lax.axis_index("lead")


def over_dp_and_lat(value, to):
    dps, lats = lax.axis_size("dp"), lax.axis_size("lat")
    pairs = []
    for dp in range(dps):
        for lat in range(lats):
            to_dp, to_lat = to(dp, lat)
            pairs.append((dp * lats + lat, to_dp * lats + to_lat))
    return lax.ppermute(value, ("dp", "lat"), pairs)


def neighbours(value_x, value_p):
    lats = lax.axis_size("lat")

    def exchange(value, offset):
        def to(dp, lat):
            other = ((lat - offset) ^ 1) + offset if lat >= offset else lats
            return (dp, other) if other < lats else (dp ^ 1, lat)

        return over_dp_and_lat(value, to)

    got_p = exchange(value_p, 1)
    return exchange(value_x, 0), got_p


def blocks_kernel(parts, *refs):
    refs[-1][...] = jnp.concatenate([r[...] for r in refs[:parts]], 0)


def spread(stats, flops=0):
    blocks, k = stats[None], 1
    while k < lax.axis_size("dp"):
        both = (blocks, swap(blocks, "dp", k))
        shape = jax.ShapeDtypeStruct((2 * k, *stats.shape), F32)
        blocks = call(functools.partial(blocks_kernel, 2), shape, [], both, "blocks", flops)
        k *= 2
    return [blocks] + [
        over_dp_and_lat(blocks, lambda dp, lat, k=k: (dp ^ 1, lat ^ k))
        for k in [1, *reversed(range(2, lax.axis_size("lat")))]
    ]


def add_chunks(parts, name, outs=1, waits=(), flops=0):
    shape = jax.ShapeDtypeStruct(parts[0].shape[-2:], BF16)
    return call(
        functools.partial(add_kernel, len(parts), len(waits)),
        [shape] * outs,
        [],
        parts,
        name,
        flops,
        waits,
    )


def sum_everywhere(send, keep, edges, block_output, input_grad):
    leads, lats = lax.axis_size("lead"), lax.axis_size("lat")
    chunks = add_chunks([keep, swap(send, "dp", 1)], "add_dp", leads)
    got = [cross(chunks[k], k, True) for k in [*range(2, leads), 1]]
    output = block_output(chunks[0])
    rows = edges(chunks[0])
    (mine,) = add_chunks([chunks[0]] + got, "add_first", waits=(output[1],), flops=HIDE)
    got = [cross(mine, k, False) for k in range(1, lats)]
    grad_input = input_grad(rows)
    (mine,) = add_chunks([mine] + got, "add_second", waits=(grad_input[1],))
    k = 2
    while k < lax.axis_size("dp"):
        (mine,) = add_chunks([mine, swap(mine, "dp", k)], "add_far_dp")
        k *= 2
    size, c = mine.shape[0] - SMALL, mine.shape[1]
    got = [cross(mine, k, True) for k in range(1, leads)]
    own = call(
        functools.partial(join_kernel, leads),
        jax.ShapeDtypeStruct((leads * size + SMALL, c), BF16),
        [],
        (mine, *got),
        "join",
    )
    whole = jax.ShapeDtypeStruct((leads * size, c), F32)
    row = jax.ShapeDtypeStruct((1, c), F32)
    dma = pltpu.SemaphoreType.DMA
    total = pltpu.VMEM(whole.shape, F32)
    other = swap(own, "dp", 1)
    grad_input, first, second = call(
        functools.partial(leave_kernel, leads),
        [jax.ShapeDtypeStruct(grad_input[0].shape, BF16), whole, whole],
        [total, dma((leads + 1,))],
        (grad_input[0], own),
        "leave",
        spaces=(VMEM, ANY),
    )
    first, second, *rows = call(
        functools.partial(finish_kernel, leads),
        [whole, whole] + [row] * 6,
        [total, pltpu.VMEM((6, 1, c), F32), dma((leads + 6,))],
        (own, other, first, second),
        "finish",
        spaces=([VMEM, VMEM, ANY, ANY], [ANY] * 8),
        aliases={2: 0, 3: 1},
    )
    return (first, *rows[:3]), (second, *rows[3:]), output[0], grad_input


def shards(
    field,
    cotangent,
    land_sea,
    conv1_weight,
    conv1_bias,
    first_norm_scale,
    norm1_shift,
    conv2_weight,
    conv2_bias,
    second_norm_scale,
    norm2_shift,
):
    x, u, mask = field[0], cotangent[0], land_sea[0]
    samples, height, across, c = x.shape
    group = lax.axis_size("dp") * lax.axis_size("lat")
    leads = lax.axis_size("lead")
    slabs = -(-samples * height // 128)
    vec = lambda v: v.reshape(1, c)
    b1, g1, t1 = vec(conv1_bias), vec(first_norm_scale), vec(norm1_shift)
    b2, g2, t2 = vec(conv2_bias), vec(second_norm_scale), vec(norm2_shift)

    array = jax.ShapeDtypeStruct
    shape = lambda rows, dtype=F32: array((samples, rows, across, c), dtype)
    edge = array((samples, across, c), BF16)
    vector = array((8, c), F32)
    weights = array((3, 4 * c, 2 * c), BF16)
    turned = array((3, 2 * c, 4 * c), BF16)
    acc = pltpu.VMEM((3 * c, 3 * c), F32)
    conv_flops = 2 * 9 * c * c * samples * height * across

    near = call(
        near_rows_kernel,
        (shape(1, BF16), shape(1, BF16)),
        [],
        (x[:, :1], x[:, height - 1 :]),
        "near_rows",
        conv_flops,
    )
    gx, gp = neighbours(*near)
    packed = array((2 * samples + slabs, across, c), BF16)
    wide_mask, count, bits = call(
        masks_kernel,
        (shape(height), vector, array((slabs, across, 128), F32)),
        [],
        (mask.reshape(samples * height, across), x, conv1_weight, b1),
        "masks",
        conv_flops,
    )
    a1, z1, w1t, part = call(
        conv1_inner_kernel,
        (shape(height - 4), shape(height - 4), weights, vector),
        [],
        (x, wide_mask, conv1_weight, b1),
        "conv1_inner",
        4 * conv_flops,
    )
    hx, hp = neighbours(
        *call(far_rows_kernel, (packed, packed), [], (x, bits), "far_rows", conv_flops, (part,))
    )
    a1o, z1o, own1 = call(
        conv1_outer_kernel,
        (shape(4), shape(4), vector),
        [],
        (gp, gx, x, wide_mask, count, w1t, b1, part),
        "conv1_outer",
        16 * conv_flops,
    )
    mu, mu_sum, w2t, w2tt = call(
        prepare_kernel,
        (shape(height), vector, weights, turned),
        [],
        (u, wide_mask, conv2_weight),
        "prepare",
        conv_flops,
    )
    a1h, halo_mask = call(
        conv1_edge_kernel,
        (shape(4), shape(4)),
        [],
        (hp, hx, gp, gx, x, own1, w1t, b1),
        "conv1_edges",
        conv_flops // 2,
    )
    st1 = spread(own1)
    n1, a2, z2, c1, own2 = call(
        functools.partial(conv2_kernel, len(st1)),
        (shape(height + 4, BF16), shape(height + 2), shape(height + 2), vector, vector),
        [],
        (own1, a1, a1o, a1h, wide_mask, halo_mask, mu, mu_sum, w2t, b2, g1, t1, *st1),
        "conv2",
        conv_flops,
    )
    ux, up = neighbours(*call(edge_rows_kernel, (edge, edge), [], (u,), "u_rows", waits=(own2,)))
    st2 = spread(own2, HIDE)
    s1, s2 = call(
        slopes_kernel,
        (shape(height), shape(height + 2)),
        [],
        (z1, z1o, z2, wide_mask, halo_mask),
        "slopes",
        conv_flops,
        waits=(st2[0],),
    )
    d2, dn1, c2, own3 = call(
        functools.partial(back2_kernel, len(st2)),
        (shape(height + 2, BF16), shape(height), vector, vector),
        [],
        (own2, own1, c1, a2, s2, mu, ux, up, wide_mask, a1, a1o, w2tt, g2, t2, *st2),
        "conv2_back",
        conv_flops,
    )
    st3 = spread(own3)
    w2, bias2 = call(
        weight2_kernel,
        (array((9 * c, c), BF16), vector),
        [acc],
        (n1, d2),
        "conv2_weight_grad",
        conv_flops,
        waits=(st3[0],),
    )
    chunks = array((leads, 9 * c // leads + SMALL, c), BF16)
    d1, send, keep = call(
        functools.partial(weight1_kernel, group, leads, len(st3)),
        (shape(height, BF16), chunks, chunks),
        [acc],
        (c1, c2, dn1, a1, a1o, s1, x, gx, gp, g1, w2, bias2, *st3),
        "conv1_weight_grad",
        conv_flops,
    )

    def edges(after):
        rows = call(edge_rows_kernel, (edge, edge), [], (d1,), "edge_rows", waits=(after,))
        return neighbours(*rows)[::-1]

    def input_grad(rows):
        return call(
            input_grad_kernel,
            (shape(height, BF16), vector),
            [pltpu.VMEM(turned.shape, BF16)],
            (*rows, d1, u, conv1_weight),
            "conv1_back",
            conv_flops,
        )

    def block_output(after):
        return call(
            output_kernel,
            (shape(height, BF16), vector),
            [pltpu.VMEM(x.shape, BF16), pltpu.SemaphoreType.DMA((samples,))],
            (x, a2, wide_mask, c2),
            "output",
            conv_flops // 2,
            waits=(after,),
            spaces=(VMEM, [ANY, VMEM]),
        )

    first, second, output, grad_input = sum_everywhere(
        send, keep, edges, block_output, input_grad
    )
    sums = []
    for part in (first, second):
        sums += [part[0].reshape(3, 3, c, c)] + [v.reshape(c) for v in part[1:]]
    return (output[None], grad_input[None], *sums)


def solution(mesh):
    tiles = P("lead", "dp", "lat", None, None)
    in_specs = (tiles, tiles, P("lead", "dp", "lat", None)) + (P(),) * 8
    out_specs = (tiles, tiles) + (P(),) * 8
    return jax.shard_map(shards, mesh=mesh, in_specs=in_specs, out_specs=out_specs, check_vma=False)
```
